128 devices in a mesh: half: 2 (over core), grp: 8 (over x_lo, z), exp: 8 (over x_hi, y).
Axes of the slice: x: 4 (x_hi: 2, x_lo: 2; x = x_hi * 2 + x_lo), y: 4, z: 4, core: 2. Of those that a mesh axis runs over, the one named last changes fastest.
Arguments:
- residual: bfloat16 [512, 32, 2304], P('exp', ('half', 'grp')), may hold values from -6 to 6
- queries: bfloat16 [512, 32, 4096], P(None, ('half', 'grp'), 'exp'), may hold values from -6 to 6
- key_in: bfloat16 [512, 32, 4096], P(None, ('half', 'grp'), 'exp'), may hold values from -6 to 6
- value_in: bfloat16 [512, 32, 4096], P(None, ('half', 'grp'), 'exp'), may hold values from -6 to 6
- log_decay: float32 [512, 32, 4096], P(None, ('half', 'grp'), 'exp'), may hold values from -0.8 to 0, as said below
- update_rate: float32 [512, 32, 32], P(None, ('half', 'grp'), 'exp'), may hold values from 0.1 to 0.9
- counts: int32 [32], P(('half', 'grp')), may hold values from 1 to 512, 12288 in all
- init_state: float32 [32, 32, 128, 128], P(('half', 'grp'), 'exp'), may hold values from -4 to 4
- w_out: bfloat16 [4096, 2304], P('exp'), may hold values from -0.09375 to 0.09375
- norm_gain: bfloat16 [2304], replicated, may hold values from 0.099609375 to 1.8984375
- w_router: bfloat16 [2304, 128], replicated, may hold values from -0.125 to 0.125
- expert_ids: int32 [512, 32, 8], P('exp', ('half', 'grp')), may hold values from 0 to 127, all different within a row
- w_gate: bfloat16 [128, 2304, 1024], P(('half', 'grp', 'exp')), may hold values from -0.125 to 0.125
- w_up: bfloat16 [128, 2304, 1024], P(('half', 'grp', 'exp')), may hold values from -0.125 to 0.125
- w_down: bfloat16 [128, 1024, 2304], P(('half', 'grp', 'exp')), may hold values from -0.1875 to 0.1875
- dec_query: bfloat16 [32, 2, 32, 128], P('half', None, 'grp'), may hold values from -6 to 6
- dec_key: bfloat16 [32, 2, 32, 128], P('half', None, 'grp'), may hold values from -6 to 6
- dec_value: bfloat16 [32, 2, 32, 128], P('half', None, 'grp', 'exp'), may hold values from -6 to 6
- dec_decay: float32 [32, 2, 32, 128], P('half', None, 'grp'), may hold values from -0.2 to 0, as said below
- dec_beta: float32 [32, 2, 32], P('half', None, 'grp'), may hold values from 0.1 to 0.9
Outputs:
- hidden_out: bfloat16 [512, 32, 2304], P('exp', ('half', 'grp'))
- dec_out: float32 [32, 2, 32, 128], P('half', None, 'grp', 'exp')
- dec_state: float32 [32, 32, 128, 128], P('half', 'grp', None, 'exp')
The draws below stay inside these ranges and needn't reach their ends.
Inputs may be any that keep to these rules, and one draw needn't show every extreme that they name: `log_decay`: log forget factors, all negative. `dec_decay`: log forget factors, all negative.
All inputs are finite; a program needn't handle non-finite values. No bound on the sum of `counts` on one device may be relied on, other than what follows from the above.
Results may differ from the reference program's by a relative error of at most 0.0075.
Values may be sent and summed in bfloat16 or wider, within the bound.
No kernel may reach another device: no remote copies, remote signals or barrier semaphores. Data moves between devices by JAX's collectives and lax.ppermute only.
A program may use at most 192 MiB of HBM per device.

```python
import math
import jax
import jax.numpy as jnp
import numpy as np
from jax import lax

D = 2304
DELTA_HEADS = 32
DK = 128
DV = 128
FF = 1024
TOPK = 8
REQ_G = 2
PREFILL_LENGTH = 512
STEPS = 2
REQUEST_COUNT = 32
EXPERTS = 128
CAP = 12
N_HALF = 2
N_GRP = 8
N_EXP = 8


def decay_rates(key, slow_weight):
    key_head, key_slow, key_fast, key_req = jax.random.split(key, 4)
    slow_heads = jax.random.randint(key_head, (DELTA_HEADS,), 0, slow_weight + 1) > 0
    chain_len = PREFILL_LENGTH + STEPS
    slow_rate = jnp.exp(jax.random.uniform(key_slow, (DELTA_HEADS, DK), minval=jnp.log(0.05), maxval=jnp.log(0.5))) / chain_len
    fast_rate = jnp.exp(jax.random.uniform(key_fast, (DELTA_HEADS, DK), minval=jnp.log(1.0 / 50.0), maxval=jnp.log(1.0 / 30.0)))
    base_rate = jnp.where(slow_heads[:, None], slow_rate, fast_rate)
    factor = jax.random.uniform(key_req, (REQUEST_COUNT, 1, 1), minval=0.6, maxval=1.5)
    return base_rate[None] * factor


def draw_log_decay(key, part):
    decay_rate_grid = decay_rates(key, 1)
    key = jax.random.fold_in(key, 101)
    key_jit, key_pos, penalty_key = jax.random.split(key, 3)
    random_offset = jax.random.uniform(key_jit, (PREFILL_LENGTH, REQUEST_COUNT, DELTA_HEADS, DK), minval=0.5, maxval=1.5)
    token_positions = jax.random.randint(key_pos, (REQUEST_COUNT, 3), 0, PREFILL_LENGTH)
    spike_mask = jnp.any(jnp.arange(PREFILL_LENGTH)[:, None, None] == token_positions[None, :, :], axis=-1)
    spike_penalty = jax.random.uniform(penalty_key, (PREFILL_LENGTH, REQUEST_COUNT, DELTA_HEADS, 1), minval=0.2, maxval=0.5)
    value_vectors = -decay_rate_grid[None] * random_offset + jnp.where(spike_mask[:, :, None, None], jnp.log1p(-spike_penalty), 0.0)
    return value_vectors.reshape(PREFILL_LENGTH, REQUEST_COUNT, DELTA_HEADS * DK).astype(jnp.float32)


def draw_dec_decay(key, part):
    decay_rate_grid = decay_rates(key, 1)
    key = jax.random.fold_in(key, 202)
    random_offset = jax.random.uniform(key, (REQUEST_COUNT, STEPS, DELTA_HEADS, DK), minval=0.5, maxval=1.5)
    return (-decay_rate_grid[:, None] * random_offset).astype(jnp.float32)


def shard_levels(key, dims, pieces, smallest, largest):
    gain = 1.0
    for dim, blocks in pieces:
        heights = jax.random.uniform(jax.random.fold_in(jax.random.fold_in(key, 6), dim), (blocks,), jnp.float32, smallest / len(pieces), largest / len(pieces))
        gain = gain * jnp.repeat(jnp.exp(heights), dims[dim] // blocks).reshape((-1,) + (1,) * (len(dims) - 1 - dim))
    return gain


def picks_of(key, rows, amount, top, lift):
    order = jax.random.permutation(jax.random.fold_in(key, 1), amount)
    favour = order
    for power in range(3):
        favour = favour * favour // amount
    favour = favour * lift // amount
    tickets = jax.random.randint(jax.random.fold_in(key, 2), (rows, amount), 0, 4096) + favour
    fixed_rows = jax.random.permutation(jax.random.fold_in(key, 3), rows)[jnp.arange(amount) % rows]
    tickets = jnp.where(jnp.arange(rows)[:, None] == fixed_rows[None, :], 1 << 14, tickets)
    priority = tickets * amount + jnp.arange(amount)
    return lax.top_k(priority.astype(jnp.int32), top)[1].astype(jnp.int32)


def profile(number_of, total, bound, slope):
    loads = [(1 << 20) // math.isqrt(rank ** slope) + 1 for rank in range(2, number_of + 1)]
    surplus, given = total - bound - (number_of - 1), [1] * (number_of - 1)
    while surplus > 0:
        free = [i for i in range(number_of - 1) if given[i] < bound]
        mass, left = sum([loads[i] for i in free]), surplus
        for i in free:
            more = min(bound - given[i], max(1, left * loads[i] // mass), surplus)
            given[i] = given[i] + more
            surplus = surplus - more
    return np.array([bound] + given)


def ragged_sizes(key, amount, total, limit, slope):
    if amount == 2:
        one = jax.random.randint(key, (), max(1, total - limit), min(limit, total - 1) + 1)
        return jnp.stack([one, total - one])
    sizes = jnp.asarray(profile(amount, total, limit, slope), jnp.int32)
    couples = (amount - 1) // 2
    donor, sink = sizes[1:1 + 2 * couples:2], sizes[2:2 + 2 * couples:2]
    margin = jnp.minimum(donor - 1, limit - sink)
    shifted = jax.random.randint(jax.random.fold_in(key, 1), (couples,), 0, 1 << 20) % (margin + 1)
    sizes = sizes.at[1:1 + 2 * couples:2].set(donor - shifted).at[2:2 + 2 * couples:2].set(sink + shifted)
    return sizes[jax.random.permutation(jax.random.fold_in(key, 2), amount)]


def normal_values(own_key, shape, deviation, bound, pieces=(), kind=jnp.bfloat16):
    entries = jax.random.normal(own_key, shape, jnp.float32) * deviation
    if len(pieces) > 0:
        entries = shard_levels(own_key, shape, pieces, -0.22, 0.18) * entries
    return jnp.clip(entries, min=-bound, max=bound).astype(kind)


def setup_inputs(seed: int = 0) -> dict:
    keys = jax.random.split(jax.random.key(seed), 21)
    residual = normal_values(keys[0], (PREFILL_LENGTH, REQUEST_COUNT, D), 1.0, 6.0, ((0, 8), (1, 16)))
    queries = normal_values(keys[1], (PREFILL_LENGTH, REQUEST_COUNT, DELTA_HEADS * DK), 1.0, 6.0, ((1, 16), (2, 8)))
    key_in = normal_values(keys[2], (PREFILL_LENGTH, REQUEST_COUNT, DELTA_HEADS * DK), 1.0, 6.0, ((1, 16), (2, 8)))
    value_in = normal_values(keys[3], (PREFILL_LENGTH, REQUEST_COUNT, DELTA_HEADS * DV), 1.0, 6.0, ((1, 16), (2, 8)))
    log_decay = draw_log_decay(jax.random.fold_in(keys[20], 71), 0)
    update_rate = jnp.clip(0.1 + 0.79999997 * jax.random.uniform(keys[5], (PREFILL_LENGTH, REQUEST_COUNT, DELTA_HEADS), jnp.float32) ** shard_levels(keys[5], (PREFILL_LENGTH, REQUEST_COUNT, DELTA_HEADS), ((1, 16), (2, 8)), -0.2, 0.2), 0.1, 0.9)
    counts = ragged_sizes(keys[6], REQUEST_COUNT, 3 * REQUEST_COUNT * PREFILL_LENGTH // 4, PREFILL_LENGTH, 2).astype(jnp.int32)
    init_state = normal_values(keys[7], (REQUEST_COUNT, DELTA_HEADS, DK, DV), 0.5, 4.0, ((0, 16), (1, 8)), jnp.float32)
    w_out = normal_values(keys[8], (DELTA_HEADS * DV, D), (DELTA_HEADS * DV) ** -0.5, 0.09375, ((0, 8),))
    norm_gain = jnp.clip(1.0 + 0.18 * jax.random.normal(keys[9], (D,), jnp.float32), 0.099609375, 1.8984375).astype(jnp.bfloat16)
    w_router = normal_values(keys[10], (D, EXPERTS), D ** -0.5, 0.125)
    expert_ids = picks_of(keys[11], PREFILL_LENGTH * REQUEST_COUNT, EXPERTS, TOPK, 1024).reshape((PREFILL_LENGTH, REQUEST_COUNT, TOPK))
    w_gate = normal_values(keys[12], (EXPERTS, D, FF), D ** -0.5, 0.125, ((0, 128),))
    w_up = normal_values(keys[13], (EXPERTS, D, FF), D ** -0.5, 0.125, ((0, 128),))
    w_down = normal_values(keys[14], (EXPERTS, FF, D), FF ** -0.5, 0.1875, ((0, 128),))
    dec_query = normal_values(keys[15], (REQUEST_COUNT, STEPS, DELTA_HEADS, DK), 1.0, 6.0, ((0, 2), (2, 8)))
    dec_key = normal_values(keys[16], (REQUEST_COUNT, STEPS, DELTA_HEADS, DK), 1.0, 6.0, ((0, 2), (2, 8)))
    dec_value = normal_values(keys[17], (REQUEST_COUNT, STEPS, DELTA_HEADS, DV), 1.0, 6.0, ((0, 2), (2, 8), (3, 8)))
    dec_decay = draw_dec_decay(jax.random.fold_in(keys[20], 71), 0)
    dec_beta = jnp.clip(0.1 + 0.79999997 * jax.random.uniform(keys[19], (REQUEST_COUNT, STEPS, DELTA_HEADS), jnp.float32) ** shard_levels(keys[19], (REQUEST_COUNT, STEPS, DELTA_HEADS), ((0, 2), (2, 8)), -0.2, 0.2), 0.1, 0.9)
    return dict(residual=residual, queries=queries, key_in=key_in, value_in=value_in, log_decay=log_decay, update_rate=update_rate, counts=counts, init_state=init_state, w_out=w_out, norm_gain=norm_gain, w_router=w_router, expert_ids=expert_ids, w_gate=w_gate, w_up=w_up, w_down=w_down, dec_query=dec_query, dec_key=dec_key, dec_value=dec_value, dec_decay=dec_decay, dec_beta=dec_beta)


EPSILON = 1e-06
ROUTE_SCALE = 2.446
highest = lax.Precision.HIGHEST

def normalize_keys(key_rows):
    return key_rows * lax.rsqrt(lax.optimization_barrier(jnp.sum(key_rows * key_rows, axis=-1, keepdims=True)) + EPSILON)

def delta_step(carry_state, query_row, key_row, value_row, decay_row, rate_row):
    carry_state = jnp.exp(decay_row)[..., None] * carry_state
    guessed = jnp.einsum('...kv,...k->...v', carry_state, key_row, precision=highest)
    carry_state = carry_state + rate_row[..., None, None] * key_row[..., :, None] * (value_row - guessed)[..., None, :]
    output = jnp.einsum('...kv,...k->...v', carry_state, query_row, precision=highest) * query_row.shape[-1] ** (-0.5)
    return (carry_state, output)

def reference(residual, queries, key_in, value_in, log_decay, update_rate, counts, init_state, w_out, norm_gain, w_router, expert_ids, w_gate, w_up, w_down, dec_query, dec_key, dec_value, dec_decay, dec_beta):
    live_mask = (jnp.arange(PREFILL_LENGTH)[:, None] < counts[None, :]).astype(jnp.float32)
    query_all = queries.astype(jnp.float32).reshape(PREFILL_LENGTH, REQUEST_COUNT, DELTA_HEADS, DK)
    key_all = normalize_keys(key_in.astype(jnp.float32).reshape(PREFILL_LENGTH, REQUEST_COUNT, DELTA_HEADS, DK))
    value_all = value_in.astype(jnp.float32).reshape(PREFILL_LENGTH, REQUEST_COUNT, DELTA_HEADS, DV)
    decay_all = log_decay.reshape(PREFILL_LENGTH, REQUEST_COUNT, DELTA_HEADS, DK) * live_mask[:, :, None, None]
    rate_all = update_rate * live_mask[:, :, None]

    def token_step(carry_state, inputs):
        return delta_step(carry_state, *inputs)
    prefill_state, attended = lax.scan(token_step, init_state, (query_all, key_all, value_all, decay_all, rate_all))
    attended_b = attended.reshape(PREFILL_LENGTH * REQUEST_COUNT, DELTA_HEADS * DV).astype(jnp.bfloat16)
    projected = jnp.dot(attended_b, w_out, preferred_element_type=jnp.float32)
    mixed_rows = residual.reshape(PREFILL_LENGTH * REQUEST_COUNT, D).astype(jnp.float32) + projected
    normed = (mixed_rows * lax.rsqrt(lax.optimization_barrier(jnp.mean(mixed_rows * mixed_rows, axis=-1, keepdims=True)) + EPSILON) * norm_gain.astype(jnp.float32)).astype(jnp.bfloat16)
    scores = jax.nn.sigmoid(jnp.dot(normed, w_router, preferred_element_type=jnp.float32))
    flat_ids = expert_ids.reshape(PREFILL_LENGTH * REQUEST_COUNT, TOPK)
    picked = jnp.take_along_axis(scores, flat_ids, axis=1)
    weights = ROUTE_SCALE * picked / lax.optimization_barrier(jnp.sum(picked, axis=1, keepdims=True))
    groups_all = N_HALF * N_GRP
    block_rows = PREFILL_LENGTH // N_EXP
    blocked = expert_ids.reshape(N_EXP, block_rows, groups_all, REQ_G, TOPK).transpose(0, 2, 1, 3, 4)
    blocked = blocked.reshape(N_EXP * groups_all, block_rows * REQ_G * TOPK)
    onehot = (blocked[:, :, None] == jnp.arange(EXPERTS, dtype=jnp.int32)[None, None, :]).astype(jnp.int32)
    running_count = jnp.cumsum(onehot, axis=1, dtype=jnp.int32) - 1
    slot_rank = lax.optimization_barrier(jnp.sum(onehot * running_count, axis=-1, dtype=jnp.int32))
    slot_rank = slot_rank.reshape(N_EXP, groups_all, block_rows, REQ_G, TOPK).transpose(0, 2, 1, 3, 4).reshape(PREFILL_LENGTH * REQUEST_COUNT, TOPK)
    block_id = ((jnp.arange(PREFILL_LENGTH, dtype=jnp.int32) // block_rows)[:, None] * groups_all + (jnp.arange(REQUEST_COUNT, dtype=jnp.int32) // REQ_G)[None, :]).reshape(PREFILL_LENGTH * REQUEST_COUNT)
    block_id = jnp.broadcast_to(block_id[:, None], (PREFILL_LENGTH * REQUEST_COUNT, TOPK)).astype(jnp.int32)
    pick_index = jnp.arange(PREFILL_LENGTH * REQUEST_COUNT * TOPK, dtype=jnp.int32).reshape(PREFILL_LENGTH * REQUEST_COUNT, TOPK)
    slot_table = jnp.full((N_EXP * groups_all, EXPERTS, CAP), -1, dtype=jnp.int32)
    slot_table = slot_table.at[block_id, flat_ids, slot_rank].set(pick_index, mode='drop')
    weight_flat = weights.reshape(-1)

    def expert_step(running, inputs):
        gate_mat, up_mat, down_mat, table_rows = inputs
        table_rows = table_rows.reshape(-1)
        present = table_rows >= 0
        safe_idx = jnp.where(present, table_rows, 0)
        token_rows = safe_idx // TOPK
        arrived = normed[token_rows]
        gate_act = jnp.dot(arrived, gate_mat, preferred_element_type=jnp.float32)
        up_act = jnp.dot(arrived, up_mat, preferred_element_type=jnp.float32)
        inner = (jax.nn.silu(gate_act) * up_act).astype(jnp.bfloat16)
        expert_out = jnp.dot(inner, down_mat, preferred_element_type=jnp.float32).astype(jnp.bfloat16).astype(jnp.float32)
        pick_scale = jnp.where(present, weight_flat[safe_idx], 0.0)
        return (running.at[token_rows].add(expert_out * pick_scale[:, None]), None)
    routed, _ = lax.scan(expert_step, jnp.zeros((PREFILL_LENGTH * REQUEST_COUNT, D), jnp.float32), (w_gate, w_up, w_down, slot_table.transpose(1, 0, 2)))
    hidden_out = (mixed_rows + routed).astype(jnp.bfloat16).reshape(PREFILL_LENGTH, REQUEST_COUNT, D)
    dec_q = dec_query.astype(jnp.float32)
    dec_k = normalize_keys(dec_key.astype(jnp.float32))
    dec_v = dec_value.astype(jnp.float32)
    carry_state = prefill_state
    outputs = []
    for turn_idx in range(STEPS):
        carry_state, output = delta_step(carry_state, dec_q[:, turn_idx], dec_k[:, turn_idx], dec_v[:, turn_idx], dec_decay[:, turn_idx], dec_beta[:, turn_idx])
        outputs.append(output)
    dec_out = jnp.stack(outputs, axis=1)
    return (hidden_out, dec_out, carry_state)
```

```python
import functools

import jax
import jax.numpy as jnp
from jax import lax
from jax.experimental import pallas as pl
from jax.experimental.pallas import tpu as pltpu
from jax.sharding import PartitionSpec as P

EPSILON = 1e-06
ROUTE_SCALE = 2.446
LANES = 128
BLOCK = 64
MIB = 1 << 20
F32 = jnp.float32
BF16 = jnp.bfloat16

NN = (((1,), (0,)), ((), ()))
NT = (((1,), (1,)), ((), ()))
TN = (((0,), (0,)), ((), ()))


def dot(left, right, dims=NN):
    return lax.dot_general(left, right, dims, preferred_element_type=F32)


def halves(member):
    high = member.astype(BF16)
    return high, (member - high.astype(F32)).astype(BF16)


def dot3(left, right, dims=NN):
    return (
        dot(left[0], right[0], dims) + dot(left[0], right[1], dims) + dot(left[1], right[0], dims)
    )


def iota(shape, dim):
    return lax.broadcasted_iota(jnp.int32, shape, dim)


def delta_kernel(
    counts, q_ref, k_ref, v_ref, d_ref, rate_ref, init_ref, w_ref,
    part_ref, final_ref,
    state, rate_col, q_all, k_all, v_all, att,
):
    step = pl.program_id(0)
    chains, key_dim, _ = init_ref.shape
    requests = chains // (w_ref.shape[0] // LANES)
    heads = chains // requests
    every = range(chains)

    @pl.when(step == 0)
    def _():
        for chain in every:
            state[chain] = init_ref[chain].T
        rate_col[...] = rate_ref[...].T

    q_all[...] = q_ref[...].astype(F32)
    k_all[...] = k_ref[...].astype(F32)
    v_all[...] = v_ref[...].astype(F32)

    row = iota((BLOCK, BLOCK), 0)
    col = iota((BLOCK, BLOCK), 1)
    lower = jnp.where(row >= col, 1.0, 0.0).astype(BF16)
    position = step * BLOCK + iota((BLOCK, 1), 0)
    rates = rate_col[pl.ds(pl.multiple_of(step * BLOCK, BLOCK), BLOCK), :]
    live = [position < counts[request] for request in range(requests)]
    live = [live[chain // heads] for chain in every]
    rows = [pl.ds((c % heads) * requests + c // heads, BLOCK, stride=chains) for c in every]

    withins = []
    for c in every:
        decay = jnp.where(live[c], d_ref[rows[c], :], 0.0)
        high, rest = decay.astype(BF16), decay - decay.astype(BF16).astype(F32)
        middle, low = halves(rest)
        withins.append(dot(lower, high) + dot(lower, middle) + dot(lower, low))
    rate = [jnp.where(live[c], rates[:, c : c + 1], 0.0) for c in every]
    key_up, key_end, query_up, fades, systems, reaches = [], [], [], [], [], []
    for c in every:
        key = k_all[rows[c], :]
        key = key * lax.rsqrt(jnp.sum(key * key, axis=-1, keepdims=True) + EPSILON)
        grow = jnp.exp(withins[c])
        fade = grow[BLOCK - 1 :, :]
        down = key * jnp.exp(-withins[c])
        up_hi, up_lo = halves(key * grow)
        down_hi, down_lo = halves(down)
        query = (q_all[rows[c], :] * grow).astype(BF16)
        both = dot(jnp.concatenate([up_hi, query], axis=0), down_hi, NT)
        pair = both[:BLOCK] + dot(up_hi, down_lo, NT) + dot(up_lo, down_hi, NT)
        reaches.append(jnp.where(row >= col, both[BLOCK:], 0.0).astype(BF16))
        systems.append(jnp.where(row > col, rate[c] * pair, 0.0))
        key_up.append(key * grow)
        key_end.append(halves(down * fade))
        query_up.append(query)
        fades.append(fade)
    near = row >> 1 == col >> 1
    inverse = [jnp.where(row == col, 1.0, 0.0) - jnp.where(near, s, 0.0) for s in systems]
    for bit in range(1, BLOCK.bit_length() - 1):
        joins = (row >> (bit + 1) == col >> (bit + 1)) & (row >> bit != col >> bit)
        split = [halves(member) for member in inverse]
        inner = [
            dot3(halves(jnp.where(joins, systems[c], 0.0)), split[c]) for c in every
        ]
        inverse = [inverse[c] - dot3(split[c], halves(inner[c])) for c in every]
    split = [halves(member) for member in inverse]
    base_v = [dot3(split[c], halves(rate[c] * v_all[rows[c], :])) for c in every]
    base_k = [halves(dot3(split[c], halves(rate[c] * key_up[c]))) for c in every]
    boths, carries, updates = [], [], []
    for c in every:
        carry = halves(state[c])
        both = dot(jnp.concatenate([base_k[c][0], query_up[c]], axis=0), carry[0], NT)
        reached = both[:BLOCK] + dot(base_k[c][0], carry[1], NT) + dot(base_k[c][1], carry[0], NT)
        updates.append(halves(base_v[c] - reached))
        boths.append(both[BLOCK:])
    for c in every:
        state[c] = fades[c] * state[c] + dot3(updates[c], key_end[c], TN)
    for c in every:
        request, head = divmod(c, heads)
        out = (boths[c] + dot(reaches[c], updates[c][0])) * key_dim ** (-0.5)
        att[request * BLOCK : (request + 1) * BLOCK, head * LANES : (head + 1) * LANES] = (
            out.astype(BF16)
        )

    width = w_ref.shape[1]
    for lane in range(0, width, 768):
        part_ref[0, :, lane : lane + 768] = dot(att[...], w_ref[:, lane : lane + 768]).astype(BF16)

    @pl.when(step == pl.num_programs(0) - 1)
    def _():
        for c in every:
            final_ref[c] = state[c].astype(BF16)


def delta(counts, queries, key_in, value_in, log_decay, update_rate, init_state, w_out):
    length, requests, features = queries.shape
    heads, key_dim, value_dim = init_state.shape[1:]
    chains = requests * heads
    width = w_out.shape[1]

    def rows_of(member):
        member = member.reshape(length, requests, heads, key_dim)
        return member.transpose(0, 2, 1, 3).reshape(length * chains, key_dim)

    def whole(*shape):
        return pl.BlockSpec(shape, lambda n, *_: (0,) * len(shape))

    tall = BLOCK * chains
    block = pl.BlockSpec((tall, key_dim), lambda n, *_: (n, 0))
    steps = length // BLOCK
    return pl.pallas_call(
        delta_kernel,
        grid_spec=pltpu.PrefetchScalarGridSpec(
            num_scalar_prefetch=1,
            grid=(steps,),
            in_specs=[block] * 4
            + [
                whole(chains, length),
                whole(chains, key_dim, value_dim),
                whole(features, width),
            ],
            out_specs=[
                pl.BlockSpec((1, requests * BLOCK, width), lambda n, *_: (n, 0, 0)),
                whole(chains, value_dim, key_dim),
            ],
            scratch_shapes=[
                pltpu.VMEM((chains, value_dim, key_dim), F32),
                pltpu.VMEM((length, chains), F32),
                pltpu.VMEM((tall, key_dim), F32),
                pltpu.VMEM((tall, key_dim), F32),
                pltpu.VMEM((tall, value_dim), F32),
                pltpu.VMEM((requests * BLOCK, features), BF16),
            ],
        ),
        out_shape=[
            jax.ShapeDtypeStruct((steps, requests * BLOCK, width), BF16),
            jax.ShapeDtypeStruct((chains, value_dim, key_dim), BF16),
        ],
        compiler_params=pltpu.CompilerParams(vmem_limit_bytes=40 * MIB),
        name="delta",
    )(
        counts,
        rows_of(queries),
        rows_of(key_in),
        rows_of(value_in),
        rows_of(log_decay),
        update_rate.transpose(1, 2, 0).reshape(chains, length),
        init_state.reshape(chains, key_dim, value_dim),
        w_out,
    )


def expand(table, rows_each):
    count = table.shape[0]
    tall = count * rows_each
    first = iota((tall, count), 1) * rows_each
    row = iota((tall, count), 0)
    pick = jnp.where((row >= first) & (row < first + rows_each), 1.0, 0.0).astype(BF16)
    return dot(pick, table)


def route_kernel(
    res_ref, part_ref, gain_ref, router_ref, ids_ref,
    mixed_ref, slot_ref, weight_ref, out_ref,
    wide, normed,
):
    members, tokens, width = part_ref.shape
    requests = tokens // BLOCK
    chunks = width // LANES
    experts = router_ref.shape[1]
    wide[...] = res_ref[...].astype(F32)
    squares = jnp.zeros((tokens, LANES), F32)
    for chunk in range(chunks):
        lanes = slice(chunk * LANES, (chunk + 1) * LANES)
        total = jnp.concatenate(
            [
                wide[pl.ds(chunk * requests + r, BLOCK, stride=chunks * requests), :]
                for r in range(requests)
            ],
            axis=0,
        )
        for member in range(members):
            total = total + part_ref[member, :, lanes].astype(F32)
        mixed_ref[:, lanes] = total
        squares = squares + total * total
    scale = lax.rsqrt(jnp.sum(squares, axis=-1, keepdims=True) / width + EPSILON)
    for chunk in range(chunks):
        lanes = slice(chunk * LANES, (chunk + 1) * LANES)
        normed[:, lanes] = (mixed_ref[:, lanes] * scale * gain_ref[:, lanes].astype(F32)).astype(
            BF16
        )

    number = iota((experts, tokens), 0)
    chosen = jnp.zeros((experts, tokens), F32)
    for pick in range(ids_ref.shape[0]):
        chosen = chosen + jnp.where(ids_ref[pick : pick + 1, :] == number, 1.0, 0.0)
    row, col = iota((tokens, tokens), 0), iota((tokens, tokens), 1)
    row = (row & (BLOCK - 1)) * requests + (row >> (BLOCK.bit_length() - 1))
    col = (col & (BLOCK - 1)) * requests + (col >> (BLOCK.bit_length() - 1))
    earlier = jnp.where(row < col, 1.0, 0.0).astype(BF16)
    slot = jnp.where(chosen > 0.0, dot(chosen.astype(BF16), earlier), -1.0)
    slot_ref[...] = slot.T

    scores = jax.nn.sigmoid(dot(normed[...], router_ref[...])) * chosen.T
    weight_ref[...] = ROUTE_SCALE * scores / jnp.sum(scores, axis=-1, keepdims=True)

    place = expand(slot.astype(BF16), 8)
    line = iota(place.shape, 0)
    head = jnp.where(place == (line & 7).astype(F32), 1.0, 0.0).astype(BF16)
    tail = place == ((line & 3) + 8).astype(F32)
    tail_a = jnp.where(tail & ((line & 4) == 0), 1.0, 0.0).astype(BF16)
    tail_b = jnp.where(tail & ((line & 4) != 0), 1.0, 0.0).astype(BF16)
    half = width // 2
    step = 3 * LANES
    for lane in range(0, width, step):
        out_ref[:, lane : lane + step] = dot(head, normed[:, lane : lane + step]).astype(BF16)
    for lane in range(0, half, step):
        out_ref[:, width + lane : width + lane + step] = (
            dot(tail_a, normed[:, lane : lane + step])
            + dot(tail_b, normed[:, half + lane : half + lane + step])
        ).astype(BF16)


def interleave(member):
    length, requests, width = member.shape
    member = member.reshape(length, requests, width // LANES, LANES).transpose(0, 2, 1, 3)
    return member.reshape(-1, LANES)


def route(residual, parts, norm_gain, w_router, expert_ids):
    length, requests, width = residual.shape
    tokens = length * requests
    experts = w_router.shape[1]
    ids = expert_ids.transpose(2, 1, 0).reshape(-1, tokens)
    vmem = pl.BlockSpec(memory_space=pltpu.VMEM)
    return pl.pallas_call(
        route_kernel,
        in_specs=[vmem] * 5,
        out_specs=[vmem] * 4,
        scratch_shapes=[
            pltpu.VMEM((tokens * width // LANES, LANES), F32),
            pltpu.VMEM((tokens, width), BF16),
        ],
        out_shape=[
            jax.ShapeDtypeStruct((tokens, width), F32),
            jax.ShapeDtypeStruct((tokens, experts), F32),
            jax.ShapeDtypeStruct((tokens, experts), F32),
            jax.ShapeDtypeStruct((experts * 8, width * 3 // 2), BF16),
        ],
        compiler_params=pltpu.CompilerParams(vmem_limit_bytes=40 * MIB),
        name="route",
    )(interleave(residual), parts, norm_gain.reshape(1, width), w_router, ids)


GROUP = 256


def unpack_rows(dtype=BF16):
    row, col = iota((GROUP, GROUP), 0), iota((GROUP, GROUP), 1)
    half = GROUP // 2
    inside = row & (half - 1)
    source = ((inside >> 2) << 3) + (inside & 3) + jnp.where(row >= half, 4, 0)
    return jnp.where(col == source, 1.0, 0.0).astype(dtype)


def expert_kernel(x_ref, gate_ref, up_ref, down_ref, out_ref, tail_in, tail_out, inner, *, ups):
    step = pl.program_id(0)
    rows, across = x_ref.shape
    width = across * 2 // 3
    half = width // 2
    tails = rows // 2
    fold = gate_ref.shape[1]
    tile = down_ref.shape[1]

    @pl.when(step == 0)
    def _():
        order = unpack_rows()
        for group in range(rows // GROUP):
            moved = dot(order, x_ref[pl.ds(group * GROUP, GROUP), width:]).astype(BF16)
            here = pl.ds(group * GROUP // 2, GROUP // 2)
            tail_in[here, :half] = moved[: GROUP // 2]
            tail_in[here, half:] = moved[GROUP // 2 :]

    @pl.when(step < ups)
    def _():
        def act(lines):
            gate = dot(lines, gate_ref[...])
            up = dot(lines, up_ref[...])
            return (gate / (1.0 + jnp.exp(-gate)) * up).astype(BF16)

        lanes = pl.ds(pl.multiple_of(step * fold, fold), fold)

        @pl.loop(0, rows // GROUP)
        def _(group):
            here = pl.ds(pl.multiple_of(group * GROUP, GROUP), GROUP)
            inner[here, lanes] = act(x_ref[here, :width])

        @pl.loop(0, tails // GROUP)
        def _(group):
            here = pl.ds(pl.multiple_of(group * GROUP, GROUP), GROUP)
            there = pl.ds(pl.multiple_of(rows + group * GROUP, GROUP), GROUP)
            inner[there, lanes] = act(tail_in[here, :])

    @pl.when(step >= ups)
    def _():
        lanes = pl.ds(pl.multiple_of((step - ups) * tile, tile), tile)

        @pl.loop(0, rows // GROUP)
        def _(group):
            here = pl.ds(pl.multiple_of(group * GROUP, GROUP), GROUP)
            out_ref[here, lanes] = dot(inner[here, :], down_ref[...]).astype(BF16)

        @pl.loop(0, tails // GROUP)
        def _(group):
            here = pl.ds(pl.multiple_of(group * GROUP, GROUP), GROUP)
            there = pl.ds(pl.multiple_of(rows + group * GROUP, GROUP), GROUP)
            tail_out[here, lanes] = dot(inner[there, :], down_ref[...]).astype(BF16)

    @pl.when(step == pl.num_programs(0) - 1)
    def _():
        order = unpack_rows()
        for group in range(rows // GROUP):
            here = pl.ds(group * GROUP // 2, GROUP // 2)
            moved = jnp.concatenate([tail_out[here, :half], tail_out[here, half:]], axis=0)
            out_ref[pl.ds(group * GROUP, GROUP), width:] = dot(order, moved, TN).astype(BF16)


def experts_of(arrived, gate, up, down):
    rows, across = arrived.shape
    width, hidden = gate.shape
    fold, tile = 256, 384
    ups, downs = hidden // fold, width // tile
    tails = rows // 2

    def column(step):
        return (0, jnp.minimum(step, ups - 1))

    def later(step):
        return (0, jnp.maximum(step - ups, 0))

    whole = pl.BlockSpec((rows, across), lambda step: (0, 0))
    return pl.pallas_call(
        functools.partial(expert_kernel, ups=ups),
        grid=(ups + downs,),
        in_specs=[
            whole,
            pl.BlockSpec((width, fold), column),
            pl.BlockSpec((width, fold), column),
            pl.BlockSpec((hidden, tile), later),
        ],
        out_specs=whole,
        scratch_shapes=[
            pltpu.VMEM((tails, width), BF16),
            pltpu.VMEM((tails, width), BF16),
            pltpu.VMEM((rows + tails, hidden), BF16),
        ],
        out_shape=jax.ShapeDtypeStruct((rows, across), BF16),
        compiler_params=pltpu.CompilerParams(vmem_limit_bytes=56 * MIB),
        name="experts",
    )(arrived, gate, up, down)


def combine_kernel(
    mixed_ref, slot_ref, weight_ref, head_ref, tail_ref, out_ref, total, heads, tails, wide
):
    step = pl.program_id(0)
    tokens, width = mixed_ref.shape
    rows = head_ref.shape[0]
    requests = tokens // BLOCK
    chunks = width // LANES
    half = width // 2

    @pl.when(step == 0)
    def _():
        total[...] = mixed_ref[...]
        first = iota((slot_ref.shape[1], rows), 0) * 8
        col = iota((slot_ref.shape[1], rows), 1)
        pick = jnp.where((col >= first) & (col < first + 8), 1.0, 0.0).astype(BF16)
        place = dot(slot_ref[...].astype(BF16), pick)
        line = iota(place.shape, 1)
        is_head = place == (line & 7).astype(F32)
        is_tail = place == ((line & 3) + 8).astype(F32)
        for index, part in enumerate(halves(weight_ref[...])):
            spread = dot(part, pick)
            here = slice(index * tokens, (index + 1) * tokens)
            heads[here, :] = jnp.where(is_head, spread, 0.0).astype(BF16)
            tails[0, here, :] = jnp.where(is_tail & ((line & 4) == 0), spread, 0.0).astype(BF16)
            tails[1, here, :] = jnp.where(is_tail & ((line & 4) != 0), spread, 0.0).astype(BF16)

    tile, thin = head_ref.shape[1], tail_ref.shape[1]
    lanes = pl.ds(pl.multiple_of(step * tile, tile), tile)
    both = dot(heads[...], head_ref[...])
    total[:, lanes] += both[:tokens] + both[tokens:]
    for side in range(2):
        lanes = pl.ds(pl.multiple_of(side * half + step * thin, thin), thin)
        both = dot(tails[side], tail_ref[...])
        total[:, lanes] += both[:tokens] + both[tokens:]

    @pl.when(step == pl.num_programs(0) - 1)
    def _():
        for chunk in range(chunks):
            for r in range(requests):
                rows_here = pl.ds(chunk * requests + r, BLOCK, stride=chunks * requests)
                wide[rows_here, :] = total[
                    r * BLOCK : (r + 1) * BLOCK, chunk * LANES : (chunk + 1) * LANES
                ]
        out_ref[...] = wide[...].astype(BF16)


def combine(mixed, slot, weight, back):
    tokens, width = mixed.shape
    rows, across = back.shape
    tile, thin = 256, 128
    steps = width // tile

    def whole(member):
        return pl.BlockSpec(member.shape, lambda step: (0, 0))

    lines = tokens * width // LANES
    return pl.pallas_call(
        combine_kernel,
        grid=(steps,),
        in_specs=[
            whole(mixed),
            whole(slot),
            whole(weight),
            pl.BlockSpec((rows, tile), lambda step: (0, step)),
            pl.BlockSpec((rows, thin), lambda step: (0, width // thin + step)),
        ],
        out_specs=pl.BlockSpec((lines, LANES), lambda step: (0, 0)),
        scratch_shapes=[
            pltpu.VMEM((tokens, width), F32),
            pltpu.VMEM((2 * tokens, rows), BF16),
            pltpu.VMEM((2, 2 * tokens, rows), BF16),
            pltpu.VMEM((lines, LANES), F32),
        ],
        out_shape=jax.ShapeDtypeStruct((lines, LANES), BF16),
        compiler_params=pltpu.CompilerParams(vmem_limit_bytes=40 * MIB),
        name="combine",
    )(mixed, slot, weight, back, back)


def decode(relaid, dec_query, dec_key, dec_value, dec_decay, dec_beta):
    query = dec_query.astype(F32)
    key = dec_key.astype(F32)
    key = key * lax.rsqrt(jnp.sum(key * key, axis=-1, keepdims=True) + EPSILON)
    value = dec_value.astype(F32)
    state = relaid.astype(F32)
    outs = []
    for turn in range(dec_query.shape[1]):
        state = jnp.exp(dec_decay[:, turn])[..., None, :] * state
        guessed = jnp.sum(state * key[:, turn, :, None, :], axis=-1)
        update = dec_beta[:, turn, :, None] * (value[:, turn] - guessed)
        state = state + update[..., None] * key[:, turn, :, None, :]
        outs.append(jnp.sum(state * query[:, turn, :, None, :], axis=-1))
    out = jnp.stack(outs, axis=1) * dec_query.shape[-1] ** (-0.5)
    return out, state.transpose(0, 1, 3, 2)


def shards(
    residual, queries, key_in, value_in, log_decay, update_rate, counts, init_state, w_out,
    norm_gain, w_router, expert_ids, w_gate, w_up, w_down,
    dec_query, dec_key, dec_value, dec_decay, dec_beta,
):
    rows_here, requests, width = residual.shape
    heads, key_dim, value_dim = init_state.shape[1:]
    members = lax.axis_size("exp")
    experts = w_router.shape[1]
    parts, final = delta(
        counts, queries, key_in, value_in, log_decay, update_rate, init_state, w_out
    )
    parts = lax.all_to_all(parts, "exp", split_axis=0, concat_axis=0, tiled=True)
    mixed, slot, weight, outgoing = route(residual, parts, norm_gain, w_router, expert_ids)

    def exchange(member):
        member = member.reshape(experts, 8, -1)
        member = lax.all_to_all(
            member, ("half", "grp", "exp"), split_axis=0, concat_axis=0, tiled=True
        )
        return member.reshape(experts * 8, -1)

    arrived = exchange(outgoing)
    back = exchange(experts_of(arrived, w_gate[0], w_up[0], w_down[0]))

    final = final.reshape(requests, heads, members, value_dim // members, key_dim)
    final = lax.all_to_all(final, "exp", split_axis=2, concat_axis=1, tiled=True)
    final = final.reshape(requests, members * heads, value_dim // members, key_dim)
    relaid = lax.all_to_all(final, "grp", split_axis=1, concat_axis=0, tiled=True)
    dec_out, dec_state = decode(relaid, dec_query, dec_key, dec_value, dec_decay, dec_beta)

    hidden = combine(mixed, slot, weight, back)
    hidden = hidden.reshape(rows_here, width // LANES, requests, LANES).transpose(0, 2, 1, 3)
    return hidden.reshape(rows_here, requests, width), dec_out, dec_state


def solution(mesh):
    return jax.shard_map(
        shards,
        mesh=mesh,
        in_specs=(
            P("exp", ("half", "grp"), None),
            P(None, ("half", "grp"), "exp"),
            P(None, ("half", "grp"), "exp"),
            P(None, ("half", "grp"), "exp"),
            P(None, ("half", "grp"), "exp"),
            P(None, ("half", "grp"), "exp"),
            P(("half", "grp")),
            P(("half", "grp"), "exp", None, None),
            P("exp", None),
            P(),
            P(),
            P("exp", ("half", "grp"), None),
            P(("half", "grp", "exp"), None, None),
            P(("half", "grp", "exp"), None, None),
            P(("half", "grp", "exp"), None, None),
            P("half", None, "grp", None),
            P("half", None, "grp", None),
            P("half", None, "grp", "exp"),
            P("half", None, "grp", None),
            P("half", None, "grp"),
        ),
        out_specs=(
            P("exp", ("half", "grp"), None),
            P("half", None, "grp", "exp"),
            P("half", "grp", None, "exp"),
        ),
        check_vma=False,
    )
```

```python
import functools

import jax
import jax.numpy as jnp
from jax import lax
from jax.experimental import pallas as pl
from jax.experimental.pallas import tpu as pltpu
from jax.sharding import PartitionSpec as P

EPSILON = 1e-06
ROUTE_SCALE = 2.446
LANES = 128
BLOCK = 64
VMEM = 60 << 20
F32 = jnp.float32
BF16 = jnp.bfloat16

NN = (((1,), (0,)), ((), ()))
NT = (((1,), (1,)), ((), ()))
TN = (((0,), (0,)), ((), ()))


def dot(left, right, dims=NN):
    return lax.dot_general(left, right, dims, preferred_element_type=F32)


def halves(member):
    high = member.astype(BF16)
    return high, (member - high.astype(F32)).astype(BF16)


def dot3(left, right, dims=NN):
    return (
        dot(left[0], right[0], dims) + dot(left[0], right[1], dims) + dot(left[1], right[0], dims)
    )


def iota(shape, dim):
    return lax.broadcasted_iota(jnp.int32, shape, dim)


def delta_kernel(
    counts, q_ref, k_ref, v_ref, d_ref, rate_ref, init_ref, w_ref,
    part_ref, final_ref,
    state, rate_col, q_all, k_all, v_all, att,
):
    step = pl.program_id(0)
    chains, key_dim, _ = init_ref.shape
    requests = chains // (w_ref.shape[0] // LANES)
    heads = chains // requests
    every = range(chains)

    @pl.when(step == 0)
    def _():
        for chain in every:
            state[chain] = init_ref[chain].T
        rate_col[...] = rate_ref[...].T

    q_all[...] = q_ref[...].astype(F32)
    k_all[...] = k_ref[...].astype(F32)
    v_all[...] = v_ref[...].astype(F32)

    row = iota((BLOCK, BLOCK), 0)
    col = iota((BLOCK, BLOCK), 1)
    lower = jnp.where(row >= col, 1.0, 0.0).astype(BF16)
    position = step * BLOCK + iota((BLOCK, 1), 0)
    rates = rate_col[pl.ds(pl.multiple_of(step * BLOCK, BLOCK), BLOCK), :]
    live = [position < counts[request] for request in range(requests)]
    live = [live[chain // heads] for chain in every]
    rows = [pl.ds((c % heads) * requests + c // heads, BLOCK, stride=chains) for c in every]

    withins = []
    for c in every:
        decay = jnp.where(live[c], d_ref[rows[c], :], 0.0)
        high, rest = decay.astype(BF16), decay - decay.astype(BF16).astype(F32)
        middle, low = halves(rest)
        withins.append(dot(lower, high) + dot(lower, middle) + dot(lower, low))
    rate = [jnp.where(live[c], rates[:, c : c + 1], 0.0) for c in every]
    key_up, key_end, query_up, fades, systems, reaches = [], [], [], [], [], []
    for c in every:
        key = k_all[rows[c], :]
        key = key * lax.rsqrt(jnp.sum(key * key, axis=-1, keepdims=True) + EPSILON)
        grow = jnp.exp(withins[c])
        fade = grow[BLOCK - 1 :, :]
        down = key * jnp.exp(-withins[c])
        up_hi, up_lo = halves(key * grow)
        down_hi, down_lo = halves(down)
        query = (q_all[rows[c], :] * grow).astype(BF16)
        both = dot(jnp.concatenate([up_hi, query], axis=0), down_hi, NT)
        pair = both[:BLOCK] + dot(up_hi, down_lo, NT) + dot(up_lo, down_hi, NT)
        reaches.append(jnp.where(row >= col, both[BLOCK:], 0.0).astype(BF16))
        systems.append(jnp.where(row > col, rate[c] * pair, 0.0))
        key_up.append(key * grow)
        key_end.append(halves(down * fade))
        query_up.append(query)
        fades.append(fade)
    near = row >> 1 == col >> 1
    inverse = [jnp.where(row == col, 1.0, 0.0) - jnp.where(near, s, 0.0) for s in systems]
    for bit in range(1, BLOCK.bit_length() - 1):
        joins = (row >> (bit + 1) == col >> (bit + 1)) & (row >> bit != col >> bit)
        split = [halves(member) for member in inverse]
        inner = [
            dot3(halves(jnp.where(joins, systems[c], 0.0)), split[c]) for c in every
        ]
        inverse = [inverse[c] - dot3(split[c], halves(inner[c])) for c in every]
    split = [halves(member) for member in inverse]
    base_v = [dot3(split[c], halves(rate[c] * v_all[rows[c], :])) for c in every]
    base_k = [halves(dot3(split[c], halves(rate[c] * key_up[c]))) for c in every]
    boths, carries, updates = [], [], []
    for c in every:
        carry = halves(state[c])
        both = dot(jnp.concatenate([base_k[c][0], query_up[c]], axis=0), carry[0], NT)
        reached = both[:BLOCK] + dot(base_k[c][0], carry[1], NT) + dot(base_k[c][1], carry[0], NT)
        updates.append(halves(base_v[c] - reached))
        boths.append(both[BLOCK:])
    for c in every:
        state[c] = fades[c] * state[c] + dot3(updates[c], key_end[c], TN)
    for c in every:
        request, head = divmod(c, heads)
        out = (boths[c] + dot(reaches[c], updates[c][0])) * key_dim ** (-0.5)
        att[request * BLOCK : (request + 1) * BLOCK, head * LANES : (head + 1) * LANES] = (
            out.astype(BF16)
        )

    width = w_ref.shape[1]
    for lane in range(0, width, 768):
        part_ref[0, :, lane : lane + 768] = dot(att[...], w_ref[:, lane : lane + 768]).astype(BF16)

    @pl.when(step == pl.num_programs(0) - 1)
    def _():
        columns = final_ref.shape[1] // chains
        for c in every:
            for member in range(final_ref.shape[0]):
                final_ref[member, c * columns : (c + 1) * columns, :] = state[
                    c, member * columns : (member + 1) * columns, :
                ].astype(BF16)


def delta(counts, queries, key_in, value_in, log_decay, update_rate, init_state, w_out, members):
    length, requests, features = queries.shape
    heads, key_dim, value_dim = init_state.shape[1:]
    chains = requests * heads
    width = w_out.shape[1]

    def rows_of(member):
        member = member.reshape(length, requests, heads, key_dim)
        return member.transpose(0, 2, 1, 3).reshape(length * chains, key_dim)

    def whole(*shape):
        return pl.BlockSpec(shape, lambda n, *_: (0,) * len(shape))

    tall = BLOCK * chains
    block = pl.BlockSpec((tall, key_dim), lambda n, *_: (n, 0))
    steps = length // BLOCK
    return pl.pallas_call(
        delta_kernel,
        grid_spec=pltpu.PrefetchScalarGridSpec(
            num_scalar_prefetch=1,
            grid=(steps,),
            in_specs=[block] * 4
            + [
                whole(chains, length),
                whole(chains, key_dim, value_dim),
                whole(features, width),
            ],
            out_specs=[
                pl.BlockSpec((1, requests * BLOCK, width), lambda n, *_: (n, 0, 0)),
                whole(members, chains * value_dim // members, key_dim),
            ],
            scratch_shapes=[
                pltpu.VMEM((chains, value_dim, key_dim), F32),
                pltpu.VMEM((length, chains), F32),
                pltpu.VMEM((tall, key_dim), F32),
                pltpu.VMEM((tall, key_dim), F32),
                pltpu.VMEM((tall, value_dim), F32),
                pltpu.VMEM((requests * BLOCK, features), BF16),
            ],
        ),
        out_shape=[
            jax.ShapeDtypeStruct((steps, requests * BLOCK, width), BF16),
            jax.ShapeDtypeStruct((members, chains * value_dim // members, key_dim), BF16),
        ],
        compiler_params=pltpu.CompilerParams(vmem_limit_bytes=VMEM),
        name="delta",
    )(
        counts,
        rows_of(queries),
        rows_of(key_in),
        rows_of(value_in),
        rows_of(log_decay),
        update_rate.transpose(1, 2, 0).reshape(chains, length),
        init_state.reshape(chains, key_dim, value_dim),
        w_out,
    )


def place_of(expert):
    return ((expert & 7) << 4) + (((expert >> 3) & 7) << 1) + (expert >> 6)


def picker(experts, rows, dim):
    shape = (experts, rows) if dim == 0 else (rows, experts)
    first = place_of(iota(shape, dim)) * 8
    row = iota(shape, 1 - dim)
    return jnp.where((row >= first) & (row < first + 8), 1.0, 0.0).astype(BF16)


def route_kernel(
    res_ref, part_ref, gain_ref, router_ref, ids_ref,
    mixed_ref, slot_ref, weight_ref, out_ref,
    wide, normed,
):
    members, tokens, width = part_ref.shape
    requests = tokens // BLOCK
    chunks = width // LANES
    experts = router_ref.shape[1]
    wide[...] = res_ref[...].astype(F32)
    squares = jnp.zeros((tokens, LANES), F32)
    for chunk in range(chunks):
        lanes = slice(chunk * LANES, (chunk + 1) * LANES)
        total = jnp.concatenate(
            [
                wide[pl.ds(chunk * requests + r, BLOCK, stride=chunks * requests), :]
                for r in range(requests)
            ],
            axis=0,
        )
        for member in range(members):
            total = total + part_ref[member, :, lanes].astype(F32)
        mixed_ref[:, lanes] = total
        squares = squares + total * total
    scale = lax.rsqrt(jnp.sum(squares, axis=-1, keepdims=True) / width + EPSILON)
    for chunk in range(chunks):
        lanes = slice(chunk * LANES, (chunk + 1) * LANES)
        normed[:, lanes] = (mixed_ref[:, lanes] * scale * gain_ref[:, lanes].astype(F32)).astype(
            BF16
        )

    number = iota((experts, tokens), 0)
    chosen = jnp.zeros((experts, tokens), F32)
    for pick in range(ids_ref.shape[0]):
        chosen = chosen + jnp.where(ids_ref[pick : pick + 1, :] == number, 1.0, 0.0)
    row, col = iota((tokens, tokens), 0), iota((tokens, tokens), 1)
    row = (row & (BLOCK - 1)) * requests + (row >> (BLOCK.bit_length() - 1))
    col = (col & (BLOCK - 1)) * requests + (col >> (BLOCK.bit_length() - 1))
    earlier = jnp.where(row < col, 1.0, 0.0).astype(BF16)
    slot = jnp.where(chosen > 0.0, dot(chosen.astype(BF16), earlier), -1.0)
    slot_ref[...] = slot.T

    scores = jax.nn.sigmoid(dot(normed[...], router_ref[...])) * chosen.T
    weight_ref[...] = ROUTE_SCALE * scores / jnp.sum(scores, axis=-1, keepdims=True)

    place = dot(picker(experts, experts * 8, 1), slot.astype(BF16))
    line = iota(place.shape, 0)
    head = jnp.where(place == (line & 7).astype(F32), 1.0, 0.0).astype(BF16)
    tail = place == ((line & 3) + 8).astype(F32)
    tail_a = jnp.where(tail & ((line & 4) == 0), 1.0, 0.0).astype(BF16)
    tail_b = jnp.where(tail & ((line & 4) != 0), 1.0, 0.0).astype(BF16)
    half = width // 2
    step = 6 * LANES
    for lane in range(0, width, step):
        out_ref[:, lane : lane + step] = dot(head, normed[:, lane : lane + step]).astype(BF16)
    step = 3 * LANES
    for lane in range(0, half, step):
        out_ref[:, width + lane : width + lane + step] = (
            dot(tail_a, normed[:, lane : lane + step])
            + dot(tail_b, normed[:, half + lane : half + lane + step])
        ).astype(BF16)


def interleave(member):
    length, requests, width = member.shape
    member = member.reshape(length, requests, width // LANES, LANES).transpose(0, 2, 1, 3)
    return member.reshape(-1, LANES)


def route(residual, parts, norm_gain, w_router, expert_ids):
    length, requests, width = residual.shape
    tokens = length * requests
    experts = w_router.shape[1]
    ids = expert_ids.transpose(2, 1, 0).reshape(-1, tokens)
    vmem = pl.BlockSpec(memory_space=pltpu.VMEM)
    return pl.pallas_call(
        route_kernel,
        in_specs=[vmem] * 5,
        out_specs=[vmem] * 4,
        scratch_shapes=[
            pltpu.VMEM((tokens * width // LANES, LANES), F32),
            pltpu.VMEM((tokens, width), BF16),
        ],
        out_shape=[
            jax.ShapeDtypeStruct((tokens, width), F32),
            jax.ShapeDtypeStruct((tokens, experts), F32),
            jax.ShapeDtypeStruct((tokens, experts), F32),
            jax.ShapeDtypeStruct((experts * 8, width * 3 // 2), BF16),
        ],
        compiler_params=pltpu.CompilerParams(vmem_limit_bytes=VMEM),
        name="route",
    )(interleave(residual), parts, norm_gain.reshape(1, width), w_router, ids)


GROUP = 256


def unpack_rows(dtype=BF16):
    row, col = iota((GROUP, GROUP), 0), iota((GROUP, GROUP), 1)
    half = GROUP // 2
    inside = row & (half - 1)
    source = ((inside >> 2) << 3) + (inside & 3) + jnp.where(row >= half, 4, 0)
    return jnp.where(col == source, 1.0, 0.0).astype(dtype)


def expert_kernel(x_ref, gate_ref, up_ref, down_ref, out_ref, tail_in, tail_out, inner, *, ups):
    step = pl.program_id(0)
    rows, across = x_ref.shape
    width = across * 2 // 3
    half = width // 2
    tails = rows // 2
    fold = gate_ref.shape[1]
    tile = down_ref.shape[1]

    @pl.when(step == 0)
    def _():
        order = unpack_rows()
        for group in range(rows // GROUP):
            moved = dot(order, x_ref[pl.ds(group * GROUP, GROUP), width:]).astype(BF16)
            here = pl.ds(group * GROUP // 2, GROUP // 2)
            tail_in[here, :half] = moved[: GROUP // 2]
            tail_in[here, half:] = moved[GROUP // 2 :]

    @pl.when(step < ups)
    def _():
        lanes = pl.ds(pl.multiple_of(step * fold, fold), fold)
        for start in range(0, rows + tails, 256):
            if start < rows:
                lines = x_ref[start : start + 256, :width]
            else:
                lines = tail_in[start - rows : start - rows + 256, :]
            gate = dot(lines, gate_ref[...])
            up = dot(lines, up_ref[...])
            inner[start : start + 256, lanes] = (gate / (1.0 + jnp.exp(-gate)) * up).astype(BF16)

    @pl.when(step >= ups)
    def _():
        lanes = pl.ds(pl.multiple_of((step - ups) * tile, tile), tile)
        for start in range(0, rows + tails, 256):
            result = dot(inner[start : start + 256, :], down_ref[...]).astype(BF16)
            if start < rows:
                out_ref[start : start + 256, lanes] = result
            else:
                tail_out[start - rows : start - rows + 256, lanes] = result

    @pl.when(step == pl.num_programs(0) - 1)
    def _():
        order = unpack_rows()
        for group in range(rows // GROUP):
            here = pl.ds(group * GROUP // 2, GROUP // 2)
            moved = jnp.concatenate([tail_out[here, :half], tail_out[here, half:]], axis=0)
            out_ref[pl.ds(group * GROUP, GROUP), width:] = dot(order, moved, TN).astype(BF16)


def experts_of(arrived, gate, up, down):
    rows, across = arrived.shape
    width, hidden = gate.shape
    fold, tile = 256, 768
    ups, downs = hidden // fold, width // tile
    tails = rows // 2

    def column(step):
        return (0, jnp.minimum(step, ups - 1))

    def later(step):
        return (0, jnp.maximum(step - ups, 0))

    whole = pl.BlockSpec((rows, across), lambda step: (0, 0))
    return pl.pallas_call(
        functools.partial(expert_kernel, ups=ups),
        grid=(ups + downs,),
        in_specs=[
            whole,
            pl.BlockSpec((width, fold), column),
            pl.BlockSpec((width, fold), column),
            pl.BlockSpec((hidden, tile), later),
        ],
        out_specs=whole,
        scratch_shapes=[
            pltpu.VMEM((tails, width), BF16),
            pltpu.VMEM((tails, width), BF16),
            pltpu.VMEM((rows + tails, hidden), BF16),
        ],
        out_shape=jax.ShapeDtypeStruct((rows, across), BF16),
        compiler_params=pltpu.CompilerParams(vmem_limit_bytes=VMEM),
        name="experts",
    )(arrived, gate, up, down)


def spread_kernel(slot_ref, weight_ref, heads, tails):
    tokens, experts = slot_ref.shape
    pick = picker(experts, heads.shape[1], 0)
    place = dot(slot_ref[...].astype(BF16), pick)
    line = iota(place.shape, 1)
    is_head = place == (line & 7).astype(F32)
    is_tail = place == ((line & 3) + 8).astype(F32)
    for index, part in enumerate(halves(weight_ref[...])):
        spread = dot(part, pick)
        here = slice(index * tokens, (index + 1) * tokens)
        heads[here, :] = jnp.where(is_head, spread, 0.0).astype(BF16)
        tails[0, here, :] = jnp.where(is_tail & ((line & 4) == 0), spread, 0.0).astype(BF16)
        tails[1, here, :] = jnp.where(is_tail & ((line & 4) != 0), spread, 0.0).astype(BF16)


def spread_of(slot, weight):
    tokens, experts = slot.shape
    rows = experts * 8
    vmem = pl.BlockSpec(memory_space=pltpu.VMEM)
    return pl.pallas_call(
        spread_kernel,
        in_specs=[vmem] * 2,
        out_specs=[vmem] * 2,
        out_shape=[
            jax.ShapeDtypeStruct((2 * tokens, rows), BF16),
            jax.ShapeDtypeStruct((2, 2 * tokens, rows), BF16),
        ],
        compiler_params=pltpu.CompilerParams(vmem_limit_bytes=VMEM),
        name="spread",
    )(slot, weight)


def combine_kernel(mixed_ref, heads, tails, head_ref, tail_ref, out_ref, total, wide):
    step = pl.program_id(0)
    tokens, width = mixed_ref.shape
    requests = tokens // BLOCK
    chunks = width // LANES
    half = width // 2

    @pl.when(step == 0)
    def _():
        total[...] = mixed_ref[...]

    tile, thin = head_ref.shape[1], tail_ref.shape[1]
    lanes = pl.ds(pl.multiple_of(step * tile, tile), tile)
    both = dot(heads[...], head_ref[...])
    total[:, lanes] += both[:tokens] + both[tokens:]
    for side in range(2):
        lanes = pl.ds(pl.multiple_of(side * half + step * thin, thin), thin)
        both = dot(tails[side], tail_ref[...])
        total[:, lanes] += both[:tokens] + both[tokens:]

    @pl.when(step == pl.num_programs(0) - 1)
    def _():
        for chunk in range(chunks):
            for r in range(requests):
                rows_here = pl.ds(chunk * requests + r, BLOCK, stride=chunks * requests)
                wide[rows_here, :] = total[
                    r * BLOCK : (r + 1) * BLOCK, chunk * LANES : (chunk + 1) * LANES
                ]
        out_ref[...] = wide[...].astype(BF16)


def combine(mixed, heads, tails, back):
    tokens, width = mixed.shape
    rows, across = back.shape
    tile, thin = 256, 128
    steps = width // tile

    def whole(member):
        return pl.BlockSpec(member.shape, lambda step: (0,) * member.ndim)

    lines = tokens * width // LANES
    return pl.pallas_call(
        combine_kernel,
        grid=(steps,),
        in_specs=[
            whole(mixed),
            whole(heads),
            whole(tails),
            pl.BlockSpec((rows, tile), lambda step: (0, step)),
            pl.BlockSpec((rows, thin), lambda step: (0, width // thin + step)),
        ],
        out_specs=pl.BlockSpec((lines, LANES), lambda step: (0, 0)),
        scratch_shapes=[
            pltpu.VMEM((tokens, width), F32),
            pltpu.VMEM((lines, LANES), F32),
        ],
        out_shape=jax.ShapeDtypeStruct((lines, LANES), BF16),
        compiler_params=pltpu.CompilerParams(vmem_limit_bytes=VMEM),
        name="combine",
    )(mixed, heads, tails, back, back)


def decode(relaid, dec_query, dec_key, dec_value, dec_decay, dec_beta):
    query = dec_query.astype(F32)
    key = dec_key.astype(F32)
    key = key * lax.rsqrt(jnp.sum(key * key, axis=-1, keepdims=True) + EPSILON)
    value = dec_value.astype(F32)
    state = relaid.astype(F32)
    outs = []
    for turn in range(dec_query.shape[1]):
        state = jnp.exp(dec_decay[:, turn])[..., None, :] * state
        guessed = jnp.sum(state * key[:, turn, :, None, :], axis=-1)
        update = dec_beta[:, turn, :, None] * (value[:, turn] - guessed)
        state = state + update[..., None] * key[:, turn, :, None, :]
        outs.append(jnp.sum(state * query[:, turn, :, None, :], axis=-1))
    out = jnp.stack(outs, axis=1) * dec_query.shape[-1] ** (-0.5)
    return out, state.transpose(0, 1, 3, 2)


def shards(
    residual, queries, key_in, value_in, log_decay, update_rate, counts, init_state, w_out,
    norm_gain, w_router, expert_ids, w_gate, w_up, w_down,
    dec_query, dec_key, dec_value, dec_decay, dec_beta,
):
    rows_here, requests, width = residual.shape
    heads, key_dim, value_dim = init_state.shape[1:]
    members = lax.axis_size("exp")
    experts = w_router.shape[1]
    groups = lax.axis_size("grp")
    parts, final = delta(
        counts, queries, key_in, value_in, log_decay, update_rate, init_state, w_out, members
    )
    final = lax.ppermute(
        final,
        ("grp", "exp"),
        [(g * members + e, e * members + g) for g in range(groups) for e in range(members)],
    )
    parts = lax.all_to_all(parts, "exp", split_axis=0, concat_axis=0, tiled=True)
    mixed, slot, weight, outgoing = route(residual, parts, norm_gain, w_router, expert_ids)

    def exchange(member):
        member = member.reshape(experts, 8, -1)
        member = lax.all_to_all(
            member, ("exp", "grp", "half"), split_axis=0, concat_axis=0, tiled=True
        )
        return member.reshape(experts * 8, -1)

    arrived = exchange(outgoing)
    heads_of, tails_of = spread_of(slot, weight)
    back = exchange(experts_of(arrived, w_gate[0], w_up[0], w_down[0]))

    relaid = lax.all_to_all(final, "exp", split_axis=0, concat_axis=0, tiled=True)
    relaid = relaid.reshape(groups * requests, heads, value_dim // members, key_dim)
    dec_out, dec_state = decode(relaid, dec_query, dec_key, dec_value, dec_decay, dec_beta)

    hidden = combine(mixed, heads_of, tails_of, back)
    hidden = hidden.reshape(rows_here, width // LANES, requests, LANES).transpose(0, 2, 1, 3)
    return hidden.reshape(rows_here, requests, width), dec_out, dec_state


def solution(mesh):
    return jax.shard_map(
        shards,
        mesh=mesh,
        in_specs=(
            P("exp", ("half", "grp"), None),
            P(None, ("half", "grp"), "exp"),
            P(None, ("half", "grp"), "exp"),
            P(None, ("half", "grp"), "exp"),
            P(None, ("half", "grp"), "exp"),
            P(None, ("half", "grp"), "exp"),
            P(("half", "grp")),
            P(("half", "grp"), "exp", None, None),
            P("exp", None),
            P(),
            P(),
            P("exp", ("half", "grp"), None),
            P(("half", "grp", "exp"), None, None),
            P(("half", "grp", "exp"), None, None),
            P(("half", "grp", "exp"), None, None),
            P("half", None, "grp", None),
            P("half", None, "grp", None),
            P("half", None, "grp", "exp"),
            P("half", None, "grp", None),
            P("half", None, "grp"),
        ),
        out_specs=(
            P("exp", ("half", "grp"), None),
            P("half", None, "grp", "exp"),
            P("half", "grp", None, "exp"),
        ),
        check_vma=False,
    )
```

```python
import functools

import jax
import jax.numpy as jnp
from jax import lax
from jax.experimental import pallas as pl
from jax.experimental.pallas import tpu as pltpu
from jax.sharding import PartitionSpec as P

EPSILON = 1e-06
ROUTE_SCALE = 2.446
LANES = 128
BLOCK = 64
SUBS = 4
VMEM = 60 << 20
F32 = jnp.float32
BF16 = jnp.bfloat16

NN = (((1,), (0,)), ((), ()))
NT = (((1,), (1,)), ((), ()))
TN = (((0,), (0,)), ((), ()))


def dot(left, right, dims=NN):
    return lax.dot_general(left, right, dims, preferred_element_type=F32)


def halves(member):
    high = member.astype(BF16)
    return high, (member - high.astype(F32)).astype(BF16)


def dot3(left, right, dims=NN):
    return (
        dot(left[0], right[0], dims) + dot(left[0], right[1], dims) + dot(left[1], right[0], dims)
    )


def iota(shape, dim):
    return lax.broadcasted_iota(jnp.int32, shape, dim)


def delta_kernel(
    counts, q_ref, k_ref, v_ref, d_ref, rate_ref, init_ref, w_ref,
    part_ref, final_ref,
    state, rate_col, q_all, k_all, v_all, att,
):
    step = pl.program_id(0)
    chains, key_dim, _ = init_ref.shape
    requests = chains // (w_ref.shape[0] // LANES)
    heads = chains // requests
    every = range(chains)

    @pl.when(step == 0)
    def _():
        for chain in every:
            state[chain] = init_ref[chain].T
        for request in range(requests):
            rate_col[:, request * heads : (request + 1) * heads] = rate_ref[request].T

    q_all[...] = q_ref[...].astype(F32)
    k_all[...] = k_ref[...].astype(F32)
    v_all[...] = v_ref[...].astype(F32)

    row = iota((BLOCK, BLOCK), 0)
    col = iota((BLOCK, BLOCK), 1)
    lower = jnp.where(row >= col, 1.0, 0.0).astype(BF16)
    identity = jnp.where(row == col, 1.0, 0.0)
    units = [(sub, c) for sub in range(SUBS) for c in every]
    rows, rate, live = [], [], []
    for sub, c in units:
        rows.append(
            pl.ds(
                sub * BLOCK * chains + (c % heads) * requests + c // heads, BLOCK, stride=chains
            )
        )
        first = pl.multiple_of((step * SUBS + sub) * BLOCK, BLOCK)
        live.append(first + iota((BLOCK, 1), 0) < counts[c // heads])
        rate.append(jnp.where(live[-1], rate_col[pl.ds(first, BLOCK), c : c + 1], 0.0))
    count = range(len(units))

    withins = []
    for u in count:
        decay = jnp.where(live[u], d_ref[rows[u], :], 0.0)
        high, rest = decay.astype(BF16), decay - decay.astype(BF16).astype(F32)
        middle, low = halves(rest)
        withins.append(dot(lower, high) + dot(lower, middle) + dot(lower, low))
    key_up, key_end, query_up, fades, systems, reaches = [], [], [], [], [], []
    for u in count:
        key = k_all[rows[u], :]
        key = key * lax.rsqrt(jnp.sum(key * key, axis=-1, keepdims=True) + EPSILON)
        grow = jnp.exp(withins[u])
        fade = grow[BLOCK - 1 :, :]
        down = key * jnp.exp(-withins[u])
        up_hi, up_lo = halves(key * grow)
        down_hi, down_lo = halves(down)
        query = (q_all[rows[u], :] * grow).astype(BF16)
        both = dot(jnp.concatenate([up_hi, query], axis=0), down_hi, NT)
        pair = both[:BLOCK] + dot(up_hi, down_lo, NT) + dot(up_lo, down_hi, NT)
        reaches.append(jnp.where(row >= col, both[BLOCK:], 0.0).astype(BF16))
        systems.append(jnp.where(row > col, rate[u] * pair, 0.0))
        key_up.append(key * grow)
        key_end.append(halves(down * fade))
        query_up.append(query)
        fades.append(fade)
    near = row >> 1 == col >> 1
    inverse = [identity - jnp.where(near, member, 0.0) for member in systems]
    for bit in range(1, BLOCK.bit_length() - 1):
        joins = (row >> (bit + 1) == col >> (bit + 1)) & (row >> bit != col >> bit)
        rough = [member.astype(BF16) for member in inverse]
        inner = [
            dot(jnp.where(joins, systems[u], 0.0).astype(BF16), rough[u]).astype(BF16)
            for u in count
        ]
        inverse = [inverse[u] - dot(rough[u], inner[u]) for u in count]
    split = [halves(member) for member in inverse]
    missing = [
        (identity - inverse[u] - dot3(halves(systems[u]), split[u])).astype(BF16) for u in count
    ]
    inverse = [inverse[u] + dot(split[u][0], missing[u]) for u in count]
    split = [halves(member) for member in inverse]
    base_v = [dot3(split[u], halves(rate[u] * v_all[rows[u], :])) for u in count]
    base_k = [halves(dot3(split[u], halves(rate[u] * key_up[u]))) for u in count]
    for sub in range(SUBS):
        here = [sub * chains + c for c in every]
        boths, updates = [], []
        for c, u in enumerate(here):
            carry = halves(state[c])
            both = dot(jnp.concatenate([base_k[u][0], query_up[u]], axis=0), carry[0], NT)
            reached = (
                both[:BLOCK] + dot(base_k[u][0], carry[1], NT) + dot(base_k[u][1], carry[0], NT)
            )
            updates.append(halves(base_v[u] - reached))
            boths.append(both[BLOCK:])
        for c, u in enumerate(here):
            state[c] = fades[u] * state[c] + dot3(updates[c], key_end[u], TN)
        for c, u in enumerate(here):
            request, head = divmod(c, heads)
            out = (boths[c] + dot(reaches[u], updates[c][0])) * key_dim ** (-0.5)
            att[
                (sub * requests + request) * BLOCK : (sub * requests + request + 1) * BLOCK,
                head * LANES : (head + 1) * LANES,
            ] = out.astype(BF16)

    width = w_ref.shape[1]
    for lane in range(0, width, 768):
        done = dot(att[...], w_ref[:, lane : lane + 768]).astype(BF16)
        for sub in range(SUBS):
            part_ref[sub, :, lane : lane + 768] = done[
                sub * requests * BLOCK : (sub + 1) * requests * BLOCK
            ]

    @pl.when(step == pl.num_programs(0) - 1)
    def _():
        columns = final_ref.shape[1] // chains
        for c in every:
            for member in range(final_ref.shape[0]):
                final_ref[member, c * columns : (c + 1) * columns, :] = state[
                    c, member * columns : (member + 1) * columns, :
                ].astype(BF16)


def delta(counts, queries, key_in, value_in, log_decay, update_rate, init_state, w_out, members):
    length, requests, features = queries.shape
    heads, key_dim, value_dim = init_state.shape[1:]
    chains = requests * heads
    width = w_out.shape[1]

    def rows_of(member):
        member = member.reshape(length, requests, heads, key_dim)
        return member.transpose(0, 2, 1, 3).reshape(length * chains, key_dim)

    def whole(*shape):
        return pl.BlockSpec(shape, lambda n, *_: (0,) * len(shape))

    tall = SUBS * BLOCK * chains
    block = pl.BlockSpec((tall, key_dim), lambda n, *_: (n, 0))
    blocks = length // BLOCK
    steps = blocks // SUBS
    return pl.pallas_call(
        delta_kernel,
        grid_spec=pltpu.PrefetchScalarGridSpec(
            num_scalar_prefetch=1,
            grid=(steps,),
            in_specs=[block] * 4
            + [
                whole(requests, heads, length),
                whole(chains, key_dim, value_dim),
                whole(features, width),
            ],
            out_specs=[
                pl.BlockSpec((SUBS, requests * BLOCK, width), lambda n, *_: (n, 0, 0)),
                whole(members, chains * value_dim // members, key_dim),
            ],
            scratch_shapes=[
                pltpu.VMEM((chains, value_dim, key_dim), F32),
                pltpu.VMEM((length, chains), F32),
                pltpu.VMEM((tall, key_dim), F32),
                pltpu.VMEM((tall, key_dim), F32),
                pltpu.VMEM((tall, value_dim), F32),
                pltpu.VMEM((SUBS * requests * BLOCK, features), BF16),
            ],
        ),
        out_shape=[
            jax.ShapeDtypeStruct((blocks, requests * BLOCK, width), BF16),
            jax.ShapeDtypeStruct((members, chains * value_dim // members, key_dim), BF16),
        ],
        compiler_params=pltpu.CompilerParams(vmem_limit_bytes=VMEM),
        name="delta",
    )(
        counts,
        rows_of(queries),
        rows_of(key_in),
        rows_of(value_in),
        rows_of(log_decay),
        update_rate.transpose(1, 2, 0),
        init_state.reshape(chains, key_dim, value_dim),
        w_out,
    )


def place_of(expert):
    return ((expert & 7) << 4) + (((expert >> 3) & 7) << 1) + (expert >> 6)


def picker(experts, rows, dim):
    shape = (experts, rows) if dim == 0 else (rows, experts)
    first = place_of(iota(shape, dim)) * 8
    row = iota(shape, 1 - dim)
    return jnp.where((row >= first) & (row < first + 8), 1.0, 0.0).astype(BF16)


def route_kernel(
    res_ref, part_ref, gain_ref, router_ref, ids_ref,
    mixed_ref, slot_ref, weight_ref, out_ref,
    wide, normed,
):
    members, tokens, width = part_ref.shape
    requests = tokens // BLOCK
    chunks = width // LANES
    experts = router_ref.shape[1]
    wide[...] = res_ref[...].astype(F32)
    squares = jnp.zeros((tokens, LANES), F32)
    for chunk in range(chunks):
        lanes = slice(chunk * LANES, (chunk + 1) * LANES)
        total = jnp.concatenate(
            [
                wide[pl.ds(chunk * requests + r, BLOCK, stride=chunks * requests), :]
                for r in range(requests)
            ],
            axis=0,
        )
        for member in range(members):
            total = total + part_ref[member, :, lanes].astype(F32)
        mixed_ref[:, lanes] = total
        squares = squares + total * total
    scale = lax.rsqrt(jnp.sum(squares, axis=-1, keepdims=True) / width + EPSILON)
    for chunk in range(chunks):
        lanes = slice(chunk * LANES, (chunk + 1) * LANES)
        normed[:, lanes] = (mixed_ref[:, lanes] * scale * gain_ref[:, lanes].astype(F32)).astype(
            BF16
        )

    number = iota((experts, tokens), 0)
    chosen = jnp.zeros((experts, tokens), F32)
    for pick in range(ids_ref.shape[0]):
        chosen = chosen + jnp.where(ids_ref[pick : pick + 1, :] == number, 1.0, 0.0)
    row, col = iota((tokens, tokens), 0), iota((tokens, tokens), 1)
    row = (row & (BLOCK - 1)) * requests + (row >> (BLOCK.bit_length() - 1))
    col = (col & (BLOCK - 1)) * requests + (col >> (BLOCK.bit_length() - 1))
    earlier = jnp.where(row < col, 1.0, 0.0).astype(BF16)
    slot = jnp.where(chosen > 0.0, dot(chosen.astype(BF16), earlier), -1.0)
    slot_ref[...] = slot.T

    scores = jax.nn.sigmoid(dot(normed[...], router_ref[...])) * chosen.T
    weight_ref[...] = ROUTE_SCALE * scores / jnp.sum(scores, axis=-1, keepdims=True)

    place = dot(picker(experts, experts * 8, 1), slot.astype(BF16))
    line = iota(place.shape, 0)
    head = jnp.where(place == (line & 7).astype(F32), 1.0, 0.0).astype(BF16)
    tail = place == ((line & 3) + 8).astype(F32)
    tail_a = jnp.where(tail & ((line & 4) == 0), 1.0, 0.0).astype(BF16)
    tail_b = jnp.where(tail & ((line & 4) != 0), 1.0, 0.0).astype(BF16)
    half = width // 2
    step = 6 * LANES
    for lane in range(0, width, step):
        out_ref[:, lane : lane + step] = dot(head, normed[:, lane : lane + step]).astype(BF16)
    step = 3 * LANES
    for lane in range(0, half, step):
        out_ref[:, width + lane : width + lane + step] = (
            dot(tail_a, normed[:, lane : lane + step])
            + dot(tail_b, normed[:, half + lane : half + lane + step])
        ).astype(BF16)


def interleave(member):
    length, requests, width = member.shape
    member = member.reshape(length, requests, width // LANES, LANES).transpose(0, 2, 1, 3)
    return member.reshape(-1, LANES)


def route(residual, parts, norm_gain, w_router, expert_ids):
    length, requests, width = residual.shape
    tokens = length * requests
    experts = w_router.shape[1]
    ids = expert_ids.transpose(2, 1, 0).reshape(-1, tokens)
    vmem = pl.BlockSpec(memory_space=pltpu.VMEM)
    return pl.pallas_call(
        route_kernel,
        in_specs=[vmem] * 5,
        out_specs=[vmem] * 4,
        scratch_shapes=[
            pltpu.VMEM((tokens * width // LANES, LANES), F32),
            pltpu.VMEM((tokens, width), BF16),
        ],
        out_shape=[
            jax.ShapeDtypeStruct((tokens, width), F32),
            jax.ShapeDtypeStruct((tokens, experts), F32),
            jax.ShapeDtypeStruct((tokens, experts), F32),
            jax.ShapeDtypeStruct((experts * 8, width * 3 // 2), BF16),
        ],
        compiler_params=pltpu.CompilerParams(vmem_limit_bytes=VMEM),
        name="route",
    )(interleave(residual), parts, norm_gain.reshape(1, width), w_router, ids)


GROUP = 256


def unpack_rows(dtype=BF16):
    row, col = iota((GROUP, GROUP), 0), iota((GROUP, GROUP), 1)
    half = GROUP // 2
    inside = row & (half - 1)
    source = ((inside >> 2) << 3) + (inside & 3) + jnp.where(row >= half, 4, 0)
    return jnp.where(col == source, 1.0, 0.0).astype(dtype)


def expert_kernel(x_ref, gate_ref, up_ref, down_ref, out_ref, tail_in, tail_out, inner, *, ups):
    step = pl.program_id(0)
    rows, across = x_ref.shape
    width = across * 2 // 3
    half = width // 2
    tails = rows // 2
    fold = gate_ref.shape[1]
    tile = down_ref.shape[1]

    @pl.when(step == 0)
    def _():
        order = unpack_rows()
        for group in range(rows // GROUP):
            moved = dot(order, x_ref[pl.ds(group * GROUP, GROUP), width:]).astype(BF16)
            here = pl.ds(group * GROUP // 2, GROUP // 2)
            tail_in[here, :half] = moved[: GROUP // 2]
            tail_in[here, half:] = moved[GROUP // 2 :]

    @pl.when(step < ups)
    def _():
        lanes = pl.ds(pl.multiple_of(step * fold, fold), fold)
        for start in range(0, rows + tails, 256):
            if start < rows:
                lines = x_ref[start : start + 256, :width]
            else:
                lines = tail_in[start - rows : start - rows + 256, :]
            gate = dot(lines, gate_ref[...])
            up = dot(lines, up_ref[...])
            inner[start : start + 256, lanes] = (gate / (1.0 + jnp.exp(-gate)) * up).astype(BF16)

    @pl.when(step >= ups)
    def _():
        lanes = pl.ds(pl.multiple_of((step - ups) * tile, tile), tile)
        for start in range(0, rows + tails, 256):
            result = dot(inner[start : start + 256, :], down_ref[...]).astype(BF16)
            if start < rows:
                out_ref[start : start + 256, lanes] = result
            else:
                tail_out[start - rows : start - rows + 256, lanes] = result

    @pl.when(step == pl.num_programs(0) - 1)
    def _():
        order = unpack_rows()
        for group in range(rows // GROUP):
            here = pl.ds(group * GROUP // 2, GROUP // 2)
            moved = jnp.concatenate([tail_out[here, :half], tail_out[here, half:]], axis=0)
            out_ref[pl.ds(group * GROUP, GROUP), width:] = dot(order, moved, TN).astype(BF16)


def experts_of(arrived, gate, up, down):
    rows, across = arrived.shape
    width, hidden = gate.shape
    fold, tile = 256, 768
    ups, downs = hidden // fold, width // tile
    tails = rows // 2

    def column(step):
        return (0, jnp.minimum(step, ups - 1))

    def later(step):
        return (0, jnp.maximum(step - ups, 0))

    whole = pl.BlockSpec((rows, across), lambda step: (0, 0))
    return pl.pallas_call(
        functools.partial(expert_kernel, ups=ups),
        grid=(ups + downs,),
        in_specs=[
            whole,
            pl.BlockSpec((width, fold), column),
            pl.BlockSpec((width, fold), column),
            pl.BlockSpec((hidden, tile), later),
        ],
        out_specs=whole,
        scratch_shapes=[
            pltpu.VMEM((tails, width), BF16),
            pltpu.VMEM((tails, width), BF16),
            pltpu.VMEM((rows + tails, hidden), BF16),
        ],
        out_shape=jax.ShapeDtypeStruct((rows, across), BF16),
        compiler_params=pltpu.CompilerParams(vmem_limit_bytes=VMEM),
        name="experts",
    )(arrived, gate, up, down)


def spread_kernel(slot_ref, weight_ref, heads, tails):
    tokens, experts = slot_ref.shape
    pick = picker(experts, heads.shape[1], 0)
    place = dot(slot_ref[...].astype(BF16), pick)
    line = iota(place.shape, 1)
    is_head = place == (line & 7).astype(F32)
    is_tail = place == ((line & 3) + 8).astype(F32)
    for index, part in enumerate(halves(weight_ref[...])):
        spread = dot(part, pick)
        here = slice(index * tokens, (index + 1) * tokens)
        there = slice((index + 2) * tokens, (index + 3) * tokens)
        heads[here, :] = jnp.where(is_head, spread, 0.0).astype(BF16)
        tails[here, :] = jnp.where(is_tail & ((line & 4) == 0), spread, 0.0).astype(BF16)
        tails[there, :] = jnp.where(is_tail & ((line & 4) != 0), spread, 0.0).astype(BF16)


def spread_of(slot, weight):
    tokens, experts = slot.shape
    rows = experts * 8
    vmem = pl.BlockSpec(memory_space=pltpu.VMEM)
    return pl.pallas_call(
        spread_kernel,
        in_specs=[vmem] * 2,
        out_specs=[vmem] * 2,
        out_shape=[
            jax.ShapeDtypeStruct((2 * tokens, rows), BF16),
            jax.ShapeDtypeStruct((4 * tokens, rows), BF16),
        ],
        compiler_params=pltpu.CompilerParams(vmem_limit_bytes=VMEM),
        name="spread",
    )(slot, weight)


def combine_kernel(mixed_ref, heads, tails, head_ref, tail_ref, out_ref, total, wide):
    step = pl.program_id(0)
    tokens, width = mixed_ref.shape
    requests = tokens // BLOCK
    chunks = width // LANES
    half = width // 2

    @pl.when(step == 0)
    def _():
        total[...] = mixed_ref[...]

    tile, thin = head_ref.shape[1], tail_ref.shape[1]
    lanes = pl.ds(pl.multiple_of(step * tile, tile), tile)
    both = dot(heads[...], head_ref[...])
    total[:, lanes] += both[:tokens] + both[tokens:]
    both = dot(tails[...], tail_ref[...])
    for side in range(2):
        lanes = pl.ds(pl.multiple_of(side * half + step * thin, thin), thin)
        first = 2 * side * tokens
        total[:, lanes] += both[first : first + tokens] + both[first + tokens : first + 2 * tokens]

    @pl.when(step == pl.num_programs(0) - 1)
    def _():
        for chunk in range(chunks):
            for r in range(requests):
                rows_here = pl.ds(chunk * requests + r, BLOCK, stride=chunks * requests)
                wide[rows_here, :] = total[
                    r * BLOCK : (r + 1) * BLOCK, chunk * LANES : (chunk + 1) * LANES
                ]
        out_ref[...] = wide[...].astype(BF16)


def combine(mixed, heads, tails, back):
    tokens, width = mixed.shape
    rows, across = back.shape
    tile, thin = 768, 384
    steps = width // tile

    def whole(member):
        return pl.BlockSpec(member.shape, lambda step: (0,) * member.ndim)

    lines = tokens * width // LANES
    return pl.pallas_call(
        combine_kernel,
        grid=(steps,),
        in_specs=[
            whole(mixed),
            whole(heads),
            whole(tails),
            pl.BlockSpec((rows, tile), lambda step: (0, step)),
            pl.BlockSpec((rows, thin), lambda step: (0, width // thin + step)),
        ],
        out_specs=pl.BlockSpec((lines, LANES), lambda step: (0, 0)),
        scratch_shapes=[
            pltpu.VMEM((tokens, width), F32),
            pltpu.VMEM((lines, LANES), F32),
        ],
        out_shape=jax.ShapeDtypeStruct((lines, LANES), BF16),
        compiler_params=pltpu.CompilerParams(vmem_limit_bytes=VMEM),
        name="combine",
    )(mixed, heads, tails, back, back)


def hand_out(member, axis):
    size = lax.axis_size(axis)
    here = lax.axis_index(axis)
    ahead = lax.dynamic_slice_in_dim(jnp.concatenate([member, member]), here, size)
    got = [ahead[0]]
    for shift in range(1, size):
        ring = [(i, (i + shift) % size) for i in range(size)]
        got.append(lax.ppermute(ahead[shift], axis, ring))
    return lax.dynamic_slice_in_dim(jnp.stack((got[::-1]) * 2), size - 1 - here, size)


def decode(relaid, dec_query, dec_key, dec_value, dec_decay, dec_beta):
    query = dec_query.astype(F32)
    key = dec_key.astype(F32)
    key = key * lax.rsqrt(jnp.sum(key * key, axis=-1, keepdims=True) + EPSILON)
    value = dec_value.astype(F32)
    state = relaid.astype(F32)
    outs = []
    for turn in range(dec_query.shape[1]):
        state = jnp.exp(dec_decay[:, turn])[..., None, :] * state
        guessed = jnp.sum(state * key[:, turn, :, None, :], axis=-1)
        update = dec_beta[:, turn, :, None] * (value[:, turn] - guessed)
        state = state + update[..., None] * key[:, turn, :, None, :]
        outs.append(jnp.sum(state * query[:, turn, :, None, :], axis=-1))
    out = jnp.stack(outs, axis=1) * dec_query.shape[-1] ** (-0.5)
    return out, state.transpose(0, 1, 3, 2)


def shards(
    residual, queries, key_in, value_in, log_decay, update_rate, counts, init_state, w_out,
    norm_gain, w_router, expert_ids, w_gate, w_up, w_down,
    dec_query, dec_key, dec_value, dec_decay, dec_beta,
):
    rows_here, requests, width = residual.shape
    heads, key_dim, value_dim = init_state.shape[1:]
    members = lax.axis_size("exp")
    experts = w_router.shape[1]
    groups = lax.axis_size("grp")
    parts, final = delta(
        counts, queries, key_in, value_in, log_decay, update_rate, init_state, w_out, members
    )
    final = lax.ppermute(
        final,
        ("grp", "exp"),
        [(g * members + e, e * members + g) for g in range(groups) for e in range(members)],
    )
    parts = lax.all_to_all(parts, "exp", split_axis=0, concat_axis=0, tiled=True)
    mixed, slot, weight, outgoing = route(residual, parts, norm_gain, w_router, expert_ids)

    def exchange(member):
        member = member.reshape(experts, 8, -1)
        member = lax.all_to_all(
            member, ("exp", "grp", "half"), split_axis=0, concat_axis=0, tiled=True
        )
        return member.reshape(experts * 8, -1)

    arrived = exchange(outgoing)
    heads_of, tails_of = spread_of(slot, weight)
    back = exchange(experts_of(arrived, w_gate[0], w_up[0], w_down[0]))

    relaid = hand_out(final, "exp")
    relaid = relaid.reshape(groups * requests, heads, value_dim // members, key_dim)
    dec_out, dec_state = decode(relaid, dec_query, dec_key, dec_value, dec_decay, dec_beta)

    hidden = combine(mixed, heads_of, tails_of, back)
    hidden = hidden.reshape(rows_here, width // LANES, requests, LANES).transpose(0, 2, 1, 3)
    return hidden.reshape(rows_here, requests, width), dec_out, dec_state


def solution(mesh):
    return jax.shard_map(
        shards,
        mesh=mesh,
        in_specs=(
            P("exp", ("half", "grp"), None),
            P(None, ("half", "grp"), "exp"),
            P(None, ("half", "grp"), "exp"),
            P(None, ("half", "grp"), "exp"),
            P(None, ("half", "grp"), "exp"),
            P(None, ("half", "grp"), "exp"),
            P(("half", "grp")),
            P(("half", "grp"), "exp", None, None),
            P("exp", None),
            P(),
            P(),
            P("exp", ("half", "grp"), None),
            P(("half", "grp", "exp"), None, None),
            P(("half", "grp", "exp"), None, None),
            P(("half", "grp", "exp"), None, None),
            P("half", None, "grp", None),
            P("half", None, "grp", None),
            P("half", None, "grp", "exp"),
            P("half", None, "grp", None),
            P("half", None, "grp"),
        ),
        out_specs=(
            P("exp", ("half", "grp"), None),
            P("half", None, "grp", "exp"),
            P("half", "grp", None, "exp"),
        ),
        check_vma=False,
    )
```

```python
import functools

import jax
import jax.numpy as jnp
from jax import lax
from jax.experimental import pallas as pl
from jax.experimental.pallas import tpu as pltpu
from jax.sharding import PartitionSpec as P

EPSILON = 1e-06
ROUTE_SCALE = 2.446
LANES = 128
BLOCK = 64
SUBS = 4
VMEM = 60 << 20
F32 = jnp.float32
BF16 = jnp.bfloat16

NN = (((1,), (0,)), ((), ()))
NT = (((1,), (1,)), ((), ()))
TN = (((0,), (0,)), ((), ()))


def dot(left, right, dims=NN):
    return lax.dot_general(left, right, dims, preferred_element_type=F32)


def halves(member):
    high = member.astype(BF16)
    return high, (member - high.astype(F32)).astype(BF16)


def dot3(left, right, dims=NN):
    return (
        dot(left[0], right[0], dims) + dot(left[0], right[1], dims) + dot(left[1], right[0], dims)
    )


def iota(shape, dim):
    return lax.broadcasted_iota(jnp.int32, shape, dim)


def delta_kernel(
    counts, q_ref, k_ref, v_ref, d_ref, rate_ref, init_ref, w_ref,
    part_ref, final_ref,
    state, rate_col, q_all, k_all, v_all, att,
):
    step = pl.program_id(0)
    chains, key_dim, _ = init_ref.shape
    requests = chains // (w_ref.shape[0] // LANES)
    heads = chains // requests
    every = range(chains)

    @pl.when(step == 0)
    def _():
        for chain in every:
            state[chain] = init_ref[chain].T
        for request in range(requests):
            rate_col[:, request * heads : (request + 1) * heads] = rate_ref[request].T

    q_all[...] = q_ref[...].astype(F32)
    k_all[...] = k_ref[...].astype(F32)
    v_all[...] = v_ref[...].astype(F32)

    row = iota((BLOCK, BLOCK), 0)
    col = iota((BLOCK, BLOCK), 1)
    lower = jnp.where(row >= col, 1.0, 0.0).astype(BF16)
    identity = jnp.where(row == col, 1.0, 0.0)
    units = [(sub, c) for sub in range(SUBS) for c in every]
    rows, rate, live = [], [], []
    for sub, c in units:
        rows.append(
            pl.ds(
                sub * BLOCK * chains + (c % heads) * requests + c // heads, BLOCK, stride=chains
            )
        )
        first = pl.multiple_of((step * SUBS + sub) * BLOCK, BLOCK)
        live.append(first + iota((BLOCK, 1), 0) < counts[c // heads])
        rate.append(jnp.where(live[-1], rate_col[pl.ds(first, BLOCK), c : c + 1], 0.0))
    count = range(len(units))

    withins = []
    for u in count:
        decay = jnp.where(live[u], d_ref[rows[u], :], 0.0)
        high, rest = decay.astype(BF16), decay - decay.astype(BF16).astype(F32)
        middle, low = halves(rest)
        withins.append(dot(lower, high) + dot(lower, middle) + dot(lower, low))
    key_up, key_end, query_up, fades, systems, reaches = [], [], [], [], [], []
    for u in count:
        key = k_all[rows[u], :]
        key = key * lax.rsqrt(jnp.sum(key * key, axis=-1, keepdims=True) + EPSILON)
        grow = jnp.exp(withins[u])
        fade = grow[BLOCK - 1 :, :]
        down = key * jnp.exp(-withins[u])
        up_hi, up_lo = halves(key * grow)
        down_hi, down_lo = halves(down)
        query = (q_all[rows[u], :] * grow).astype(BF16)
        both = dot(jnp.concatenate([up_hi, query], axis=0), down_hi, NT)
        pair = both[:BLOCK] + dot(up_hi, down_lo, NT) + dot(up_lo, down_hi, NT)
        reaches.append(jnp.where(row >= col, both[BLOCK:], 0.0).astype(BF16))
        systems.append(jnp.where(row > col, rate[u] * pair, 0.0))
        key_up.append(key * grow)
        key_end.append(halves(down * fade))
        query_up.append(query)
        fades.append(fade)
    near = row >> 1 == col >> 1
    inverse = [identity - jnp.where(near, member, 0.0) for member in systems]
    for bit in range(1, BLOCK.bit_length() - 1):
        joins = (row >> (bit + 1) == col >> (bit + 1)) & (row >> bit != col >> bit)
        rough = [member.astype(BF16) for member in inverse]
        inner = [
            dot(jnp.where(joins, systems[u], 0.0).astype(BF16), rough[u]).astype(BF16)
            for u in count
        ]
        inverse = [inverse[u] - dot(rough[u], inner[u]) for u in count]
    split = [halves(member) for member in inverse]
    missing = [
        (identity - inverse[u] - dot3(halves(systems[u]), split[u])).astype(BF16) for u in count
    ]
    inverse = [inverse[u] + dot(split[u][0], missing[u]) for u in count]
    split = [halves(member) for member in inverse]
    base_v = [dot3(split[u], halves(rate[u] * v_all[rows[u], :])) for u in count]
    base_k = [halves(dot3(split[u], halves(rate[u] * key_up[u]))) for u in count]
    for sub in range(SUBS):
        here = [sub * chains + c for c in every]
        boths, updates = [], []
        for c, u in enumerate(here):
            carry = halves(state[c])
            both = dot(jnp.concatenate([base_k[u][0], query_up[u]], axis=0), carry[0], NT)
            reached = (
                both[:BLOCK] + dot(base_k[u][0], carry[1], NT) + dot(base_k[u][1], carry[0], NT)
            )
            updates.append(halves(base_v[u] - reached))
            boths.append(both[BLOCK:])
        for c, u in enumerate(here):
            state[c] = fades[u] * state[c] + dot3(updates[c], key_end[u], TN)
        for c, u in enumerate(here):
            request, head = divmod(c, heads)
            out = (boths[c] + dot(reaches[u], updates[c][0])) * key_dim ** (-0.5)
            att[
                (sub * requests + request) * BLOCK : (sub * requests + request + 1) * BLOCK,
                head * LANES : (head + 1) * LANES,
            ] = out.astype(BF16)

    width = w_ref.shape[1]
    for lane in range(0, width, 768):
        done = dot(att[...], w_ref[:, lane : lane + 768]).astype(BF16)
        for sub in range(SUBS):
            part_ref[sub, :, lane : lane + 768] = done[
                sub * requests * BLOCK : (sub + 1) * requests * BLOCK
            ]

    @pl.when(step == pl.num_programs(0) - 1)
    def _():
        columns = final_ref.shape[1] // chains
        for c in every:
            for member in range(final_ref.shape[0]):
                final_ref[member, c * columns : (c + 1) * columns, :] = state[
                    c, member * columns : (member + 1) * columns, :
                ].astype(BF16)


def delta(counts, queries, key_in, value_in, log_decay, update_rate, init_state, w_out, members):
    length, requests, features = queries.shape
    heads, key_dim, value_dim = init_state.shape[1:]
    chains = requests * heads
    width = w_out.shape[1]

    def rows_of(member):
        member = member.reshape(length, requests, heads, key_dim)
        return member.transpose(0, 2, 1, 3).reshape(length * chains, key_dim)

    def whole(*shape):
        return pl.BlockSpec(shape, lambda n, *_: (0,) * len(shape))

    tall = SUBS * BLOCK * chains
    block = pl.BlockSpec((tall, key_dim), lambda n, *_: (n, 0))
    blocks = length // BLOCK
    steps = blocks // SUBS
    return pl.pallas_call(
        delta_kernel,
        grid_spec=pltpu.PrefetchScalarGridSpec(
            num_scalar_prefetch=1,
            grid=(steps,),
            in_specs=[block] * 4
            + [
                whole(requests, heads, length),
                whole(chains, key_dim, value_dim),
                whole(features, width),
            ],
            out_specs=[
                pl.BlockSpec((SUBS, requests * BLOCK, width), lambda n, *_: (n, 0, 0)),
                whole(members, chains * value_dim // members, key_dim),
            ],
            scratch_shapes=[
                pltpu.VMEM((chains, value_dim, key_dim), F32),
                pltpu.VMEM((length, chains), F32),
                pltpu.VMEM((tall, key_dim), F32),
                pltpu.VMEM((tall, key_dim), F32),
                pltpu.VMEM((tall, value_dim), F32),
                pltpu.VMEM((SUBS * requests * BLOCK, features), BF16),
            ],
        ),
        out_shape=[
            jax.ShapeDtypeStruct((blocks, requests * BLOCK, width), BF16),
            jax.ShapeDtypeStruct((members, chains * value_dim // members, key_dim), BF16),
        ],
        compiler_params=pltpu.CompilerParams(vmem_limit_bytes=VMEM),
        name="delta",
    )(
        counts,
        rows_of(queries),
        rows_of(key_in),
        rows_of(value_in),
        rows_of(log_decay),
        update_rate.transpose(1, 2, 0),
        init_state.reshape(chains, key_dim, value_dim),
        w_out,
    )


def place_of(expert):
    return ((expert & 7) << 4) + (((expert >> 3) & 7) << 1) + (expert >> 6)


def picker(experts, rows, dim):
    shape = (experts, rows) if dim == 0 else (rows, experts)
    first = place_of(iota(shape, dim)) * 8
    row = iota(shape, 1 - dim)
    return jnp.where((row >= first) & (row < first + 8), 1.0, 0.0).astype(BF16)


def route_kernel(
    res_ref, part_ref, gain_ref, router_ref, ids_ref,
    mixed_ref, slot_ref, weight_ref, head_ref, tail_ref,
    wide, normed, head_buf, tail_buf, sems,
):
    members, tokens, width = part_ref.shape
    requests = tokens // BLOCK
    chunks = width // LANES
    experts = router_ref.shape[1]
    wide[...] = res_ref[...].astype(F32)
    squares = jnp.zeros((tokens, LANES), F32)
    for chunk in range(chunks):
        lanes = slice(chunk * LANES, (chunk + 1) * LANES)
        total = jnp.concatenate(
            [
                wide[pl.ds(chunk * requests + r, BLOCK, stride=chunks * requests), :]
                for r in range(requests)
            ],
            axis=0,
        )
        for member in range(members):
            total = total + part_ref[member, :, lanes].astype(F32)
        mixed_ref[:, lanes] = total
        squares = squares + total * total
    scale = lax.rsqrt(jnp.sum(squares, axis=-1, keepdims=True) / width + EPSILON)
    for chunk in range(chunks):
        lanes = slice(chunk * LANES, (chunk + 1) * LANES)
        normed[:, lanes] = (mixed_ref[:, lanes] * scale * gain_ref[:, lanes].astype(F32)).astype(
            BF16
        )

    number = iota((experts, tokens), 0)
    chosen = jnp.zeros((experts, tokens), F32)
    for pick in range(ids_ref.shape[0]):
        chosen = chosen + jnp.where(ids_ref[pick : pick + 1, :] == number, 1.0, 0.0)
    row, col = iota((tokens, tokens), 0), iota((tokens, tokens), 1)
    row = (row & (BLOCK - 1)) * requests + (row >> (BLOCK.bit_length() - 1))
    col = (col & (BLOCK - 1)) * requests + (col >> (BLOCK.bit_length() - 1))
    earlier = jnp.where(row < col, 1.0, 0.0).astype(BF16)
    slot = jnp.where(chosen > 0.0, dot(chosen.astype(BF16), earlier), -1.0)
    slot_ref[...] = slot.T

    scores = jax.nn.sigmoid(dot(normed[...], router_ref[...])) * chosen.T
    weight_ref[...] = ROUTE_SCALE * scores / jnp.sum(scores, axis=-1, keepdims=True)

    place = dot(picker(experts, experts * 8, 1), slot.astype(BF16))
    line = iota(place.shape, 0)
    head = jnp.where(place == (line & 7).astype(F32), 1.0, 0.0).astype(BF16)
    tail = place == ((line & 3) + 8).astype(F32)
    tail_a = jnp.where(tail & ((line & 4) == 0), 1.0, 0.0).astype(BF16)
    tail_b = jnp.where(tail & ((line & 4) != 0), 1.0, 0.0).astype(BF16)
    half = width // 2
    copies = []

    def send(buf, ref, lane, step):
        lanes = pl.ds(lane, step)
        copies.append(
            pltpu.make_async_copy(buf.at[:, lanes], ref.at[:, lanes], sems.at[len(copies)])
        )
        copies[-1].start()

    step = 6 * LANES
    for lane in range(0, width, step):
        head_buf[:, lane : lane + step] = dot(head, normed[:, lane : lane + step]).astype(BF16)
        send(head_buf, head_ref, lane, step)
    step = 3 * LANES
    for lane in range(0, half, step):
        tail_buf[:, lane : lane + step] = (
            dot(tail_a, normed[:, lane : lane + step])
            + dot(tail_b, normed[:, half + lane : half + lane + step])
        ).astype(BF16)
        send(tail_buf, tail_ref, lane, step)
    for copy in copies:
        copy.wait()


def interleave(member):
    length, requests, width = member.shape
    member = member.reshape(length, requests, width // LANES, LANES).transpose(0, 2, 1, 3)
    return member.reshape(-1, LANES)


def route(residual, parts, norm_gain, w_router, expert_ids):
    length, requests, width = residual.shape
    tokens = length * requests
    experts = w_router.shape[1]
    ids = expert_ids.transpose(2, 1, 0).reshape(-1, tokens)
    vmem = pl.BlockSpec(memory_space=pltpu.VMEM)
    return pl.pallas_call(
        route_kernel,
        in_specs=[vmem] * 5,
        out_specs=[vmem] * 3 + [pl.BlockSpec(memory_space=pl.ANY)] * 2,
        scratch_shapes=[
            pltpu.VMEM((tokens * width // LANES, LANES), F32),
            pltpu.VMEM((tokens, width), BF16),
            pltpu.VMEM((experts * 8, width), BF16),
            pltpu.VMEM((experts * 8, width // 2), BF16),
            pltpu.SemaphoreType.DMA((6,)),
        ],
        out_shape=[
            jax.ShapeDtypeStruct((tokens, width), F32),
            jax.ShapeDtypeStruct((tokens, experts), F32),
            jax.ShapeDtypeStruct((tokens, experts), F32),
            jax.ShapeDtypeStruct((experts * 8, width), BF16),
            jax.ShapeDtypeStruct((experts * 8, width // 2), BF16),
        ],
        compiler_params=pltpu.CompilerParams(vmem_limit_bytes=VMEM),
        name="route",
    )(interleave(residual), parts, norm_gain.reshape(1, width), w_router, ids)


GROUP = 256


def unpack_rows(dtype=BF16):
    row, col = iota((GROUP, GROUP), 0), iota((GROUP, GROUP), 1)
    half = GROUP // 2
    inside = row & (half - 1)
    source = ((inside >> 2) << 3) + (inside & 3) + jnp.where(row >= half, 4, 0)
    return jnp.where(col == source, 1.0, 0.0).astype(dtype)


def act(lines, gate_ref, up_ref):
    gate = dot(lines, gate_ref[...])
    up = dot(lines, up_ref[...])
    return (gate / (1.0 + jnp.exp(-gate)) * up).astype(BF16)


def head_kernel(x_ref, gate_ref, up_ref, down_ref, out_ref, inner, *, ups):
    step = pl.program_id(0)
    rows = x_ref.shape[0]
    fold = gate_ref.shape[1]

    @pl.when(step < ups)
    def _():
        lanes = pl.ds(pl.multiple_of(step * fold, fold), fold)
        for start in range(0, rows, GROUP):
            here = slice(start, start + GROUP)
            inner[here, lanes] = act(x_ref[here, :], gate_ref, up_ref)

    @pl.when(step >= ups)
    def _():
        for start in range(0, rows, GROUP):
            here = slice(start, start + GROUP)
            out_ref[here, :] = dot(inner[here, :], down_ref[...]).astype(BF16)


def tail_kernel(
    x_ref, gate_ref, up_ref, down_ref, done_ref, out_ref, lines_in, lines_out, inner, *, ups
):
    step = pl.program_id(0)
    rows, half = x_ref.shape
    fold = gate_ref.shape[1]
    tile = down_ref.shape[1]
    tails = rows // 2

    @pl.when(step == 0)
    def _():
        order = unpack_rows()
        for group in range(rows // GROUP):
            moved = dot(order, x_ref[pl.ds(group * GROUP, GROUP), :]).astype(BF16)
            here = pl.ds(group * GROUP // 2, GROUP // 2)
            lines_in[here, :half] = moved[: GROUP // 2]
            lines_in[here, half:] = moved[GROUP // 2 :]

    @pl.when(step < ups)
    def _():
        lanes = pl.ds(pl.multiple_of(step * fold, fold), fold)
        for start in range(0, tails, GROUP):
            here = slice(start, start + GROUP)
            inner[here, lanes] = act(lines_in[here, :], gate_ref, up_ref)

    @pl.when(step >= ups)
    def _():
        lanes = pl.ds(pl.multiple_of((step - ups) * tile, tile), tile)
        for start in range(0, tails, GROUP):
            here = slice(start, start + GROUP)
            lines_out[here, lanes] = dot(inner[here, :], down_ref[...]).astype(BF16)

    @pl.when(step == pl.num_programs(0) - 1)
    def _():
        order = unpack_rows()
        for group in range(rows // GROUP):
            here = pl.ds(group * GROUP // 2, GROUP // 2)
            moved = jnp.concatenate([lines_out[here, :half], lines_out[here, half:]], axis=0)
            out_ref[pl.ds(group * GROUP, GROUP), :] = dot(order, moved, TN).astype(BF16)


def experts_of(arrived, gate, up, down, done=None):
    rows = arrived.shape[0]
    width, hidden = gate.shape
    fold, tile = 256, 768
    ups, downs = hidden // fold, width // tile
    tails = rows // 2

    def column(step):
        return (0, jnp.minimum(step, ups - 1))

    def later(step):
        return (0, jnp.maximum(step - ups, 0))

    in_specs = [
        pl.BlockSpec(arrived.shape, lambda step: (0, 0)),
        pl.BlockSpec((width, fold), column),
        pl.BlockSpec((width, fold), column),
        pl.BlockSpec((hidden, tile), later),
    ]
    common = dict(
        grid=(ups + downs,),
        out_shape=jax.ShapeDtypeStruct((rows, width * 3 // 2), BF16),
        compiler_params=pltpu.CompilerParams(vmem_limit_bytes=VMEM),
    )
    if done is None:
        return pl.pallas_call(
            functools.partial(head_kernel, ups=ups),
            in_specs=in_specs,
            out_specs=pl.BlockSpec((rows, tile), later),
            scratch_shapes=[pltpu.VMEM((rows, hidden), BF16)],
            name="experts_head",
            **common,
        )(arrived, gate, up, down)
    return pl.pallas_call(
        functools.partial(tail_kernel, ups=ups),
        in_specs=in_specs + [pl.BlockSpec(memory_space=pl.ANY)],
        out_specs=pl.BlockSpec((rows, width // 2), lambda step: (0, 2)),
        scratch_shapes=[
            pltpu.VMEM((tails, width), BF16),
            pltpu.VMEM((tails, width), BF16),
            pltpu.VMEM((tails, hidden), BF16),
        ],
        input_output_aliases={4: 0},
        name="experts_tail",
        **common,
    )(arrived, gate, up, down, done)


def spread_kernel(slot_ref, weight_ref, heads, tails):
    tokens, experts = slot_ref.shape
    pick = picker(experts, heads.shape[1], 0)
    place = dot(slot_ref[...].astype(BF16), pick)
    line = iota(place.shape, 1)
    is_head = place == (line & 7).astype(F32)
    is_tail = place == ((line & 3) + 8).astype(F32)
    for index, part in enumerate(halves(weight_ref[...])):
        spread = dot(part, pick)
        here = slice(index * tokens, (index + 1) * tokens)
        there = slice((index + 2) * tokens, (index + 3) * tokens)
        heads[here, :] = jnp.where(is_head, spread, 0.0).astype(BF16)
        tails[here, :] = jnp.where(is_tail & ((line & 4) == 0), spread, 0.0).astype(BF16)
        tails[there, :] = jnp.where(is_tail & ((line & 4) != 0), spread, 0.0).astype(BF16)


def spread_of(slot, weight):
    tokens, experts = slot.shape
    rows = experts * 8
    vmem = pl.BlockSpec(memory_space=pltpu.VMEM)
    return pl.pallas_call(
        spread_kernel,
        in_specs=[vmem] * 2,
        out_specs=[vmem] * 2,
        out_shape=[
            jax.ShapeDtypeStruct((2 * tokens, rows), BF16),
            jax.ShapeDtypeStruct((4 * tokens, rows), BF16),
        ],
        compiler_params=pltpu.CompilerParams(vmem_limit_bytes=VMEM),
        name="spread",
    )(slot, weight)


def combine_kernel(mixed_ref, heads, tails, head_ref, tail_ref, out_ref, total, wide):
    step = pl.program_id(0)
    tokens, width = mixed_ref.shape
    requests = tokens // BLOCK
    chunks = width // LANES
    half = width // 2

    @pl.when(step == 0)
    def _():
        total[...] = mixed_ref[...]

    tile, thin = head_ref.shape[1], tail_ref.shape[1]
    lanes = pl.ds(pl.multiple_of(step * tile, tile), tile)
    both = dot(heads[...], head_ref[...])
    total[:, lanes] += both[:tokens] + both[tokens:]
    both = dot(tails[...], tail_ref[...])
    for side in range(2):
        lanes = pl.ds(pl.multiple_of(side * half + step * thin, thin), thin)
        first = 2 * side * tokens
        total[:, lanes] += both[first : first + tokens] + both[first + tokens : first + 2 * tokens]

    @pl.when(step == pl.num_programs(0) - 1)
    def _():
        for chunk in range(chunks):
            for r in range(requests):
                rows_here = pl.ds(chunk * requests + r, BLOCK, stride=chunks * requests)
                wide[rows_here, :] = total[
                    r * BLOCK : (r + 1) * BLOCK, chunk * LANES : (chunk + 1) * LANES
                ]
        out_ref[...] = wide[...].astype(BF16)


def combine(mixed, heads, tails, back):
    tokens, width = mixed.shape
    rows, across = back.shape
    tile, thin = 768, 384
    steps = width // tile

    def whole(member):
        return pl.BlockSpec(member.shape, lambda step: (0,) * member.ndim)

    lines = tokens * width // LANES
    return pl.pallas_call(
        combine_kernel,
        grid=(steps,),
        in_specs=[
            whole(mixed),
            whole(heads),
            whole(tails),
            pl.BlockSpec((rows, tile), lambda step: (0, step)),
            pl.BlockSpec((rows, thin), lambda step: (0, width // thin + step)),
        ],
        out_specs=pl.BlockSpec((lines, LANES), lambda step: (0, 0)),
        scratch_shapes=[
            pltpu.VMEM((tokens, width), F32),
            pltpu.VMEM((lines, LANES), F32),
        ],
        out_shape=jax.ShapeDtypeStruct((lines, LANES), BF16),
        compiler_params=pltpu.CompilerParams(vmem_limit_bytes=VMEM),
        name="combine",
    )(mixed, heads, tails, back, back)


def decode(relaid, dec_query, dec_key, dec_value, dec_decay, dec_beta):
    query = dec_query.astype(F32)
    key = dec_key.astype(F32)
    key = key * lax.rsqrt(jnp.sum(key * key, axis=-1, keepdims=True) + EPSILON)
    value = dec_value.astype(F32)
    state = relaid.astype(F32)
    outs = []
    for turn in range(dec_query.shape[1]):
        state = jnp.exp(dec_decay[:, turn])[..., None, :] * state
        guessed = jnp.sum(state * key[:, turn, :, None, :], axis=-1)
        update = dec_beta[:, turn, :, None] * (value[:, turn] - guessed)
        state = state + update[..., None] * key[:, turn, :, None, :]
        outs.append(jnp.sum(state * query[:, turn, :, None, :], axis=-1))
    out = jnp.stack(outs, axis=1) * dec_query.shape[-1] ** (-0.5)
    return out, state.transpose(0, 1, 3, 2)


def shards(
    residual, queries, key_in, value_in, log_decay, update_rate, counts, init_state, w_out,
    norm_gain, w_router, expert_ids, w_gate, w_up, w_down,
    dec_query, dec_key, dec_value, dec_decay, dec_beta,
):
    rows_here, requests, width = residual.shape
    heads, key_dim, value_dim = init_state.shape[1:]
    members = lax.axis_size("exp")
    experts = w_router.shape[1]
    groups = lax.axis_size("grp")
    parts, final = delta(
        counts, queries, key_in, value_in, log_decay, update_rate, init_state, w_out, members
    )
    final = lax.ppermute(
        final,
        ("grp", "exp"),
        [(g * members + e, e * members + g) for g in range(groups) for e in range(members)],
    )
    parts = lax.all_to_all(parts, "exp", split_axis=0, concat_axis=0, tiled=True)
    mixed, slot, weight, head, tail = route(residual, parts, norm_gain, w_router, expert_ids)

    def exchange(member):
        member = member.reshape(experts, 8, -1)
        member = lax.all_to_all(
            member, ("exp", "grp", "half"), split_axis=0, concat_axis=0, tiled=True
        )
        return member.reshape(experts * 8, -1)

    head = exchange(head)
    head, tail = lax.optimization_barrier((head, tail))
    tail = exchange(tail)
    heads_of, tails_of = spread_of(slot, weight)
    matrices = (w_gate[0], w_up[0], w_down[0])
    back = exchange(experts_of(tail, *matrices, done=experts_of(head, *matrices)))

    relaid = lax.all_to_all(final, "exp", split_axis=0, concat_axis=0, tiled=True)
    relaid = relaid.reshape(groups * requests, heads, value_dim // members, key_dim)
    dec_out, dec_state = decode(relaid, dec_query, dec_key, dec_value, dec_decay, dec_beta)

    hidden = combine(mixed, heads_of, tails_of, back)
    hidden = hidden.reshape(rows_here, width // LANES, requests, LANES).transpose(0, 2, 1, 3)
    return hidden.reshape(rows_here, requests, width), dec_out, dec_state


def solution(mesh):
    return jax.shard_map(
        shards,
        mesh=mesh,
        in_specs=(
            P("exp", ("half", "grp"), None),
            P(None, ("half", "grp"), "exp"),
            P(None, ("half", "grp"), "exp"),
            P(None, ("half", "grp"), "exp"),
            P(None, ("half", "grp"), "exp"),
            P(None, ("half", "grp"), "exp"),
            P(("half", "grp")),
            P(("half", "grp"), "exp", None, None),
            P("exp", None),
            P(),
            P(),
            P("exp", ("half", "grp"), None),
            P(("half", "grp", "exp"), None, None),
            P(("half", "grp", "exp"), None, None),
            P(("half", "grp", "exp"), None, None),
            P("half", None, "grp", None),
            P("half", None, "grp", None),
            P("half", None, "grp", "exp"),
            P("half", None, "grp", None),
            P("half", None, "grp"),
        ),
        out_specs=(
            P("exp", ("half", "grp"), None),
            P("half", None, "grp", "exp"),
            P("half", "grp", None, "exp"),
        ),
        check_vma=False,
    )
```

```python
import functools

import jax
import jax.numpy as jnp
from jax import lax
from jax.experimental import pallas as pl
from jax.experimental.pallas import tpu as pltpu
from jax.sharding import PartitionSpec as P

EPSILON = 1e-06
ROUTE_SCALE = 2.446
LANES = 128
BLOCK = 64
SUBS = 4
VMEM = 60 << 20
F32 = jnp.float32
BF16 = jnp.bfloat16

NN = (((1,), (0,)), ((), ()))
NT = (((1,), (1,)), ((), ()))
TN = (((0,), (0,)), ((), ()))


def dot(left, right, dims=NN):
    return lax.dot_general(left, right, dims, preferred_element_type=F32)


def halves(member):
    high = member.astype(BF16)
    return high, (member - high.astype(F32)).astype(BF16)


def dot3(left, right, dims=NN):
    return (
        dot(left[0], right[0], dims) + dot(left[0], right[1], dims) + dot(left[1], right[0], dims)
    )


def iota(shape, dim):
    return lax.broadcasted_iota(jnp.int32, shape, dim)


def delta_kernel(
    counts, q_ref, k_ref, v_ref, d_ref, rate_ref, init_ref, w_ref,
    part_ref, final_ref,
    state, rate_col, q_all, k_all, v_all, att,
):
    step = pl.program_id(0)
    chains, key_dim, _ = init_ref.shape
    requests = chains // (w_ref.shape[0] // LANES)
    heads = chains // requests
    every = range(chains)

    @pl.when(step == 0)
    def _():
        for chain in every:
            state[chain] = init_ref[chain].T
        for request in range(requests):
            rate_col[:, request * heads : (request + 1) * heads] = rate_ref[request].T

    q_all[...] = q_ref[...].astype(F32)
    k_all[...] = k_ref[...].astype(F32)
    v_all[...] = v_ref[...].astype(F32)

    row = iota((BLOCK, BLOCK), 0)
    col = iota((BLOCK, BLOCK), 1)
    lower = jnp.where(row >= col, 1.0, 0.0).astype(BF16)
    identity = jnp.where(row == col, 1.0, 0.0)
    units = [(sub, c) for sub in range(SUBS) for c in every]
    rows, rate, live = [], [], []
    for sub, c in units:
        rows.append(
            pl.ds(
                sub * BLOCK * chains + (c % heads) * requests + c // heads, BLOCK, stride=chains
            )
        )
        first = pl.multiple_of((step * SUBS + sub) * BLOCK, BLOCK)
        live.append(first + iota((BLOCK, 1), 0) < counts[c // heads])
        rate.append(jnp.where(live[-1], rate_col[pl.ds(first, BLOCK), c : c + 1], 0.0))
    count = range(len(units))

    withins = []
    for u in count:
        decay = jnp.where(live[u], d_ref[rows[u], :], 0.0)
        high, rest = decay.astype(BF16), decay - decay.astype(BF16).astype(F32)
        middle, low = halves(rest)
        withins.append(dot(lower, high) + dot(lower, middle) + dot(lower, low))
    key_up, key_end, query_up, fades, systems, reaches = [], [], [], [], [], []
    for u in count:
        key = k_all[rows[u], :]
        key = key * lax.rsqrt(jnp.sum(key * key, axis=-1, keepdims=True) + EPSILON)
        grow = jnp.exp(withins[u])
        fade = grow[BLOCK - 1 :, :]
        down = key * jnp.exp(-withins[u])
        up_hi, up_lo = halves(key * grow)
        down_hi, down_lo = halves(down)
        query = (q_all[rows[u], :] * grow).astype(BF16)
        both = dot(jnp.concatenate([up_hi, query], axis=0), down_hi, NT)
        pair = both[:BLOCK] + dot(up_hi, down_lo, NT) + dot(up_lo, down_hi, NT)
        reaches.append(jnp.where(row >= col, both[BLOCK:], 0.0).astype(BF16))
        systems.append(jnp.where(row > col, rate[u] * pair, 0.0))
        key_up.append(key * grow)
        key_end.append(halves(down * fade))
        query_up.append(query)
        fades.append(fade)
    near = row >> 1 == col >> 1
    inverse = [identity - jnp.where(near, member, 0.0) for member in systems]
    for bit in range(1, BLOCK.bit_length() - 1):
        joins = (row >> (bit + 1) == col >> (bit + 1)) & (row >> bit != col >> bit)
        rough = [member.astype(BF16) for member in inverse]
        inner = [
            dot(jnp.where(joins, systems[u], 0.0).astype(BF16), rough[u]).astype(BF16)
            for u in count
        ]
        inverse = [inverse[u] - dot(rough[u], inner[u]) for u in count]
    split = [halves(member) for member in inverse]
    missing = [
        (identity - inverse[u] - dot3(halves(systems[u]), split[u])).astype(BF16) for u in count
    ]
    inverse = [inverse[u] + dot(split[u][0], missing[u]) for u in count]
    split = [halves(member) for member in inverse]
    base_v = [dot3(split[u], halves(rate[u] * v_all[rows[u], :])) for u in count]
    base_k = [halves(dot3(split[u], halves(rate[u] * key_up[u]))) for u in count]
    for sub in range(SUBS):
        here = [sub * chains + c for c in every]
        boths, updates = [], []
        for c, u in enumerate(here):
            carry = halves(state[c])
            both = dot(jnp.concatenate([base_k[u][0], query_up[u]], axis=0), carry[0], NT)
            reached = (
                both[:BLOCK] + dot(base_k[u][0], carry[1], NT) + dot(base_k[u][1], carry[0], NT)
            )
            updates.append(halves(base_v[u] - reached))
            boths.append(both[BLOCK:])
        for c, u in enumerate(here):
            state[c] = fades[u] * state[c] + dot3(updates[c], key_end[u], TN)
        for c, u in enumerate(here):
            request, head = divmod(c, heads)
            out = (boths[c] + dot(reaches[u], updates[c][0])) * key_dim ** (-0.5)
            att[
                (sub * requests + request) * BLOCK : (sub * requests + request + 1) * BLOCK,
                head * LANES : (head + 1) * LANES,
            ] = out.astype(BF16)

    width = w_ref.shape[1]
    for lane in range(0, width, 768):
        done = dot(att[...], w_ref[:, lane : lane + 768]).astype(BF16)
        for sub in range(SUBS):
            part_ref[sub, :, lane : lane + 768] = done[
                sub * requests * BLOCK : (sub + 1) * requests * BLOCK
            ]

    @pl.when(step == pl.num_programs(0) - 1)
    def _():
        columns = final_ref.shape[1] // chains
        for c in every:
            for member in range(final_ref.shape[0]):
                final_ref[member, c * columns : (c + 1) * columns, :] = state[
                    c, member * columns : (member + 1) * columns, :
                ].astype(BF16)


def delta(counts, queries, key_in, value_in, log_decay, update_rate, init_state, w_out, members):
    length, requests, features = queries.shape
    heads, key_dim, value_dim = init_state.shape[1:]
    chains = requests * heads
    width = w_out.shape[1]

    def rows_of(member):
        member = member.reshape(length, requests, heads, key_dim)
        return member.transpose(0, 2, 1, 3).reshape(length * chains, key_dim)

    def whole(*shape):
        return pl.BlockSpec(shape, lambda n, *_: (0,) * len(shape))

    tall = SUBS * BLOCK * chains
    block = pl.BlockSpec((tall, key_dim), lambda n, *_: (n, 0))
    blocks = length // BLOCK
    steps = blocks // SUBS
    return pl.pallas_call(
        delta_kernel,
        grid_spec=pltpu.PrefetchScalarGridSpec(
            num_scalar_prefetch=1,
            grid=(steps,),
            in_specs=[block] * 4
            + [
                whole(requests, heads, length),
                whole(chains, key_dim, value_dim),
                whole(features, width),
            ],
            out_specs=[
                pl.BlockSpec((SUBS, requests * BLOCK, width), lambda n, *_: (n, 0, 0)),
                whole(members, chains * value_dim // members, key_dim),
            ],
            scratch_shapes=[
                pltpu.VMEM((chains, value_dim, key_dim), F32),
                pltpu.VMEM((length, chains), F32),
                pltpu.VMEM((tall, key_dim), F32),
                pltpu.VMEM((tall, key_dim), F32),
                pltpu.VMEM((tall, value_dim), F32),
                pltpu.VMEM((SUBS * requests * BLOCK, features), BF16),
            ],
        ),
        out_shape=[
            jax.ShapeDtypeStruct((blocks, requests * BLOCK, width), BF16),
            jax.ShapeDtypeStruct((members, chains * value_dim // members, key_dim), BF16),
        ],
        compiler_params=pltpu.CompilerParams(vmem_limit_bytes=VMEM),
        cost_estimate=pl.CostEstimate(flops=8 * 10**9, bytes_accessed=16 * 10**6, transcendentals=0),
        name="delta",
    )(
        counts,
        rows_of(queries),
        rows_of(key_in),
        rows_of(value_in),
        rows_of(log_decay),
        update_rate.transpose(1, 2, 0),
        init_state.reshape(chains, key_dim, value_dim),
        w_out,
    )


def place_of(expert):
    return ((expert & 7) << 4) + (((expert >> 3) & 7) << 1) + (expert >> 6)


def picker(experts, rows, dim):
    shape = (experts, rows) if dim == 0 else (rows, experts)
    first = place_of(iota(shape, dim)) * 8
    row = iota(shape, 1 - dim)
    return jnp.where((row >= first) & (row < first + 8), 1.0, 0.0).astype(BF16)


def route_kernel(
    res_ref, part_ref, gain_ref, router_ref, ids_ref,
    mixed_ref, slot_ref, weight_ref, head_ref, tail_ref,
    wide, normed, head_buf, tail_buf, sems,
):
    members, tokens, width = part_ref.shape
    requests = tokens // BLOCK
    chunks = width // LANES
    experts = router_ref.shape[1]
    wide[...] = res_ref[...].astype(F32)
    squares = jnp.zeros((tokens, LANES), F32)
    for chunk in range(chunks):
        lanes = slice(chunk * LANES, (chunk + 1) * LANES)
        total = jnp.concatenate(
            [
                wide[pl.ds(chunk * requests + r, BLOCK, stride=chunks * requests), :]
                for r in range(requests)
            ],
            axis=0,
        )
        for member in range(members):
            total = total + part_ref[member, :, lanes].astype(F32)
        mixed_ref[:, lanes] = total
        squares = squares + total * total
    scale = lax.rsqrt(jnp.sum(squares, axis=-1, keepdims=True) / width + EPSILON)
    for chunk in range(chunks):
        lanes = slice(chunk * LANES, (chunk + 1) * LANES)
        normed[:, lanes] = (mixed_ref[:, lanes] * scale * gain_ref[:, lanes].astype(F32)).astype(
            BF16
        )

    number = iota((experts, tokens), 0)
    chosen = jnp.zeros((experts, tokens), F32)
    for pick in range(ids_ref.shape[0]):
        chosen = chosen + jnp.where(ids_ref[pick : pick + 1, :] == number, 1.0, 0.0)
    row, col = iota((tokens, tokens), 0), iota((tokens, tokens), 1)
    row = (row & (BLOCK - 1)) * requests + (row >> (BLOCK.bit_length() - 1))
    col = (col & (BLOCK - 1)) * requests + (col >> (BLOCK.bit_length() - 1))
    earlier = jnp.where(row < col, 1.0, 0.0).astype(BF16)
    slot = jnp.where(chosen > 0.0, dot(chosen.astype(BF16), earlier), -1.0)
    slot_ref[...] = slot.T

    scores = jax.nn.sigmoid(dot(normed[...], router_ref[...])) * chosen.T
    weight_ref[...] = ROUTE_SCALE * scores / jnp.sum(scores, axis=-1, keepdims=True)

    place = dot(picker(experts, experts * 8, 1), slot.astype(BF16))
    line = iota(place.shape, 0)
    head = jnp.where(place == (line & 7).astype(F32), 1.0, 0.0).astype(BF16)
    tail = place == ((line & 3) + 8).astype(F32)
    tail_a = jnp.where(tail & ((line & 4) == 0), 1.0, 0.0).astype(BF16)
    tail_b = jnp.where(tail & ((line & 4) != 0), 1.0, 0.0).astype(BF16)
    half = width // 2
    copies = []

    def send(buf, ref, lane, step):
        lanes = pl.ds(lane, step)
        copies.append(
            pltpu.make_async_copy(buf.at[:, lanes], ref.at[:, lanes], sems.at[len(copies)])
        )
        copies[-1].start()

    step = 6 * LANES
    for lane in range(0, width, step):
        head_buf[:, lane : lane + step] = dot(head, normed[:, lane : lane + step]).astype(BF16)
        send(head_buf, head_ref, lane, step)
    step = 3 * LANES
    for lane in range(0, half, step):
        tail_buf[:, lane : lane + step] = (
            dot(tail_a, normed[:, lane : lane + step])
            + dot(tail_b, normed[:, half + lane : half + lane + step])
        ).astype(BF16)
        send(tail_buf, tail_ref, lane, step)
    for copy in copies:
        copy.wait()


def interleave(member):
    length, requests, width = member.shape
    member = member.reshape(length, requests, width // LANES, LANES).transpose(0, 2, 1, 3)
    return member.reshape(-1, LANES)


def route(residual, parts, norm_gain, w_router, expert_ids):
    length, requests, width = residual.shape
    tokens = length * requests
    experts = w_router.shape[1]
    ids = expert_ids.transpose(2, 1, 0).reshape(-1, tokens)
    vmem = pl.BlockSpec(memory_space=pltpu.VMEM)
    return pl.pallas_call(
        route_kernel,
        in_specs=[vmem] * 5,
        out_specs=[vmem] * 3 + [pl.BlockSpec(memory_space=pl.ANY)] * 2,
        scratch_shapes=[
            pltpu.VMEM((tokens * width // LANES, LANES), F32),
            pltpu.VMEM((tokens, width), BF16),
            pltpu.VMEM((experts * 8, width), BF16),
            pltpu.VMEM((experts * 8, width // 2), BF16),
            pltpu.SemaphoreType.DMA((6,)),
        ],
        out_shape=[
            jax.ShapeDtypeStruct((tokens, width), F32),
            jax.ShapeDtypeStruct((tokens, experts), F32),
            jax.ShapeDtypeStruct((tokens, experts), F32),
            jax.ShapeDtypeStruct((experts * 8, width), BF16),
            jax.ShapeDtypeStruct((experts * 8, width // 2), BF16),
        ],
        compiler_params=pltpu.CompilerParams(vmem_limit_bytes=VMEM),
        cost_estimate=pl.CostEstimate(flops=2 * 10**9, bytes_accessed=14 * 10**6, transcendentals=0),
        name="route",
    )(interleave(residual), parts, norm_gain.reshape(1, width), w_router, ids)


GROUP = 256


def unpack_rows(dtype=BF16):
    row, col = iota((GROUP, GROUP), 0), iota((GROUP, GROUP), 1)
    half = GROUP // 2
    inside = row & (half - 1)
    source = ((inside >> 2) << 3) + (inside & 3) + jnp.where(row >= half, 4, 0)
    return jnp.where(col == source, 1.0, 0.0).astype(dtype)


def act(lines, gate_ref, up_ref):
    gate = dot(lines, gate_ref[...])
    up = dot(lines, up_ref[...])
    return (gate / (1.0 + jnp.exp(-gate)) * up).astype(BF16)


def head_kernel(x_ref, gate_ref, up_ref, down_ref, out_ref, inner, *, ups):
    step = pl.program_id(0)
    rows = x_ref.shape[0]
    fold = gate_ref.shape[1]

    @pl.when(step < ups)
    def _():
        lanes = pl.ds(pl.multiple_of(step * fold, fold), fold)
        for start in range(0, rows, GROUP):
            here = slice(start, start + GROUP)
            inner[here, lanes] = act(x_ref[here, :], gate_ref, up_ref)

    @pl.when(step >= ups)
    def _():
        for start in range(0, rows, GROUP):
            here = slice(start, start + GROUP)
            out_ref[here, :] = dot(inner[here, :], down_ref[...]).astype(BF16)


def tail_kernel(
    x_ref, gate_ref, up_ref, down_ref, done_ref, out_ref, lines_in, lines_out, inner, *, ups
):
    step = pl.program_id(0)
    rows, half = x_ref.shape
    fold = gate_ref.shape[1]
    tile = down_ref.shape[1]
    tails = rows // 2

    @pl.when(step == 0)
    def _():
        order = unpack_rows()
        for group in range(rows // GROUP):
            moved = dot(order, x_ref[pl.ds(group * GROUP, GROUP), :]).astype(BF16)
            here = pl.ds(group * GROUP // 2, GROUP // 2)
            lines_in[here, :half] = moved[: GROUP // 2]
            lines_in[here, half:] = moved[GROUP // 2 :]

    @pl.when(step < ups)
    def _():
        lanes = pl.ds(pl.multiple_of(step * fold, fold), fold)
        for start in range(0, tails, GROUP):
            here = slice(start, start + GROUP)
            inner[here, lanes] = act(lines_in[here, :], gate_ref, up_ref)

    @pl.when(step >= ups)
    def _():
        lanes = pl.ds(pl.multiple_of((step - ups) * tile, tile), tile)
        for start in range(0, tails, GROUP):
            here = slice(start, start + GROUP)
            lines_out[here, lanes] = dot(inner[here, :], down_ref[...]).astype(BF16)

    @pl.when(step == pl.num_programs(0) - 1)
    def _():
        order = unpack_rows()
        for group in range(rows // GROUP):
            here = pl.ds(group * GROUP // 2, GROUP // 2)
            moved = jnp.concatenate([lines_out[here, :half], lines_out[here, half:]], axis=0)
            out_ref[pl.ds(group * GROUP, GROUP), :] = dot(order, moved, TN).astype(BF16)


def experts_of(arrived, gate, up, down, done=None):
    rows = arrived.shape[0]
    width, hidden = gate.shape
    fold, tile = 256, 768
    ups, downs = hidden // fold, width // tile
    tails = rows // 2

    def column(step):
        return (0, jnp.minimum(step, ups - 1))

    def later(step):
        return (0, jnp.maximum(step - ups, 0))

    in_specs = [
        pl.BlockSpec(arrived.shape, lambda step: (0, 0)),
        pl.BlockSpec((width, fold), column),
        pl.BlockSpec((width, fold), column),
        pl.BlockSpec((hidden, tile), later),
    ]
    common = dict(
        grid=(ups + downs,),
        out_shape=jax.ShapeDtypeStruct((rows, width * 3 // 2), BF16),
        compiler_params=pltpu.CompilerParams(vmem_limit_bytes=VMEM),
    )
    if done is None:
        return pl.pallas_call(
            functools.partial(head_kernel, ups=ups),
            in_specs=in_specs,
            out_specs=pl.BlockSpec((rows, tile), later),
            scratch_shapes=[pltpu.VMEM((rows, hidden), BF16)],
            cost_estimate=pl.CostEstimate(flops=6 * rows * width * hidden, bytes_accessed=4 * rows * width + 6 * width * hidden, transcendentals=0),
            name="experts_head",
            **common,
        )(arrived, gate, up, down)
    return pl.pallas_call(
        functools.partial(tail_kernel, ups=ups),
        in_specs=in_specs + [pl.BlockSpec(memory_space=pl.ANY)],
        out_specs=pl.BlockSpec((rows, width // 2), lambda step: (0, 2)),
        scratch_shapes=[
            pltpu.VMEM((tails, width), BF16),
            pltpu.VMEM((tails, width), BF16),
            pltpu.VMEM((tails, hidden), BF16),
        ],
        input_output_aliases={4: 0},
        cost_estimate=pl.CostEstimate(flops=6 * tails * width * hidden, bytes_accessed=4 * tails * width + 6 * width * hidden, transcendentals=0),
        name="experts_tail",
        **common,
    )(arrived, gate, up, down, done)


def spread_kernel(slot_ref, weight_ref, heads, tails):
    tokens, experts = slot_ref.shape
    pick = picker(experts, heads.shape[1], 0)
    place = dot(slot_ref[...].astype(BF16), pick)
    line = iota(place.shape, 1)
    is_head = place == (line & 7).astype(F32)
    is_tail = place == ((line & 3) + 8).astype(F32)
    for index, part in enumerate(halves(weight_ref[...])):
        spread = dot(part, pick)
        here = slice(index * tokens, (index + 1) * tokens)
        there = slice((index + 2) * tokens, (index + 3) * tokens)
        heads[here, :] = jnp.where(is_head, spread, 0.0).astype(BF16)
        tails[here, :] = jnp.where(is_tail & ((line & 4) == 0), spread, 0.0).astype(BF16)
        tails[there, :] = jnp.where(is_tail & ((line & 4) != 0), spread, 0.0).astype(BF16)


def spread_of(slot, weight):
    tokens, experts = slot.shape
    rows = experts * 8
    vmem = pl.BlockSpec(memory_space=pltpu.VMEM)
    return pl.pallas_call(
        spread_kernel,
        in_specs=[vmem] * 2,
        out_specs=[vmem] * 2,
        out_shape=[
            jax.ShapeDtypeStruct((2 * tokens, rows), BF16),
            jax.ShapeDtypeStruct((4 * tokens, rows), BF16),
        ],
        compiler_params=pltpu.CompilerParams(vmem_limit_bytes=VMEM),
        cost_estimate=pl.CostEstimate(flops=10**9, bytes_accessed=2 * 10**6, transcendentals=0),
        name="spread",
    )(slot, weight)


def combine_kernel(mixed_ref, heads, tails, head_ref, tail_ref, out_ref, total, wide):
    step = pl.program_id(0)
    tokens, width = mixed_ref.shape
    requests = tokens // BLOCK
    chunks = width // LANES
    half = width // 2

    @pl.when(step == 0)
    def _():
        total[...] = mixed_ref[...]

    tile, thin = head_ref.shape[1], tail_ref.shape[1]
    lanes = pl.ds(pl.multiple_of(step * tile, tile), tile)
    both = dot(heads[...], head_ref[...])
    total[:, lanes] += both[:tokens] + both[tokens:]
    both = dot(tails[...], tail_ref[...])
    for side in range(2):
        lanes = pl.ds(pl.multiple_of(side * half + step * thin, thin), thin)
        first = 2 * side * tokens
        total[:, lanes] += both[first : first + tokens] + both[first + tokens : first + 2 * tokens]

    @pl.when(step == pl.num_programs(0) - 1)
    def _():
        for chunk in range(chunks):
            for r in range(requests):
                rows_here = pl.ds(chunk * requests + r, BLOCK, stride=chunks * requests)
                wide[rows_here, :] = total[
                    r * BLOCK : (r + 1) * BLOCK, chunk * LANES : (chunk + 1) * LANES
                ]
        out_ref[...] = wide[...].astype(BF16)


def combine(mixed, heads, tails, back):
    tokens, width = mixed.shape
    rows, across = back.shape
    tile, thin = 768, 384
    steps = width // tile

    def whole(member):
        return pl.BlockSpec(member.shape, lambda step: (0,) * member.ndim)

    lines = tokens * width // LANES
    return pl.pallas_call(
        combine_kernel,
        grid=(steps,),
        in_specs=[
            whole(mixed),
            whole(heads),
            whole(tails),
            pl.BlockSpec((rows, tile), lambda step: (0, step)),
            pl.BlockSpec((rows, thin), lambda step: (0, width // thin + step)),
        ],
        out_specs=pl.BlockSpec((lines, LANES), lambda step: (0, 0)),
        scratch_shapes=[
            pltpu.VMEM((tokens, width), F32),
            pltpu.VMEM((lines, LANES), F32),
        ],
        out_shape=jax.ShapeDtypeStruct((lines, LANES), BF16),
        compiler_params=pltpu.CompilerParams(vmem_limit_bytes=VMEM),
        cost_estimate=pl.CostEstimate(flops=4 * 10**9, bytes_accessed=11 * 10**6, transcendentals=0),
        name="combine",
    )(mixed, heads, tails, back, back)


def decode(relaid, dec_query, dec_key, dec_value, dec_decay, dec_beta):
    query = dec_query.astype(F32)
    key = dec_key.astype(F32)
    key = key * lax.rsqrt(jnp.sum(key * key, axis=-1, keepdims=True) + EPSILON)
    value = dec_value.astype(F32)
    state = relaid.astype(F32)
    outs = []
    for turn in range(dec_query.shape[1]):
        state = jnp.exp(dec_decay[:, turn])[..., None, :] * state
        guessed = jnp.sum(state * key[:, turn, :, None, :], axis=-1)
        update = dec_beta[:, turn, :, None] * (value[:, turn] - guessed)
        state = state + update[..., None] * key[:, turn, :, None, :]
        outs.append(jnp.sum(state * query[:, turn, :, None, :], axis=-1))
    out = jnp.stack(outs, axis=1) * dec_query.shape[-1] ** (-0.5)
    return out, state.transpose(0, 1, 3, 2)


def shards(
    residual, queries, key_in, value_in, log_decay, update_rate, counts, init_state, w_out,
    norm_gain, w_router, expert_ids, w_gate, w_up, w_down,
    dec_query, dec_key, dec_value, dec_decay, dec_beta,
):
    rows_here, requests, width = residual.shape
    heads, key_dim, value_dim = init_state.shape[1:]
    members = lax.axis_size("exp")
    experts = w_router.shape[1]
    groups = lax.axis_size("grp")
    parts, final = delta(
        counts, queries, key_in, value_in, log_decay, update_rate, init_state, w_out, members
    )
    final = lax.ppermute(
        final,
        ("grp", "exp"),
        [(g * members + e, e * members + g) for g in range(groups) for e in range(members)],
    )
    parts = lax.all_to_all(parts, "exp", split_axis=0, concat_axis=0, tiled=True)
    mixed, slot, weight, head, tail = route(residual, parts, norm_gain, w_router, expert_ids)

    def exchange(member):
        member = member.reshape(experts, 8, -1)
        member = lax.all_to_all(
            member, ("exp", "grp", "half"), split_axis=0, concat_axis=0, tiled=True
        )
        return member.reshape(experts * 8, -1)

    head = exchange(head)
    head, tail = lax.optimization_barrier((head, tail))
    tail = exchange(tail)
    heads_of, tails_of = spread_of(slot, weight)
    matrices = (w_gate[0], w_up[0], w_down[0])
    back = exchange(experts_of(tail, *matrices, done=experts_of(head, *matrices)))

    relaid = lax.all_to_all(final, "exp", split_axis=0, concat_axis=0, tiled=True)
    relaid = relaid.reshape(groups * requests, heads, value_dim // members, key_dim)
    dec_out, dec_state = decode(relaid, dec_query, dec_key, dec_value, dec_decay, dec_beta)

    hidden = combine(mixed, heads_of, tails_of, back)
    hidden = hidden.reshape(rows_here, width // LANES, requests, LANES).transpose(0, 2, 1, 3)
    return hidden.reshape(rows_here, requests, width), dec_out, dec_state


def solution(mesh):
    return jax.shard_map(
        shards,
        mesh=mesh,
        in_specs=(
            P("exp", ("half", "grp"), None),
            P(None, ("half", "grp"), "exp"),
            P(None, ("half", "grp"), "exp"),
            P(None, ("half", "grp"), "exp"),
            P(None, ("half", "grp"), "exp"),
            P(None, ("half", "grp"), "exp"),
            P(("half", "grp")),
            P(("half", "grp"), "exp", None, None),
            P("exp", None),
            P(),
            P(),
            P("exp", ("half", "grp"), None),
            P(("half", "grp", "exp"), None, None),
            P(("half", "grp", "exp"), None, None),
            P(("half", "grp", "exp"), None, None),
            P("half", None, "grp", None),
            P("half", None, "grp", None),
            P("half", None, "grp", "exp"),
            P("half", None, "grp", None),
            P("half", None, "grp"),
        ),
        out_specs=(
            P("exp", ("half", "grp"), None),
            P("half", None, "grp", "exp"),
            P("half", "grp", None, "exp"),
        ),
        check_vma=False,
    )
```

```python
import functools

import jax
import jax.numpy as jnp
from jax import lax
from jax.experimental import pallas as pl
from jax.experimental.pallas import tpu as pltpu
from jax.sharding import PartitionSpec as P

EPSILON = 1e-06
ROUTE_SCALE = 2.446
LANES = 128
BLOCK = 64
SUBS = 4
VMEM = 60 << 20
F32 = jnp.float32
BF16 = jnp.bfloat16

NN = (((1,), (0,)), ((), ()))
NT = (((1,), (1,)), ((), ()))
TN = (((0,), (0,)), ((), ()))


def dot(left, right, dims=NN):
    return lax.dot_general(left, right, dims, preferred_element_type=F32)


def halves(member):
    high = member.astype(BF16)
    return high, (member - high.astype(F32)).astype(BF16)


def dot3(left, right, dims=NN):
    return (
        dot(left[0], right[0], dims) + dot(left[0], right[1], dims) + dot(left[1], right[0], dims)
    )


def iota(shape, dim):
    return lax.broadcasted_iota(jnp.int32, shape, dim)


def delta_kernel(
    counts, q_ref, k_ref, v_ref, d_ref, rate_ref, init_ref, w_ref,
    part_ref, final_ref,
    state, rate_col, q_all, k_all, v_all, att,
):
    step = pl.program_id(0)
    chains, key_dim, _ = init_ref.shape
    requests = chains // (w_ref.shape[0] // LANES)
    heads = chains // requests
    every = range(chains)

    @pl.when(step == 0)
    def _():
        for chain in every:
            state[chain] = init_ref[chain].T
        for request in range(requests):
            rate_col[:, request * heads : (request + 1) * heads] = rate_ref[request].T

    q_all[...] = q_ref[...].astype(F32)
    k_all[...] = k_ref[...].astype(F32)
    v_all[...] = v_ref[...].astype(F32)

    row = iota((BLOCK, BLOCK), 0)
    col = iota((BLOCK, BLOCK), 1)
    lower = jnp.where(row >= col, 1.0, 0.0).astype(BF16)
    identity = jnp.where(row == col, 1.0, 0.0)
    units = [(sub, c) for sub in range(SUBS) for c in every]
    rows, rate, live = [], [], []
    for sub, c in units:
        rows.append(
            pl.ds(
                sub * BLOCK * chains + (c % heads) * requests + c // heads, BLOCK, stride=chains
            )
        )
        first = pl.multiple_of((step * SUBS + sub) * BLOCK, BLOCK)
        live.append(first + iota((BLOCK, 1), 0) < counts[c // heads])
        rate.append(jnp.where(live[-1], rate_col[pl.ds(first, BLOCK), c : c + 1], 0.0))
    count = range(len(units))

    withins = []
    for u in count:
        decay = jnp.where(live[u], d_ref[rows[u], :], 0.0)
        high, rest = decay.astype(BF16), decay - decay.astype(BF16).astype(F32)
        middle, low = halves(rest)
        withins.append(dot(lower, high) + dot(lower, middle) + dot(lower, low))
    key_up, key_end, query_up, fades, systems, reaches = [], [], [], [], [], []
    for u in count:
        key = k_all[rows[u], :]
        key = key * lax.rsqrt(jnp.sum(key * key, axis=-1, keepdims=True) + EPSILON)
        grow = jnp.exp(withins[u])
        fade = grow[BLOCK - 1 :, :]
        down = key * jnp.exp(-withins[u])
        up_hi, up_lo = halves(key * grow)
        down_hi, down_lo = halves(down)
        query = (q_all[rows[u], :] * grow).astype(BF16)
        both = dot(jnp.concatenate([up_hi, query], axis=0), down_hi, NT)
        pair = both[:BLOCK] + dot(up_hi, down_lo, NT) + dot(up_lo, down_hi, NT)
        reaches.append(jnp.where(row >= col, both[BLOCK:], 0.0).astype(BF16))
        systems.append(jnp.where(row > col, rate[u] * pair, 0.0))
        key_up.append(key * grow)
        key_end.append(halves(down * fade))
        query_up.append(query)
        fades.append(fade)
    near = row >> 1 == col >> 1
    inverse = [identity - jnp.where(near, member, 0.0) for member in systems]
    for bit in range(1, BLOCK.bit_length() - 1):
        joins = (row >> (bit + 1) == col >> (bit + 1)) & (row >> bit != col >> bit)
        rough = [member.astype(BF16) for member in inverse]
        inner = [
            dot(jnp.where(joins, systems[u], 0.0).astype(BF16), rough[u]).astype(BF16)
            for u in count
        ]
        inverse = [inverse[u] - dot(rough[u], inner[u]) for u in count]
    split = [halves(member) for member in inverse]
    missing = [
        (identity - inverse[u] - dot3(halves(systems[u]), split[u])).astype(BF16) for u in count
    ]
    inverse = [inverse[u] + dot(split[u][0], missing[u]) for u in count]
    split = [halves(member) for member in inverse]
    base_v = [dot3(split[u], halves(rate[u] * v_all[rows[u], :])) for u in count]
    base_k = [halves(dot3(split[u], halves(rate[u] * key_up[u]))) for u in count]
    for sub in range(SUBS):
        here = [sub * chains + c for c in every]
        boths, updates = [], []
        for c, u in enumerate(here):
            carry = halves(state[c])
            both = dot(jnp.concatenate([base_k[u][0], query_up[u]], axis=0), carry[0], NT)
            reached = (
                both[:BLOCK] + dot(base_k[u][0], carry[1], NT) + dot(base_k[u][1], carry[0], NT)
            )
            updates.append(halves(base_v[u] - reached))
            boths.append(both[BLOCK:])
        for c, u in enumerate(here):
            state[c] = fades[u] * state[c] + dot3(updates[c], key_end[u], TN)
        for c, u in enumerate(here):
            request, head = divmod(c, heads)
            out = (boths[c] + dot(reaches[u], updates[c][0])) * key_dim ** (-0.5)
            att[
                (sub * requests + request) * BLOCK : (sub * requests + request + 1) * BLOCK,
                head * LANES : (head + 1) * LANES,
            ] = out.astype(BF16)

    width = w_ref.shape[1]
    for lane in range(0, width, 768):
        done = dot(att[...], w_ref[:, lane : lane + 768]).astype(BF16)
        for sub in range(SUBS):
            part_ref[sub, :, lane : lane + 768] = done[
                sub * requests * BLOCK : (sub + 1) * requests * BLOCK
            ]

    @pl.when(step == pl.num_programs(0) - 1)
    def _():
        columns = final_ref.shape[1] // chains
        for c in every:
            for member in range(final_ref.shape[0]):
                final_ref[member, c * columns : (c + 1) * columns, :] = state[
                    c, member * columns : (member + 1) * columns, :
                ].astype(BF16)


def delta(counts, queries, key_in, value_in, log_decay, update_rate, init_state, w_out, members):
    length, requests, features = queries.shape
    heads, key_dim, value_dim = init_state.shape[1:]
    chains = requests * heads
    width = w_out.shape[1]

    def rows_of(member):
        member = member.reshape(length, requests, heads, key_dim)
        return member.transpose(0, 2, 1, 3).reshape(length * chains, key_dim)

    def whole(*shape):
        return pl.BlockSpec(shape, lambda n, *_: (0,) * len(shape))

    tall = SUBS * BLOCK * chains
    block = pl.BlockSpec((tall, key_dim), lambda n, *_: (n, 0))
    blocks = length // BLOCK
    steps = blocks // SUBS
    return pl.pallas_call(
        delta_kernel,
        grid_spec=pltpu.PrefetchScalarGridSpec(
            num_scalar_prefetch=1,
            grid=(steps,),
            in_specs=[block] * 4
            + [
                whole(requests, heads, length),
                whole(chains, key_dim, value_dim),
                whole(features, width),
            ],
            out_specs=[
                pl.BlockSpec((SUBS, requests * BLOCK, width), lambda n, *_: (n, 0, 0)),
                whole(members, chains * value_dim // members, key_dim),
            ],
            scratch_shapes=[
                pltpu.VMEM((chains, value_dim, key_dim), F32),
                pltpu.VMEM((length, chains), F32),
                pltpu.VMEM((tall, key_dim), F32),
                pltpu.VMEM((tall, key_dim), F32),
                pltpu.VMEM((tall, value_dim), F32),
                pltpu.VMEM((SUBS * requests * BLOCK, features), BF16),
            ],
        ),
        out_shape=[
            jax.ShapeDtypeStruct((blocks, requests * BLOCK, width), BF16),
            jax.ShapeDtypeStruct((members, chains * value_dim // members, key_dim), BF16),
        ],
        compiler_params=pltpu.CompilerParams(vmem_limit_bytes=VMEM),
        cost_estimate=pl.CostEstimate(flops=8 * 10**9, bytes_accessed=16 * 10**6, transcendentals=0),
        name="delta",
    )(
        counts,
        rows_of(queries),
        rows_of(key_in),
        rows_of(value_in),
        rows_of(log_decay),
        update_rate.transpose(1, 2, 0),
        init_state.reshape(chains, key_dim, value_dim),
        w_out,
    )


def place_of(expert):
    return ((expert & 7) << 4) + (((expert >> 3) & 7) << 1) + (expert >> 6)


def picker(experts, rows, dim):
    shape = (experts, rows) if dim == 0 else (rows, experts)
    first = place_of(iota(shape, dim)) * 8
    row = iota(shape, 1 - dim)
    return jnp.where((row >= first) & (row < first + 8), 1.0, 0.0).astype(BF16)


def route_kernel(
    res_ref, part_ref, gain_ref, router_ref, ids_ref,
    mixed_ref, slot_ref, weight_ref, head_ref, tail_ref,
    wide, normed, head_buf, tail_buf, sems,
):
    members, tokens, width = part_ref.shape
    requests = tokens // BLOCK
    chunks = width // LANES
    experts = router_ref.shape[1]
    wide[...] = res_ref[...].astype(F32)
    squares = jnp.zeros((tokens, LANES), F32)
    for chunk in range(chunks):
        lanes = slice(chunk * LANES, (chunk + 1) * LANES)
        total = jnp.concatenate(
            [
                wide[pl.ds(chunk * requests + r, BLOCK, stride=chunks * requests), :]
                for r in range(requests)
            ],
            axis=0,
        )
        for member in range(members):
            total = total + part_ref[member, :, lanes].astype(F32)
        mixed_ref[:, lanes] = total
        squares = squares + total * total
    scale = lax.rsqrt(jnp.sum(squares, axis=-1, keepdims=True) / width + EPSILON)
    for chunk in range(chunks):
        lanes = slice(chunk * LANES, (chunk + 1) * LANES)
        normed[:, lanes] = (mixed_ref[:, lanes] * scale * gain_ref[:, lanes].astype(F32)).astype(
            BF16
        )

    number = iota((experts, tokens), 0)
    chosen = jnp.zeros((experts, tokens), F32)
    for pick in range(ids_ref.shape[0]):
        chosen = chosen + jnp.where(ids_ref[pick : pick + 1, :] == number, 1.0, 0.0)
    row, col = iota((tokens, tokens), 0), iota((tokens, tokens), 1)
    row = (row & (BLOCK - 1)) * requests + (row >> (BLOCK.bit_length() - 1))
    col = (col & (BLOCK - 1)) * requests + (col >> (BLOCK.bit_length() - 1))
    earlier = jnp.where(row < col, 1.0, 0.0).astype(BF16)
    slot = jnp.where(chosen > 0.0, dot(chosen.astype(BF16), earlier), -1.0)
    slot_ref[...] = slot.T

    scores = jax.nn.sigmoid(dot(normed[...], router_ref[...])) * chosen.T
    weight_ref[...] = ROUTE_SCALE * scores / jnp.sum(scores, axis=-1, keepdims=True)

    place = dot(picker(experts, experts * 8, 1), slot.astype(BF16))
    line = iota(place.shape, 0)
    head = jnp.where(place == (line & 7).astype(F32), 1.0, 0.0).astype(BF16)
    tail = place == ((line & 3) + 8).astype(F32)
    tail_a = jnp.where(tail & ((line & 4) == 0), 1.0, 0.0).astype(BF16)
    tail_b = jnp.where(tail & ((line & 4) != 0), 1.0, 0.0).astype(BF16)
    half = width // 2
    copies = []

    def send(buf, ref, lane, step):
        lanes = pl.ds(lane, step)
        copies.append(
            pltpu.make_async_copy(buf.at[:, lanes], ref.at[:, lanes], sems.at[len(copies)])
        )
        copies[-1].start()

    step = 6 * LANES
    for lane in range(0, width, step):
        head_buf[:, lane : lane + step] = dot(head, normed[:, lane : lane + step]).astype(BF16)
        send(head_buf, head_ref, lane, step)
    step = 3 * LANES
    for lane in range(0, half, step):
        tail_buf[:, lane : lane + step] = (
            dot(tail_a, normed[:, lane : lane + step])
            + dot(tail_b, normed[:, half + lane : half + lane + step])
        ).astype(BF16)
        send(tail_buf, tail_ref, lane, step)
    for copy in copies:
        copy.wait()


def interleave(member):
    length, requests, width = member.shape
    member = member.reshape(length, requests, width // LANES, LANES).transpose(0, 2, 1, 3)
    return member.reshape(-1, LANES)


def route(residual, parts, norm_gain, w_router, expert_ids):
    length, requests, width = residual.shape
    tokens = length * requests
    experts = w_router.shape[1]
    ids = expert_ids.transpose(2, 1, 0).reshape(-1, tokens)
    vmem = pl.BlockSpec(memory_space=pltpu.VMEM)
    return pl.pallas_call(
        route_kernel,
        in_specs=[vmem] * 5,
        out_specs=[vmem] * 3 + [pl.BlockSpec(memory_space=pl.ANY)] * 2,
        scratch_shapes=[
            pltpu.VMEM((tokens * width // LANES, LANES), F32),
            pltpu.VMEM((tokens, width), BF16),
            pltpu.VMEM((experts * 8, width), BF16),
            pltpu.VMEM((experts * 8, width // 2), BF16),
            pltpu.SemaphoreType.DMA((6,)),
        ],
        out_shape=[
            jax.ShapeDtypeStruct((tokens, width), F32),
            jax.ShapeDtypeStruct((tokens, experts), F32),
            jax.ShapeDtypeStruct((tokens, experts), F32),
            jax.ShapeDtypeStruct((experts * 8, width), BF16),
            jax.ShapeDtypeStruct((experts * 8, width // 2), BF16),
        ],
        compiler_params=pltpu.CompilerParams(vmem_limit_bytes=VMEM),
        cost_estimate=pl.CostEstimate(flops=2 * 10**9, bytes_accessed=14 * 10**6, transcendentals=0),
        name="route",
    )(interleave(residual), parts, norm_gain.reshape(1, width), w_router, ids)


GROUP = 256


def unpack_rows(dtype=BF16):
    row, col = iota((GROUP, GROUP), 0), iota((GROUP, GROUP), 1)
    half = GROUP // 2
    inside = row & (half - 1)
    source = ((inside >> 2) << 3) + (inside & 3) + jnp.where(row >= half, 4, 0)
    return jnp.where(col == source, 1.0, 0.0).astype(dtype)


def act(lines, gate_ref, up_ref):
    gate = dot(lines, gate_ref[...])
    up = dot(lines, up_ref[...])
    return (gate / (1.0 + jnp.exp(-gate)) * up).astype(BF16)


def head_kernel(x_ref, gate_ref, up_ref, down_ref, out_ref, inner, *, ups):
    step = pl.program_id(0)
    rows = x_ref.shape[0]
    fold = gate_ref.shape[1]

    @pl.when(step < ups)
    def _():
        lanes = pl.ds(pl.multiple_of(step * fold, fold), fold)
        for start in range(0, rows, GROUP):
            here = slice(start, start + GROUP)
            inner[here, lanes] = act(x_ref[here, :], gate_ref, up_ref)

    @pl.when(step >= ups)
    def _():
        for start in range(0, rows, GROUP):
            here = slice(start, start + GROUP)
            out_ref[here, :] = dot(inner[here, :], down_ref[...]).astype(BF16)


def tail_kernel(
    x_ref, gate_ref, up_ref, down_ref, out_ref, lines_in, lines_out, inner, *, ups
):
    step = pl.program_id(0)
    rows, half = x_ref.shape
    fold = gate_ref.shape[1]
    tile = down_ref.shape[1]
    tails = rows // 2

    @pl.when(step == 0)
    def _():
        order = unpack_rows()
        for group in range(rows // GROUP):
            moved = dot(order, x_ref[pl.ds(group * GROUP, GROUP), :]).astype(BF16)
            here = pl.ds(group * GROUP // 2, GROUP // 2)
            lines_in[here, :half] = moved[: GROUP // 2]
            lines_in[here, half:] = moved[GROUP // 2 :]

    @pl.when(step < ups)
    def _():
        lanes = pl.ds(pl.multiple_of(step * fold, fold), fold)
        for start in range(0, tails, GROUP):
            here = slice(start, start + GROUP)
            inner[here, lanes] = act(lines_in[here, :], gate_ref, up_ref)

    @pl.when(step >= ups)
    def _():
        lanes = pl.ds(pl.multiple_of((step - ups) * tile, tile), tile)
        for start in range(0, tails, GROUP):
            here = slice(start, start + GROUP)
            lines_out[here, lanes] = dot(inner[here, :], down_ref[...]).astype(BF16)

    @pl.when(step == pl.num_programs(0) - 1)
    def _():
        order = unpack_rows()
        for group in range(rows // GROUP):
            here = pl.ds(group * GROUP // 2, GROUP // 2)
            moved = jnp.concatenate([lines_out[here, :half], lines_out[here, half:]], axis=0)
            out_ref[pl.ds(group * GROUP, GROUP), :] = dot(order, moved, TN).astype(BF16)


def experts_of(arrived, gate, up, down):
    rows = arrived.shape[0]
    width, hidden = gate.shape
    fold, tile = 256, 768
    ups, downs = hidden // fold, width // tile
    tails = rows // 2

    def column(step):
        return (0, jnp.minimum(step, ups - 1))

    def later(step):
        return (0, jnp.maximum(step - ups, 0))

    in_specs = [
        pl.BlockSpec(arrived.shape, lambda step: (0, 0)),
        pl.BlockSpec((width, fold), column),
        pl.BlockSpec((width, fold), column),
        pl.BlockSpec((hidden, tile), later),
    ]
    common = dict(
        grid=(ups + downs,),
        out_shape=jax.ShapeDtypeStruct(arrived.shape, BF16),
        compiler_params=pltpu.CompilerParams(vmem_limit_bytes=VMEM),
    )
    if arrived.shape[1] == width:
        return pl.pallas_call(
            functools.partial(head_kernel, ups=ups),
            in_specs=in_specs,
            out_specs=pl.BlockSpec((rows, tile), later),
            scratch_shapes=[pltpu.VMEM((rows, hidden), BF16)],
            cost_estimate=pl.CostEstimate(flops=6 * rows * width * hidden, bytes_accessed=4 * rows * width + 6 * width * hidden, transcendentals=0),
            name="experts_head",
            **common,
        )(arrived, gate, up, down)
    return pl.pallas_call(
        functools.partial(tail_kernel, ups=ups),
        in_specs=in_specs,
        out_specs=pl.BlockSpec(arrived.shape, lambda step: (0, 0)),
        scratch_shapes=[
            pltpu.VMEM((tails, width), BF16),
            pltpu.VMEM((tails, width), BF16),
            pltpu.VMEM((tails, hidden), BF16),
        ],
        cost_estimate=pl.CostEstimate(flops=6 * tails * width * hidden, bytes_accessed=4 * tails * width + 6 * width * hidden, transcendentals=0),
        name="experts_tail",
        **common,
    )(arrived, gate, up, down)


def spread_kernel(slot_ref, weight_ref, heads, tails):
    tokens, experts = slot_ref.shape
    pick = picker(experts, heads.shape[1], 0)
    place = dot(slot_ref[...].astype(BF16), pick)
    line = iota(place.shape, 1)
    is_head = place == (line & 7).astype(F32)
    is_tail = place == ((line & 3) + 8).astype(F32)
    for index, part in enumerate(halves(weight_ref[...])):
        spread = dot(part, pick)
        here = slice(index * tokens, (index + 1) * tokens)
        there = slice((index + 2) * tokens, (index + 3) * tokens)
        heads[here, :] = jnp.where(is_head, spread, 0.0).astype(BF16)
        tails[here, :] = jnp.where(is_tail & ((line & 4) == 0), spread, 0.0).astype(BF16)
        tails[there, :] = jnp.where(is_tail & ((line & 4) != 0), spread, 0.0).astype(BF16)


def spread_of(slot, weight):
    tokens, experts = slot.shape
    rows = experts * 8
    vmem = pl.BlockSpec(memory_space=pltpu.VMEM)
    return pl.pallas_call(
        spread_kernel,
        in_specs=[vmem] * 2,
        out_specs=[vmem] * 2,
        out_shape=[
            jax.ShapeDtypeStruct((2 * tokens, rows), BF16),
            jax.ShapeDtypeStruct((4 * tokens, rows), BF16),
        ],
        compiler_params=pltpu.CompilerParams(vmem_limit_bytes=VMEM),
        cost_estimate=pl.CostEstimate(flops=10**9, bytes_accessed=2 * 10**6, transcendentals=0),
        name="spread",
    )(slot, weight)


def add_kernel(mixed_ref, heads, back_ref, total_ref):
    tokens = mixed_ref.shape[0]
    both = dot(heads[...], back_ref[...])
    total_ref[...] = mixed_ref[...] + both[:tokens] + both[tokens:]


def add_heads(mixed, heads, back):
    tokens, width = mixed.shape
    tile = 768
    column = pl.BlockSpec((tokens, tile), lambda step: (0, step))
    return pl.pallas_call(
        add_kernel,
        grid=(width // tile,),
        in_specs=[
            column,
            pl.BlockSpec(heads.shape, lambda step: (0, 0)),
            pl.BlockSpec((back.shape[0], tile), lambda step: (0, step)),
        ],
        out_specs=column,
        out_shape=jax.ShapeDtypeStruct((tokens, width), F32),
        compiler_params=pltpu.CompilerParams(vmem_limit_bytes=VMEM),
        cost_estimate=pl.CostEstimate(
            flops=3 * 10**9, bytes_accessed=8 * 10**6, transcendentals=0
        ),
        name="add_heads",
    )(mixed, heads, back)


def combine_kernel(total_ref, tails, back_ref, out_ref):
    step = pl.program_id(0)
    tokens, width = total_ref.shape
    requests = tokens // BLOCK
    half = width // 2
    thin = back_ref.shape[1]
    both = dot(tails[...], back_ref[...])
    for side in range(2):
        lanes = pl.ds(pl.multiple_of(side * half + step * thin, thin), thin)
        first = 2 * side * tokens
        done = (
            total_ref[:, lanes]
            + both[first : first + tokens]
            + both[first + tokens : first + 2 * tokens]
        )
        pieces = [done[r * BLOCK : (r + 1) * BLOCK] for r in range(requests)]
        out_ref[:, :, lanes] = jnp.stack(pieces, axis=1).astype(BF16)


def combine(total, tails, back):
    tokens, width = total.shape
    thin = 384

    def whole(*shape):
        return pl.BlockSpec(shape, lambda step: (0,) * len(shape))

    return pl.pallas_call(
        combine_kernel,
        grid=(width // 2 // thin,),
        in_specs=[
            whole(*total.shape),
            whole(*tails.shape),
            pl.BlockSpec((back.shape[0], thin), lambda step: (0, step)),
        ],
        out_specs=whole(BLOCK, tokens // BLOCK, width),
        out_shape=jax.ShapeDtypeStruct((BLOCK, tokens // BLOCK, width), BF16),
        compiler_params=pltpu.CompilerParams(vmem_limit_bytes=VMEM),
        cost_estimate=pl.CostEstimate(
            flops=2 * 10**9, bytes_accessed=6 * 10**6, transcendentals=0
        ),
        name="combine",
    )(total, tails, back)


def decode(relaid, dec_query, dec_key, dec_value, dec_decay, dec_beta):
    query = dec_query.astype(F32)
    key = dec_key.astype(F32)
    key = key * lax.rsqrt(jnp.sum(key * key, axis=-1, keepdims=True) + EPSILON)
    value = dec_value.astype(F32)
    state = relaid.astype(F32)
    outs = []
    for turn in range(dec_query.shape[1]):
        state = jnp.exp(dec_decay[:, turn])[..., None, :] * state
        guessed = jnp.sum(state * key[:, turn, :, None, :], axis=-1)
        update = dec_beta[:, turn, :, None] * (value[:, turn] - guessed)
        state = state + update[..., None] * key[:, turn, :, None, :]
        outs.append(jnp.sum(state * query[:, turn, :, None, :], axis=-1))
    out = jnp.stack(outs, axis=1) * dec_query.shape[-1] ** (-0.5)
    return out, state.transpose(0, 1, 3, 2)


def shards(
    residual, queries, key_in, value_in, log_decay, update_rate, counts, init_state, w_out,
    norm_gain, w_router, expert_ids, w_gate, w_up, w_down,
    dec_query, dec_key, dec_value, dec_decay, dec_beta,
):
    requests = residual.shape[1]
    heads, key_dim, value_dim = init_state.shape[1:]
    members = lax.axis_size("exp")
    experts = w_router.shape[1]
    groups = lax.axis_size("grp")
    parts, final = delta(
        counts, queries, key_in, value_in, log_decay, update_rate, init_state, w_out, members
    )
    final = lax.ppermute(
        final,
        ("grp", "exp"),
        [(g * members + e, e * members + g) for g in range(groups) for e in range(members)],
    )
    parts = lax.all_to_all(parts, "exp", split_axis=0, concat_axis=0, tiled=True)
    mixed, slot, weight, head, tail = route(residual, parts, norm_gain, w_router, expert_ids)

    def exchange(member):
        member = member.reshape(experts, 8, -1)
        member = lax.all_to_all(
            member, ("exp", "grp", "half"), split_axis=0, concat_axis=0, tiled=True
        )
        return member.reshape(experts * 8, -1)

    head = exchange(head)
    head, tail = lax.optimization_barrier((head, tail))
    tail = exchange(tail)
    heads_of, tails_of = spread_of(slot, weight)
    matrices = (w_gate[0], w_up[0], w_down[0])
    head, tail, final = lax.optimization_barrier((experts_of(head, *matrices), tail, final))
    relaid = lax.all_to_all(final, "exp", split_axis=0, concat_axis=0, tiled=True)
    head, relaid = lax.optimization_barrier((head, relaid))
    head = exchange(head)
    head, tail = lax.optimization_barrier((head, experts_of(tail, *matrices)))
    tail = exchange(tail)
    relaid = relaid.reshape(groups * requests, heads, value_dim // members, key_dim)
    dec_out, dec_state = decode(relaid, dec_query, dec_key, dec_value, dec_decay, dec_beta)

    hidden = combine(add_heads(mixed, heads_of, head), tails_of, tail)
    return hidden, dec_out, dec_state


def solution(mesh):
    return jax.shard_map(
        shards,
        mesh=mesh,
        in_specs=(
            P("exp", ("half", "grp"), None),
            P(None, ("half", "grp"), "exp"),
            P(None, ("half", "grp"), "exp"),
            P(None, ("half", "grp"), "exp"),
            P(None, ("half", "grp"), "exp"),
            P(None, ("half", "grp"), "exp"),
            P(("half", "grp")),
            P(("half", "grp"), "exp", None, None),
            P("exp", None),
            P(),
            P(),
            P("exp", ("half", "grp"), None),
            P(("half", "grp", "exp"), None, None),
            P(("half", "grp", "exp"), None, None),
            P(("half", "grp", "exp"), None, None),
            P("half", None, "grp", None),
            P("half", None, "grp", None),
            P("half", None, "grp", "exp"),
            P("half", None, "grp", None),
            P("half", None, "grp"),
        ),
        out_specs=(
            P("exp", ("half", "grp"), None),
            P("half", None, "grp", "exp"),
            P("half", "grp", None, "exp"),
        ),
        check_vma=False,
    )
```

```python
import functools

import jax
import jax.numpy as jnp
from jax import lax
from jax.experimental import pallas as pl
from jax.experimental.pallas import tpu as pltpu
from jax.sharding import PartitionSpec as P

EPSILON = 1e-06
ROUTE_SCALE = 2.446
LANES = 128
BLOCK = 64
SUBS = 4
VMEM = 60 << 20
F32 = jnp.float32
BF16 = jnp.bfloat16

NN = (((1,), (0,)), ((), ()))
NT = (((1,), (1,)), ((), ()))
TN = (((0,), (0,)), ((), ()))


def dot(left, right, dims=NN):
    return lax.dot_general(left, right, dims, preferred_element_type=F32)


def halves(member):
    high = member.astype(BF16)
    return high, (member - high.astype(F32)).astype(BF16)


def dot3(left, right, dims=NN):
    return (
        dot(left[0], right[0], dims) + dot(left[0], right[1], dims) + dot(left[1], right[0], dims)
    )


def iota(shape, dim):
    return lax.broadcasted_iota(jnp.int32, shape, dim)


def delta_kernel(
    counts, q_ref, k_ref, v_ref, d_ref, rate_ref, init_ref, w_ref,
    part_ref, final_ref,
    state, rate_col, q_all, k_all, v_all, att,
):
    step = pl.program_id(0)
    chains, key_dim, _ = init_ref.shape
    requests = chains // (w_ref.shape[0] // LANES)
    heads = chains // requests
    every = range(chains)

    @pl.when(step == 0)
    def _():
        for chain in every:
            state[chain] = init_ref[chain].T
        for request in range(requests):
            rate_col[:, request * heads : (request + 1) * heads] = rate_ref[request].T

    q_all[...] = q_ref[...].astype(F32)
    k_all[...] = k_ref[...].astype(F32)
    v_all[...] = v_ref[...].astype(F32)

    row = iota((BLOCK, BLOCK), 0)
    col = iota((BLOCK, BLOCK), 1)
    lower = jnp.where(row >= col, 1.0, 0.0).astype(BF16)
    identity = jnp.where(row == col, 1.0, 0.0)
    units = [(sub, c) for sub in range(SUBS) for c in every]
    rows, rate, live = [], [], []
    for sub, c in units:
        rows.append(
            pl.ds(
                sub * BLOCK * chains + (c % heads) * requests + c // heads, BLOCK, stride=chains
            )
        )
        first = pl.multiple_of((step * SUBS + sub) * BLOCK, BLOCK)
        live.append(first + iota((BLOCK, 1), 0) < counts[c // heads])
        rate.append(jnp.where(live[-1], rate_col[pl.ds(first, BLOCK), c : c + 1], 0.0))
    count = range(len(units))

    withins = []
    for u in count:
        decay = jnp.where(live[u], d_ref[rows[u], :], 0.0)
        high, rest = decay.astype(BF16), decay - decay.astype(BF16).astype(F32)
        middle, low = halves(rest)
        withins.append(dot(lower, high) + dot(lower, middle) + dot(lower, low))
    key_up, key_end, query_up, fades, systems, reaches = [], [], [], [], [], []
    for u in count:
        key = k_all[rows[u], :]
        key = key * lax.rsqrt(jnp.sum(key * key, axis=-1, keepdims=True) + EPSILON)
        grow = jnp.exp(withins[u])
        fade = grow[BLOCK - 1 :, :]
        down = key * jnp.exp(-withins[u])
        up_hi, up_lo = halves(key * grow)
        down_hi, down_lo = halves(down)
        query = (q_all[rows[u], :] * grow).astype(BF16)
        both = dot(jnp.concatenate([up_hi, query], axis=0), down_hi, NT)
        pair = both[:BLOCK] + dot(up_hi, down_lo, NT) + dot(up_lo, down_hi, NT)
        reaches.append(jnp.where(row >= col, both[BLOCK:], 0.0).astype(BF16))
        systems.append(jnp.where(row > col, rate[u] * pair, 0.0))
        key_up.append(key * grow)
        key_end.append(halves(down * fade))
        query_up.append(query)
        fades.append(fade)
    near = row >> 1 == col >> 1
    inverse = [identity - jnp.where(near, member, 0.0) for member in systems]
    for bit in range(1, BLOCK.bit_length() - 1):
        joins = (row >> (bit + 1) == col >> (bit + 1)) & (row >> bit != col >> bit)
        rough = [member.astype(BF16) for member in inverse]
        inner = [
            dot(jnp.where(joins, systems[u], 0.0).astype(BF16), rough[u]).astype(BF16)
            for u in count
        ]
        inverse = [inverse[u] - dot(rough[u], inner[u]) for u in count]
    split = [halves(member) for member in inverse]
    missing = [
        (identity - inverse[u] - dot3(halves(systems[u]), split[u])).astype(BF16) for u in count
    ]
    inverse = [inverse[u] + dot(split[u][0], missing[u]) for u in count]
    split = [halves(member) for member in inverse]
    base_v = [dot3(split[u], halves(rate[u] * v_all[rows[u], :])) for u in count]
    base_k = [halves(dot3(split[u], halves(rate[u] * key_up[u]))) for u in count]
    for sub in range(SUBS):
        here = [sub * chains + c for c in every]
        boths, updates = [], []
        for c, u in enumerate(here):
            carry = halves(state[c])
            both = dot(jnp.concatenate([base_k[u][0], query_up[u]], axis=0), carry[0], NT)
            reached = (
                both[:BLOCK] + dot(base_k[u][0], carry[1], NT) + dot(base_k[u][1], carry[0], NT)
            )
            updates.append(halves(base_v[u] - reached))
            boths.append(both[BLOCK:])
        for c, u in enumerate(here):
            state[c] = fades[u] * state[c] + dot3(updates[c], key_end[u], TN)
        for c, u in enumerate(here):
            request, head = divmod(c, heads)
            out = (boths[c] + dot(reaches[u], updates[c][0])) * key_dim ** (-0.5)
            att[
                (sub * requests + request) * BLOCK : (sub * requests + request + 1) * BLOCK,
                head * LANES : (head + 1) * LANES,
            ] = out.astype(BF16)

    width = w_ref.shape[1]
    for lane in range(0, width, 768):
        done = dot(att[...], w_ref[:, lane : lane + 768]).astype(BF16)
        for sub in range(SUBS):
            part_ref[sub, :, lane : lane + 768] = done[
                sub * requests * BLOCK : (sub + 1) * requests * BLOCK
            ]

    @pl.when(step == pl.num_programs(0) - 1)
    def _():
        columns = final_ref.shape[1] // chains
        for c in every:
            for member in range(final_ref.shape[0]):
                final_ref[member, c * columns : (c + 1) * columns, :] = state[
                    c, member * columns : (member + 1) * columns, :
                ].astype(BF16)


def delta(counts, queries, key_in, value_in, log_decay, update_rate, init_state, w_out, members):
    length, requests, features = queries.shape
    heads, key_dim, value_dim = init_state.shape[1:]
    chains = requests * heads
    width = w_out.shape[1]

    def rows_of(member):
        member = member.reshape(length, requests, heads, key_dim)
        return member.transpose(0, 2, 1, 3).reshape(length * chains, key_dim)

    def whole(*shape):
        return pl.BlockSpec(shape, lambda n, *_: (0,) * len(shape))

    tall = SUBS * BLOCK * chains
    block = pl.BlockSpec((tall, key_dim), lambda n, *_: (n, 0))
    blocks = length // BLOCK
    steps = blocks // SUBS
    return pl.pallas_call(
        delta_kernel,
        grid_spec=pltpu.PrefetchScalarGridSpec(
            num_scalar_prefetch=1,
            grid=(steps,),
            in_specs=[block] * 4
            + [
                whole(requests, heads, length),
                whole(chains, key_dim, value_dim),
                whole(features, width),
            ],
            out_specs=[
                pl.BlockSpec((SUBS, requests * BLOCK, width), lambda n, *_: (n, 0, 0)),
                whole(members, chains * value_dim // members, key_dim),
            ],
            scratch_shapes=[
                pltpu.VMEM((chains, value_dim, key_dim), F32),
                pltpu.VMEM((length, chains), F32),
                pltpu.VMEM((tall, key_dim), F32),
                pltpu.VMEM((tall, key_dim), F32),
                pltpu.VMEM((tall, value_dim), F32),
                pltpu.VMEM((SUBS * requests * BLOCK, features), BF16),
            ],
        ),
        out_shape=[
            jax.ShapeDtypeStruct((blocks, requests * BLOCK, width), BF16),
            jax.ShapeDtypeStruct((members, chains * value_dim // members, key_dim), BF16),
        ],
        compiler_params=pltpu.CompilerParams(vmem_limit_bytes=VMEM),
        cost_estimate=pl.CostEstimate(flops=8 * 10**9, bytes_accessed=16 * 10**6, transcendentals=0),
        name="delta",
    )(
        counts,
        rows_of(queries),
        rows_of(key_in),
        rows_of(value_in),
        rows_of(log_decay),
        update_rate.transpose(1, 2, 0),
        init_state.reshape(chains, key_dim, value_dim),
        w_out,
    )


def place_of(expert):
    return ((expert & 7) << 4) + (((expert >> 3) & 7) << 1) + (expert >> 6)


def picker(experts, rows, dim):
    shape = (experts, rows) if dim == 0 else (rows, experts)
    first = place_of(iota(shape, dim)) * 8
    row = iota(shape, 1 - dim)
    return jnp.where((row >= first) & (row < first + 8), 1.0, 0.0).astype(BF16)


def route_kernel(
    res_ref, part_ref, gain_ref, router_ref, ids_ref,
    mixed_ref, slot_ref, weight_ref, head_ref, tail_ref,
    wide, normed, head_buf, tail_buf, sems,
):
    members, tokens, width = part_ref.shape
    requests = tokens // BLOCK
    chunks = width // LANES
    experts = router_ref.shape[1]
    wide[...] = res_ref[...].astype(F32)
    squares = jnp.zeros((tokens, LANES), F32)
    for chunk in range(chunks):
        lanes = slice(chunk * LANES, (chunk + 1) * LANES)
        total = jnp.concatenate(
            [
                wide[pl.ds(chunk * requests + r, BLOCK, stride=chunks * requests), :]
                for r in range(requests)
            ],
            axis=0,
        )
        for member in range(members):
            total = total + part_ref[member, :, lanes].astype(F32)
        mixed_ref[:, lanes] = total
        squares = squares + total * total
    scale = lax.rsqrt(jnp.sum(squares, axis=-1, keepdims=True) / width + EPSILON)
    for chunk in range(chunks):
        lanes = slice(chunk * LANES, (chunk + 1) * LANES)
        normed[:, lanes] = (mixed_ref[:, lanes] * scale * gain_ref[:, lanes].astype(F32)).astype(
            BF16
        )

    number = iota((experts, tokens), 0)
    chosen = jnp.zeros((experts, tokens), F32)
    for pick in range(ids_ref.shape[0]):
        chosen = chosen + jnp.where(ids_ref[pick : pick + 1, :] == number, 1.0, 0.0)
    row, col = iota((tokens, tokens), 0), iota((tokens, tokens), 1)
    row = (row & (BLOCK - 1)) * requests + (row >> (BLOCK.bit_length() - 1))
    col = (col & (BLOCK - 1)) * requests + (col >> (BLOCK.bit_length() - 1))
    earlier = jnp.where(row < col, 1.0, 0.0).astype(BF16)
    slot = jnp.where(chosen > 0.0, dot(chosen.astype(BF16), earlier), -1.0)
    slot_ref[...] = slot.T

    scores = jax.nn.sigmoid(dot(normed[...], router_ref[...])) * chosen.T
    weight_ref[...] = ROUTE_SCALE * scores / jnp.sum(scores, axis=-1, keepdims=True)

    place = dot(picker(experts, experts * 8, 1), slot.astype(BF16))
    line = iota(place.shape, 0)
    head = jnp.where(place == (line & 7).astype(F32), 1.0, 0.0).astype(BF16)
    tail = place == ((line & 3) + 8).astype(F32)
    tail_a = jnp.where(tail & ((line & 4) == 0), 1.0, 0.0).astype(BF16)
    tail_b = jnp.where(tail & ((line & 4) != 0), 1.0, 0.0).astype(BF16)
    half = width // 2
    copies = []

    def send(buf, ref, lane, step):
        lanes = pl.ds(lane, step)
        copies.append(
            pltpu.make_async_copy(buf.at[:, lanes], ref.at[:, lanes], sems.at[len(copies)])
        )
        copies[-1].start()

    step = 6 * LANES
    for lane in range(0, width, step):
        head_buf[:, lane : lane + step] = dot(head, normed[:, lane : lane + step]).astype(BF16)
        send(head_buf, head_ref, lane, step)
    step = 3 * LANES
    for lane in range(0, half, step):
        tail_buf[:, lane : lane + step] = (
            dot(tail_a, normed[:, lane : lane + step])
            + dot(tail_b, normed[:, half + lane : half + lane + step])
        ).astype(BF16)
        send(tail_buf, tail_ref, lane, step)
    for copy in copies:
        copy.wait()


def interleave(member):
    length, requests, width = member.shape
    member = member.reshape(length, requests, width // LANES, LANES).transpose(0, 2, 1, 3)
    return member.reshape(-1, LANES)


def route(residual, parts, norm_gain, w_router, expert_ids):
    length, requests, width = residual.shape
    tokens = length * requests
    experts = w_router.shape[1]
    ids = expert_ids.transpose(2, 1, 0).reshape(-1, tokens)
    vmem = pl.BlockSpec(memory_space=pltpu.VMEM)
    return pl.pallas_call(
        route_kernel,
        in_specs=[vmem] * 5,
        out_specs=[vmem] * 3 + [pl.BlockSpec(memory_space=pl.ANY)] * 2,
        scratch_shapes=[
            pltpu.VMEM((tokens * width // LANES, LANES), F32),
            pltpu.VMEM((tokens, width), BF16),
            pltpu.VMEM((experts * 8, width), BF16),
            pltpu.VMEM((experts * 8, width // 2), BF16),
            pltpu.SemaphoreType.DMA((6,)),
        ],
        out_shape=[
            jax.ShapeDtypeStruct((tokens, width), F32),
            jax.ShapeDtypeStruct((tokens, experts), F32),
            jax.ShapeDtypeStruct((tokens, experts), F32),
            jax.ShapeDtypeStruct((experts * 8, width), BF16),
            jax.ShapeDtypeStruct((experts * 8, width // 2), BF16),
        ],
        compiler_params=pltpu.CompilerParams(vmem_limit_bytes=VMEM),
        cost_estimate=pl.CostEstimate(flops=2 * 10**9, bytes_accessed=14 * 10**6, transcendentals=0),
        name="route",
    )(interleave(residual), parts, norm_gain.reshape(1, width), w_router, ids)


GROUP = 256


def unpack_rows(dtype=BF16):
    row, col = iota((GROUP, GROUP), 0), iota((GROUP, GROUP), 1)
    half = GROUP // 2
    inside = row & (half - 1)
    source = ((inside >> 2) << 3) + (inside & 3) + jnp.where(row >= half, 4, 0)
    return jnp.where(col == source, 1.0, 0.0).astype(dtype)


def act(lines, gate_ref, up_ref):
    gate = dot(lines, gate_ref[...])
    up = dot(lines, up_ref[...])
    return (gate / (1.0 + jnp.exp(-gate)) * up).astype(BF16)


def head_kernel(x_ref, gate_ref, up_ref, down_ref, out_ref, inner, *, ups):
    step = pl.program_id(0)
    rows = x_ref.shape[0]
    fold = gate_ref.shape[1]

    @pl.when(step < ups)
    def _():
        lanes = pl.ds(pl.multiple_of(step * fold, fold), fold)
        for start in range(0, rows, GROUP):
            here = slice(start, start + GROUP)
            inner[here, lanes] = act(x_ref[here, :], gate_ref, up_ref)

    @pl.when(step >= ups)
    def _():
        for start in range(0, rows, GROUP):
            here = slice(start, start + GROUP)
            out_ref[here, :] = dot(inner[here, :], down_ref[...]).astype(BF16)


def tail_kernel(
    x_ref, gate_ref, up_ref, down_ref, out_ref, lines_in, lines_out, inner, *, ups
):
    step = pl.program_id(0)
    rows, half = x_ref.shape
    fold = gate_ref.shape[1]
    tile = down_ref.shape[1]
    tails = rows // 2

    @pl.when(step == 0)
    def _():
        order = unpack_rows()
        for group in range(rows // GROUP):
            moved = dot(order, x_ref[pl.ds(group * GROUP, GROUP), :]).astype(BF16)
            here = pl.ds(group * GROUP // 2, GROUP // 2)
            lines_in[here, :half] = moved[: GROUP // 2]
            lines_in[here, half:] = moved[GROUP // 2 :]

    @pl.when(step < ups)
    def _():
        lanes = pl.ds(pl.multiple_of(step * fold, fold), fold)
        for start in range(0, tails, GROUP):
            here = slice(start, start + GROUP)
            inner[here, lanes] = act(lines_in[here, :], gate_ref, up_ref)

    @pl.when(step >= ups)
    def _():
        lanes = pl.ds(pl.multiple_of((step - ups) * tile, tile), tile)
        for start in range(0, tails, GROUP):
            here = slice(start, start + GROUP)
            lines_out[here, lanes] = dot(inner[here, :], down_ref[...]).astype(BF16)

    @pl.when(step == pl.num_programs(0) - 1)
    def _():
        order = unpack_rows()
        for group in range(rows // GROUP):
            here = pl.ds(group * GROUP // 2, GROUP // 2)
            moved = jnp.concatenate([lines_out[here, :half], lines_out[here, half:]], axis=0)
            out_ref[pl.ds(group * GROUP, GROUP), :] = dot(order, moved, TN).astype(BF16)


def experts_of(arrived, gate, up, down):
    rows = arrived.shape[0]
    width, hidden = gate.shape
    fold, tile = 256, 768
    ups, downs = hidden // fold, width // tile
    tails = rows // 2

    def column(step):
        return (0, jnp.minimum(step, ups - 1))

    def later(step):
        return (0, jnp.maximum(step - ups, 0))

    in_specs = [
        pl.BlockSpec(arrived.shape, lambda step: (0, 0)),
        pl.BlockSpec((width, fold), column),
        pl.BlockSpec((width, fold), column),
        pl.BlockSpec((hidden, tile), later),
    ]
    common = dict(
        grid=(ups + downs,),
        out_shape=jax.ShapeDtypeStruct(arrived.shape, BF16),
        compiler_params=pltpu.CompilerParams(vmem_limit_bytes=VMEM),
    )
    if arrived.shape[1] == width:
        return pl.pallas_call(
            functools.partial(head_kernel, ups=ups),
            in_specs=in_specs,
            out_specs=pl.BlockSpec((rows, tile), later),
            scratch_shapes=[pltpu.VMEM((rows, hidden), BF16)],
            cost_estimate=pl.CostEstimate(flops=6 * rows * width * hidden, bytes_accessed=4 * rows * width + 6 * width * hidden, transcendentals=0),
            name="experts_head",
            **common,
        )(arrived, gate, up, down)
    return pl.pallas_call(
        functools.partial(tail_kernel, ups=ups),
        in_specs=in_specs,
        out_specs=pl.BlockSpec(arrived.shape, lambda step: (0, 0)),
        scratch_shapes=[
            pltpu.VMEM((tails, width), BF16),
            pltpu.VMEM((tails, width), BF16),
            pltpu.VMEM((tails, hidden), BF16),
        ],
        cost_estimate=pl.CostEstimate(flops=6 * tails * width * hidden, bytes_accessed=4 * tails * width + 6 * width * hidden, transcendentals=0),
        name="experts_tail",
        **common,
    )(arrived, gate, up, down)


def spread_kernel(slot_ref, weight_ref, heads, tails):
    tokens, experts = slot_ref.shape
    pick = picker(experts, heads.shape[1], 0)
    place = dot(slot_ref[...].astype(BF16), pick)
    line = iota(place.shape, 1)
    is_head = place == (line & 7).astype(F32)
    is_tail = place == ((line & 3) + 8).astype(F32)
    for index, part in enumerate(halves(weight_ref[...])):
        spread = dot(part, pick)
        here = slice(index * tokens, (index + 1) * tokens)
        there = slice((index + 2) * tokens, (index + 3) * tokens)
        heads[here, :] = jnp.where(is_head, spread, 0.0).astype(BF16)
        tails[here, :] = jnp.where(is_tail & ((line & 4) == 0), spread, 0.0).astype(BF16)
        tails[there, :] = jnp.where(is_tail & ((line & 4) != 0), spread, 0.0).astype(BF16)


def spread_of(slot, weight):
    tokens, experts = slot.shape
    rows = experts * 8
    vmem = pl.BlockSpec(memory_space=pltpu.VMEM)
    return pl.pallas_call(
        spread_kernel,
        in_specs=[vmem] * 2,
        out_specs=[vmem] * 2,
        out_shape=[
            jax.ShapeDtypeStruct((2 * tokens, rows), BF16),
            jax.ShapeDtypeStruct((4 * tokens, rows), BF16),
        ],
        compiler_params=pltpu.CompilerParams(vmem_limit_bytes=VMEM),
        cost_estimate=pl.CostEstimate(flops=10**9, bytes_accessed=2 * 10**6, transcendentals=0),
        name="spread",
    )(slot, weight)


def add_kernel(mixed_ref, heads, back_ref, total_ref):
    tokens = mixed_ref.shape[0]
    both = dot(heads[...], back_ref[...])
    total_ref[...] = mixed_ref[...] + both[:tokens] + both[tokens:]


def add_heads(mixed, heads, back):
    tokens, width = mixed.shape
    tile = 768
    column = pl.BlockSpec((tokens, tile), lambda step: (0, step))
    return pl.pallas_call(
        add_kernel,
        grid=(width // tile,),
        in_specs=[
            column,
            pl.BlockSpec(heads.shape, lambda step: (0, 0)),
            pl.BlockSpec((back.shape[0], tile), lambda step: (0, step)),
        ],
        out_specs=column,
        out_shape=jax.ShapeDtypeStruct((tokens, width), F32),
        compiler_params=pltpu.CompilerParams(vmem_limit_bytes=VMEM),
        cost_estimate=pl.CostEstimate(
            flops=3 * 10**9, bytes_accessed=8 * 10**6, transcendentals=0
        ),
        name="add_heads",
    )(mixed, heads, back)


def combine_kernel(total_ref, tails, back_ref, out_ref):
    step = pl.program_id(0)
    tokens, width = total_ref.shape
    requests = tokens // BLOCK
    half = width // 2
    thin = back_ref.shape[1]
    both = dot(tails[...], back_ref[...])
    for side in range(2):
        lanes = pl.ds(pl.multiple_of(side * half + step * thin, thin), thin)
        first = 2 * side * tokens
        done = (
            total_ref[:, lanes]
            + both[first : first + tokens]
            + both[first + tokens : first + 2 * tokens]
        )
        pieces = [done[r * BLOCK : (r + 1) * BLOCK] for r in range(requests)]
        out_ref[:, :, lanes] = jnp.stack(pieces, axis=1).astype(BF16)


def combine(total, tails, back):
    tokens, width = total.shape
    thin = 384

    def whole(*shape):
        return pl.BlockSpec(shape, lambda step: (0,) * len(shape))

    return pl.pallas_call(
        combine_kernel,
        grid=(width // 2 // thin,),
        in_specs=[
            whole(*total.shape),
            whole(*tails.shape),
            pl.BlockSpec((back.shape[0], thin), lambda step: (0, step)),
        ],
        out_specs=whole(BLOCK, tokens // BLOCK, width),
        out_shape=jax.ShapeDtypeStruct((BLOCK, tokens // BLOCK, width), BF16),
        compiler_params=pltpu.CompilerParams(vmem_limit_bytes=VMEM),
        cost_estimate=pl.CostEstimate(
            flops=2 * 10**9, bytes_accessed=6 * 10**6, transcendentals=0
        ),
        name="combine",
    )(total, tails, back)


def decode(relaid, dec_query, dec_key, dec_value, dec_decay, dec_beta):
    query = dec_query.astype(F32)
    key = dec_key.astype(F32)
    key = key * lax.rsqrt(jnp.sum(key * key, axis=-1, keepdims=True) + EPSILON)
    value = dec_value.astype(F32)
    state = relaid.astype(F32)
    outs = []
    for turn in range(dec_query.shape[1]):
        state = jnp.exp(dec_decay[:, turn])[..., None, :] * state
        guessed = jnp.sum(state * key[:, turn, :, None, :], axis=-1)
        update = dec_beta[:, turn, :, None] * (value[:, turn] - guessed)
        state = state + update[..., None] * key[:, turn, :, None, :]
        outs.append(jnp.sum(state * query[:, turn, :, None, :], axis=-1))
    out = jnp.stack(outs, axis=1) * dec_query.shape[-1] ** (-0.5)
    return out, state.transpose(0, 1, 3, 2)


def shards(
    residual, queries, key_in, value_in, log_decay, update_rate, counts, init_state, w_out,
    norm_gain, w_router, expert_ids, w_gate, w_up, w_down,
    dec_query, dec_key, dec_value, dec_decay, dec_beta,
):
    requests = residual.shape[1]
    heads, key_dim, value_dim = init_state.shape[1:]
    members = lax.axis_size("exp")
    experts = w_router.shape[1]
    groups = lax.axis_size("grp")
    parts, final = delta(
        counts, queries, key_in, value_in, log_decay, update_rate, init_state, w_out, members
    )
    final = lax.ppermute(
        final,
        ("grp", "exp"),
        [(g * members + e, e * members + g) for g in range(groups) for e in range(members)],
    )
    parts = lax.all_to_all(parts, "exp", split_axis=0, concat_axis=0, tiled=True)
    mixed, slot, weight, head, tail = route(residual, parts, norm_gain, w_router, expert_ids)

    def exchange(member):
        member = member.reshape(experts, 8, -1)
        member = lax.all_to_all(
            member, ("exp", "grp", "half"), split_axis=0, concat_axis=0, tiled=True
        )
        return member.reshape(experts * 8, -1)

    head = exchange(head)
    head, tail = lax.optimization_barrier((head, tail))
    tail = exchange(tail)
    heads_of, tails_of = spread_of(slot, weight)
    matrices = (w_gate[0], w_up[0], w_down[0])
    head, tail, final = lax.optimization_barrier(
        (exchange(experts_of(head, *matrices)), experts_of(tail, *matrices), final)
    )
    relaid = lax.all_to_all(final, "exp", split_axis=0, concat_axis=0, tiled=True)
    tail, relaid = lax.optimization_barrier((tail, relaid))
    tail = exchange(tail)
    relaid = relaid.reshape(groups * requests, heads, value_dim // members, key_dim)
    dec_out, dec_state = decode(relaid, dec_query, dec_key, dec_value, dec_decay, dec_beta)

    hidden = combine(add_heads(mixed, heads_of, head), tails_of, tail)
    return hidden, dec_out, dec_state


def solution(mesh):
    return jax.shard_map(
        shards,
        mesh=mesh,
        in_specs=(
            P("exp", ("half", "grp"), None),
            P(None, ("half", "grp"), "exp"),
            P(None, ("half", "grp"), "exp"),
            P(None, ("half", "grp"), "exp"),
            P(None, ("half", "grp"), "exp"),
            P(None, ("half", "grp"), "exp"),
            P(("half", "grp")),
            P(("half", "grp"), "exp", None, None),
            P("exp", None),
            P(),
            P(),
            P("exp", ("half", "grp"), None),
            P(("half", "grp", "exp"), None, None),
            P(("half", "grp", "exp"), None, None),
            P(("half", "grp", "exp"), None, None),
            P("half", None, "grp", None),
            P("half", None, "grp", None),
            P("half", None, "grp", "exp"),
            P("half", None, "grp", None),
            P("half", None, "grp"),
        ),
        out_specs=(
            P("exp", ("half", "grp"), None),
            P("half", None, "grp", "exp"),
            P("half", "grp", None, "exp"),
        ),
        check_vma=False,
    )
```
